128 devices in a mesh: sp: 4 (over x_hi, core), vel: 32 (over x_lo, y, z).
Axes of the slice: x: 4 (x_hi: 2, x_lo: 2; x = x_hi * 2 + x_lo), y: 4, z: 4, core: 2. Of those that a mesh axis runs over, the one named last changes fastest.
Arguments:
- prior: float32 [4, 4, 4, 4096, 512], P(None, None, None, 'vel', 'sp'), may hold values from -50 to 50
- block_inverse: float32 [4096, 64, 64], P('vel'), may hold values from -0.2 to 0.7
Outputs:
- iterate: float32 [4, 4, 4, 4096, 512], P(None, None, None, 'vel', 'sp')
The draws below stay inside these ranges and needn't reach their ends.
All inputs are finite; a program needn't handle non-finite values.
Results may differ from the reference program's by a relative error of at most 0.0001.
Values sent between devices are 32-bit elements; how exact they have to be, the bound alone decides.
No kernel may reach another device: no remote copies, remote signals or barrier semaphores. Data moves between devices by JAX's collectives and lax.ppermute only.
A program may use at most 128 MiB of HBM per device.

```python
import jax
import jax.numpy as jnp
from jax import lax

MODES = 4
BASIS = 64
NV1 = 16
V = 4096
NY = 8
NZ = 8
NX = 8
CELLS = 512
ITERS = 2


COLLISION = 1.0


COUPLING = 0.25


def velocity_grid_drawn(points):
    total = points * points * points
    serial = jnp.arange(total, dtype=jnp.int32)
    spacing = 6.0 / points
    centre = 0.5 * (points - 1)
    speed_x = ((serial // (points * points)).astype(jnp.float32) - centre) * spacing
    speed_y = ((serial // points % points).astype(jnp.float32) - centre) * spacing
    speed_z = ((serial % points).astype(jnp.float32) - centre) * spacing
    return (speed_x, speed_y, speed_z)


def draw_prior(key, part):
    key = jax.random.fold_in(key, 7)
    noise_key, common_key = jax.random.split(key)
    speed_x, speed_y, speed_z = velocity_grid_drawn(NV1)
    profile = (1.0 + 0.5 * speed_x + 0.3 * (speed_y * speed_y - 1.0)).reshape(1, 1, 1, V, 1)
    noise = jnp.clip(jax.random.normal(noise_key, (MODES, MODES, MODES, V, CELLS), jnp.float32), -4.0, 4.0)
    common = jnp.clip(jax.random.normal(common_key, (MODES, MODES, MODES, 1, CELLS), jnp.float32), -4.0, 4.0) * 1.5
    return noise + common * profile


def draw_block_inverse(key, part):
    key = jax.random.fold_in(key, 13)
    diagonal_key, spread_key = jax.random.split(key)
    speed_x, speed_y, speed_z = velocity_grid_drawn(NV1)
    speed_sum = jnp.abs(speed_x) + jnp.abs(speed_y) + jnp.abs(speed_z)
    damping = 1.0 / (1.0 + COLLISION + 8.0 * COUPLING * speed_sum)
    jitter = jax.random.uniform(diagonal_key, (V, BASIS), jnp.float32, -1.0, 1.0)
    spread = jnp.clip(jax.random.normal(spread_key, (V, BASIS, BASIS), jnp.float32), -4.0, 4.0) * 0.03
    identity = jnp.eye(BASIS, dtype=jnp.float32)
    matrix = identity[None, :, :] * (1.0 + 0.3 * jitter)[:, :, None] + spread * (1.0 - identity[None, :, :])
    return matrix * damping[:, None, None]


def setup_inputs(seed: int = 0) -> dict:
    streams_of = jax.random.split(jax.random.key(seed), 3)
    return {
        "prior": draw_prior(jax.random.fold_in(streams_of[2], 71), 0),
        "block_inverse": draw_block_inverse(jax.random.fold_in(streams_of[2], 71), 0),
    }


COLLISION = 1.0
COUPLING = 0.25
LID_SPEED = 0.6
HIGHEST = lax.Precision.HIGHEST

def velocity_grid(points):
    total = points * points * points
    serial = jnp.arange(total, dtype=jnp.int32)
    spacing = 6.0 / points
    centre = 0.5 * (points - 1)
    speed_x = ((serial // (points * points)).astype(jnp.float32) - centre) * spacing
    speed_y = ((serial // points % points).astype(jnp.float32) - centre) * spacing
    speed_z = ((serial % points).astype(jnp.float32) - centre) * spacing
    return (speed_x, speed_y, speed_z)

def moment_tables(points):
    speed_x, speed_y, speed_z = velocity_grid(points)
    square = speed_x * speed_x + speed_y * speed_y + speed_z * speed_z
    rows = [jnp.ones_like(square), speed_x, speed_y, speed_z, speed_x * speed_x - 1.0, speed_y * speed_y - 1.0, speed_z * speed_z - 1.0, speed_x * speed_y, speed_x * speed_z, speed_y * speed_z, (square - 5.0) * speed_x, (square - 5.0) * speed_y, (square - 5.0) * speed_z]
    polynomials = jnp.stack(rows)
    density = jnp.exp(-0.5 * square)
    density = density / jnp.sum(density)
    weighted = polynomials * density
    scaled = polynomials / lax.optimization_barrier(jnp.sum(weighted * polynomials, axis=1, keepdims=True))
    return (weighted, scaled, speed_x, speed_y, speed_z)

def face_tables(mode_count):
    degree = jnp.arange(mode_count, dtype=jnp.int32)
    face_high = jnp.sqrt(degree.astype(jnp.float32) + 0.5)
    face_low = jnp.where(degree % 2 == 0, 1.0, -1.0).astype(jnp.float32) * face_high
    return (face_high, face_low)

def face_trace(values, field_part, direction):
    return jnp.tensordot(values, field_part, axes=([0], [direction]), precision=HIGHEST)

def lift_face(values, face_value, direction):
    shape = [1] * (face_value.ndim + 1)
    shape[direction] = values.shape[0]
    return jnp.expand_dims(face_value, direction) * values.reshape(shape)

def wall_face(wall_value, mode_count, cell_count):
    corner = (jnp.arange(mode_count, dtype=jnp.int32) == 0).astype(jnp.float32)
    pattern = 2.0 * corner[:, None] * corner[None, :]
    return pattern[:, :, None, None] * wall_value[None, None, :, None] * jnp.ones((1, 1, 1, cell_count), jnp.float32)

def from_below(face_value, stride, incoming):
    return jnp.concatenate([incoming, face_value[..., :face_value.shape[-1] - stride]], axis=-1)

def from_above(face_value, stride, incoming):
    return jnp.concatenate([face_value[..., stride:], incoming], axis=-1)

def direction_term(lower_raw, upper_raw, coordinate, extent, speed, lower_wall, upper_wall, direction, face_high, face_low):
    mode_count = face_high.shape[0]
    cell_count = lower_raw.shape[-1]
    lower_face = jnp.where(coordinate > 0, lower_raw, wall_face(lower_wall, mode_count, cell_count))
    upper_face = jnp.where(coordinate < extent - 1, upper_raw, wall_face(upper_wall, mode_count, cell_count))
    forward = jnp.maximum(speed, 0.0)[:, None]
    backward = jnp.maximum(-speed, 0.0)[:, None]
    return lift_face(face_low, forward * lower_face, direction) + lift_face(face_high, backward * upper_face, direction)

def relax_block(iterate, prior, inverse, scaled, moments, speeds, coords, extents):
    mode_count = iterate.shape[0]
    block_width = iterate.shape[3]
    cell_count = iterate.shape[4]
    basis = mode_count ** 3
    face_high, face_low = face_tables(mode_count)
    equilibrium = jnp.einsum('kv,kpc->pvc', scaled, moments, precision=HIGHEST).reshape(iterate.shape)
    unit_wall = jnp.ones_like(speeds[0])
    lid_wall = jnp.exp(LID_SPEED * speeds[0] - 0.5 * LID_SPEED * LID_SPEED)
    strides = (extents[1] * extents[2], extents[2], 1)
    upper_walls = (unit_wall, unit_wall, lid_wall)
    right_side = prior + COLLISION * equilibrium
    for direction in range(3):
        upward = face_trace(face_high, iterate, direction)
        downward = face_trace(face_low, iterate, direction)
        empty_plane = jnp.zeros(upward.shape[:-1] + (strides[direction],), jnp.float32)
        lower_raw = from_below(upward, strides[direction], empty_plane)
        upper_raw = from_above(downward, strides[direction], empty_plane)
        right_side = right_side + COUPLING * direction_term(lower_raw, upper_raw, coords[direction], extents[direction], speeds[direction], unit_wall, upper_walls[direction], direction, face_high, face_low)
    flat = right_side.reshape(basis, block_width, cell_count)
    return jnp.einsum('vpq,qvc->pvc', inverse, flat, precision=HIGHEST).reshape(iterate.shape)

def reference(prior, block_inverse):
    mode_count = prior.shape[0]
    velocity_count = prior.shape[3]
    cell_count = prior.shape[4]
    basis = mode_count ** 3
    block_width = min(velocity_count, 256)
    blocks = velocity_count // block_width
    weighted, scaled, speed_x, speed_y, speed_z = moment_tables(NV1)
    cell_index = jnp.arange(cell_count, dtype=jnp.int32)
    coords = (cell_index // (NY * NZ), cell_index // NZ % NY, cell_index % NZ)
    extents = (NX, NY, NZ)

    def to_blocks(field_part):
        shaped = field_part.reshape(mode_count, mode_count, mode_count, blocks, block_width, cell_count)
        return jnp.moveaxis(shaped, 3, 0)
    prior_blocks = to_blocks(prior)
    inverse_blocks = block_inverse.reshape(blocks, block_width, basis, basis)
    scaled_blocks = jnp.moveaxis(scaled.reshape(13, blocks, block_width), 1, 0)
    speed_blocks = tuple((component.reshape(blocks, block_width) for component in (speed_x, speed_y, speed_z)))
    iterate = prior
    for iteration in range(ITERS):
        moments = jnp.einsum('kv,pvc->kpc', weighted, iterate.reshape(basis, velocity_count, cell_count), precision=HIGHEST)

        def update_block(pieces):
            return relax_block(pieces[0], pieces[1], pieces[2], pieces[3], moments, (pieces[4], pieces[5], pieces[6]), coords, extents)
        fresh = lax.map(update_block, (to_blocks(iterate), prior_blocks, inverse_blocks, scaled_blocks) + speed_blocks)
        iterate = jnp.moveaxis(fresh, 0, 3).reshape(prior.shape)
    return iterate
```

```python
import functools

import jax
import jax.numpy as jnp
import numpy as np
from jax import lax
from jax.experimental import pallas as pl
from jax.experimental.pallas import tpu as pltpu
from jax.sharding import PartitionSpec as P

NV1 = 16
ITERS = 2
COUPLING = 0.25
LID_SPEED = 0.6
STEP = 6.0 / NV1
CENTRE = 0.5 * (NV1 - 1)
VEL = 32
LOCAL_Y = 8
HIGH = [float(np.sqrt(k + 0.5)) for k in range(4)]
HIGHEST = lax.Precision.HIGHEST
F32 = jnp.float32
BF16 = jnp.bfloat16
HALF = 64


def grid_speed(index):
    return (np.asarray(index, np.float64) - CENTRE) * STEP


def local_polynomials(y, z):
    r2 = y * y + z * z
    return [np.ones_like(r2), y, z, y * y, z * z, y * z, r2 * y, r2 * z]


def combination(x):
    c = np.zeros((13, 8))
    c[0, 0] = 1.0
    c[1, 0] = x
    c[2, 1] = 1.0
    c[3, 2] = 1.0
    c[4, 0] = x * x - 1.0
    c[5, 3], c[5, 0] = 1.0, -1.0
    c[6, 4], c[6, 0] = 1.0, -1.0
    c[7, 1] = x
    c[8, 2] = x
    c[9, 5] = 1.0
    c[10, 0], c[10, 3], c[10, 4] = x * (x * x - 5.0), x, x
    c[11, 1], c[11, 6] = x * x - 5.0, 1.0
    c[12, 2], c[12, 7] = x * x - 5.0, 1.0
    return c


def tables():
    speed = grid_speed(np.arange(NV1))
    weight = np.exp(-0.5 * speed * speed)
    weight = weight / weight.sum()
    x, y, z = np.meshgrid(speed, speed, speed, indexing="ij")
    w = weight[:, None, None] * weight[None, :, None] * weight[None, None, :]
    g = np.stack(local_polynomials(y, z))
    per_x = np.stack([combination(s) for s in speed])
    h = np.einsum("xkj,jxyz->kxyz", per_x, g)
    norm = (w * h * h).sum(axis=(1, 2, 3))
    source = np.repeat(per_x * weight[:, None, None], 2, axis=0)
    target = np.repeat(per_x, 2, axis=0)
    mix = np.einsum("tkj,k,ski->tjsi", target, 1.0 / norm, source).reshape(VEL * 8, VEL * 8)
    local = np.zeros((2, 8, 128))
    for part in range(2):
        ys = speed[part * LOCAL_Y : (part + 1) * LOCAL_Y]
        yy, zz = np.meshgrid(ys, speed, indexing="ij")
        wy = weight[part * LOCAL_Y : (part + 1) * LOCAL_Y]
        ww = wy[:, None] * weight[None, :]
        local[part] = np.stack([(ww * p).reshape(-1) for p in local_polynomials(yy, zz)])
    scalars = np.zeros((VEL, 24))
    for i in range(VEL):
        vx = speed[i // 2]
        part = i % 2
        scalars[i, 0] = 1.0 if vx > 0 else -1.0
        scalars[i, 1] = 1.0 if part else -1.0
        scalars[i, 2] = COUPLING * abs(vx)
        scalars[i, 3] = 2.0 * np.exp(LID_SPEED * vx - 0.5 * LID_SPEED * LID_SPEED)
        scalars[i, 8:16] = speed[part * LOCAL_Y : (part + 1) * LOCAL_Y]
        scalars[i, 16:24] = weight[part * LOCAL_Y : (part + 1) * LOCAL_Y]
    return mix.astype(np.float32), local.astype(np.float32), scalars.astype(np.float32), speed, weight


MIX, LOCAL, SCALARS, SPEED, WEIGHT = tables()


def split(a):
    hi = a.astype(BF16)
    return hi, (a - hi.astype(F32)).astype(BF16)


def lane_index(shape):
    return lax.broadcasted_iota(jnp.int32, shape, len(shape) - 1)


def outgoing_mask(lane, sign):
    return jnp.where(sign > 0, lane, 2 * HALF - 1 - lane) >= HALF


def trace_face(sign):
    return [HIGH[k] if k % 2 == 0 else HIGH[k] * sign for k in range(4)]


def lift_faces(sign):
    return [HIGH[k] if k % 2 == 0 else -HIGH[k] * sign for k in range(4)]


def first_moments_kernel(place, scalars, local_ref, prior_ref, moments_ref, send_ref):
    step = pl.program_id(0)
    vel = place[0]
    sign = scalars[vel, 0]
    face = trace_face(sign)
    weights = local_ref[vel % 2]
    traces = []
    for half in range(2):
        trace = None
        for p0 in range(4):
            block = prior_ref[p0, half, 0]
            hi, lo = split(block)
            both = jnp.concatenate([hi, lo], axis=0)
            product = jnp.dot(weights, both, preferred_element_type=F32)
            moments_ref[p0, half, 0] = product[:8] + product[8:]
            term = face[p0] * block
            trace = term if trace is None else trace + term
        traces.append(trace)
    mask = outgoing_mask(lane_index(traces[0].shape), sign)
    send_ref[pl.ds(step, 128, stride=8), :] = jnp.where(mask, traces[1], pltpu.roll(traces[0], HALF, 1))


def first_moments(place, scalars, local, prior):
    view = prior.reshape(4, 2, 8, 128, 128)
    moments, send = pl.pallas_call(
        first_moments_kernel,
        grid=(8,),
        in_specs=[
            pl.BlockSpec(memory_space=pltpu.SMEM),
            pl.BlockSpec(memory_space=pltpu.SMEM),
            pl.BlockSpec((2, 16, 256), lambda i: (0, 0, 0)),
            pl.BlockSpec((4, 2, 1, 128, 128), lambda i: (0, 0, i, 0, 0)),
        ],
        out_specs=[
            pl.BlockSpec((4, 2, 1, 8, 128), lambda i: (0, 0, i, 0, 0)),
            pl.BlockSpec((1024, 128), lambda i: (0, 0)),
        ],
        out_shape=[
            jax.ShapeDtypeStruct((4, 2, 8, 8, 128), F32),
            jax.ShapeDtypeStruct((1024, 128), F32),
        ],
        compiler_params=pltpu.CompilerParams(vmem_limit_bytes=48 * 2**20),
        name="first_moments",
    )(place, scalars, local, view)
    return moments.reshape(VEL, 16, 128), send


def mix_kernel(mix_ref, in_ref, out_ref):
    for low in range(2):
        part = in_ref[:, low * 8 : low * 8 + 8, :].reshape(VEL * 8, 128)
        mixed = jnp.dot(mix_ref[...], part, preferred_element_type=F32, precision=HIGHEST)
        out_ref[:, low * 8 : low * 8 + 8, :] = mixed.reshape(VEL, 8, 128)


def mix_moments(mix, partial_sums):
    return pl.pallas_call(
        mix_kernel,
        out_shape=jax.ShapeDtypeStruct((VEL, 16, 128), F32),
        name="mix_moments",
    )(mix, partial_sums)


def sum_over_velocities(mix, partial_sums):
    gathered = lax.all_to_all(partial_sums, "vel", 0, 0)
    mixed = mix_moments(mix, gathered)
    return lax.all_to_all(mixed, "vel", 0, 0)


def inflow_yz(source, base, target, scalars, vel, y):
    lane = lane_index((8, 128))
    sublane = lax.broadcasted_iota(jnp.int32, (8, 128), 0)
    sign_y = scalars[vel, 1]
    trace_y, lift_y = trace_face(sign_y), lift_faces(sign_y)
    up_y = sign_y > 0
    shift_y = jnp.where(up_y, 8, 120)
    cell_y = jnp.where(up_y, lane // 8 % 8, 7 - lane // 8 % 8)
    scale_y = jnp.where(cell_y > 0, COUPLING * jnp.abs(y), 0.0)
    wall_y = jnp.where(cell_y > 0, 0.0, 2.0 * COUPLING * jnp.abs(y))
    for part in range(2):
        rows = pl.ds(part * 8, 8)
        up = part == 1
        speed = jnp.abs((sublane + (part * 8)).astype(F32) - CENTRE) * (STEP * COUPLING)
        inside = (lane % 8 > 0) if up else (lane % 8 < 7)
        scale_z = jnp.where(inside, speed, 0.0)
        wall_z = jnp.where(inside, 0.0, speed * (2.0 if up else scalars[vel, 3]))
        trace_z, lift_z = trace_face(1.0 if up else -1.0), lift_faces(1.0 if up else -1.0)
        for p0 in range(4):
            x = [[source[p0 * 16 + p1 * 4 + p2, rows, :] for p2 in range(4)] for p1 in range(4)]
            face_y, face_z = [], []
            for k in range(4):
                ty = sum(trace_y[p1] * x[p1][k] for p1 in range(4))
                ty = pltpu.roll(ty, shift_y, 1) * scale_y
                tz = sum(trace_z[p2] * x[k][p2] for p2 in range(4))
                tz = pltpu.roll(tz, 1 if up else 127, 1) * scale_z
                if p0 == 0 and k == 0:
                    ty = ty + wall_y
                    tz = tz + wall_z
                face_y.append(ty)
                face_z.append(tz)
            for p1 in range(4):
                for p2 in range(4):
                    q = p0 * 16 + p1 * 4 + p2
                    value = base[q, rows, :] + lift_y[p1] * face_y[p2] + lift_z[p2] * face_z[p1]
                    target[q * 16 + part * 8 : q * 16 + part * 8 + 8, :] = value


def own_inflow_x(column, place, scalars, vel, mask):
    sign = scalars[vel, 0]
    face, lift = trace_face(sign), lift_faces(sign)
    trace = sum(face[p0] * column[p0 * 16 : p0 * 16 + 16] for p0 in range(4))
    turned = pltpu.roll(trace, HALF, 1)
    send = jnp.where(mask[:8], trace[8:], turned[:8])
    row = lax.broadcasted_iota(jnp.int32, (16, 128), 0)
    wall = jnp.where(row == 0, scalars_wall(place, sign), 0.0)
    own = jnp.where(mask, turned, wall) * scalars[vel, 2]
    return send, jnp.concatenate([lift[p0] * own for p0 in range(4)], axis=0)


def scalars_wall(place, sign):
    last = jnp.where(sign > 0, 0, place[2] - 1)
    return jnp.where(place[1] == last, 2.0, 0.0)


def prepare_kernel(place, scalars, prior_ref, inverse_ref, right_ref, packed_ref, scratch):
    step = pl.program_id(0)
    vel = place[0]
    inflow_yz(prior_ref, prior_ref, scratch, scalars, vel, scalars[vel, 8 + step])
    flat = prior_ref.reshape(1024, 128)
    mask = outgoing_mask(lane_index((16, 128)), scalars[vel, 0])
    lane = lane_index((64, 128))
    for v in range(16):
        _, own = own_inflow_x(flat[pl.ds(v, 64, stride=16), :], place, scalars, vel, mask)
        right_ref[v] = scratch[pl.ds(v, 64, stride=16), :] + own
        block = inverse_ref[v]
        hi, lo = split(jnp.concatenate([block, block], axis=1))
        packed_ref[v] = jnp.where(lane < HALF, hi.astype(F32), lo.astype(F32)).astype(BF16)


def prepare(place, scalars, prior, inverse):
    return pl.pallas_call(
        prepare_kernel,
        grid=(8,),
        in_specs=[
            pl.BlockSpec(memory_space=pltpu.SMEM),
            pl.BlockSpec(memory_space=pltpu.SMEM),
            pl.BlockSpec((64, 16, 128), lambda i: (0, i, 0)),
            pl.BlockSpec((16, 64, 64), lambda i: (i, 0, 0)),
        ],
        out_specs=[
            pl.BlockSpec((16, 64, 128), lambda i: (i, 0, 0)),
            pl.BlockSpec((16, 64, 128), lambda i: (i, 0, 0)),
        ],
        out_shape=[
            jax.ShapeDtypeStruct((128, 64, 128), F32),
            jax.ShapeDtypeStruct((128, 64, 128), BF16),
        ],
        scratch_shapes=[pltpu.VMEM((1024, 128), F32)],
        compiler_params=pltpu.CompilerParams(vmem_limit_bytes=48 * 2**20),
        name="prepare",
    )(place, scalars, prior, inverse)


def relax(scalars, vel, step, right_ref, packed_ref, recv_ref, mixed_ref, planes, columns, mask, store):
    @pl.when(step == 0)
    def _():
        for j in range(8):
            planes[j] = mixed_ref[pl.ds(j, 64, stride=8), :]

    y = scalars[vel, 8 + step]
    e = [planes[j] for j in range(8)]
    columns[0] = e[0] + y * (e[1] + y * (e[3] + y * e[6]))
    columns[1] = e[2] + y * (e[5] + y * e[7])
    columns[2] = e[4] + y * e[6]
    columns[3] = e[7]
    sign = scalars[vel, 0]
    lift = lift_faces(sign)
    for v in range(16):
        z = float(SPEED[v])
        equilibrium = columns[0] + z * (columns[1] + z * (columns[2] + z * columns[3]))
        recv = recv_ref[v]
        both = jnp.concatenate([recv, pltpu.roll(recv, HALF, 1)], axis=0)
        edge = jnp.where(mask, 0.0, both) * scalars[vel, 2]
        inflow = jnp.concatenate([lift[p0] * edge for p0 in range(4)], axis=0)
        hi, lo = split(right_ref[v] + equilibrium + inflow)
        packed = packed_ref[v]
        fresh = jnp.dot(
            jnp.concatenate([packed, packed], axis=1),
            jnp.concatenate([hi, hi, lo, lo], axis=0),
            preferred_element_type=F32,
        )
        store(v, fresh)


def middle_kernel(
    place, scalars, prior_ref, right_ref, packed_ref, recv_ref, mixed_ref,
    next_ref, send_ref, moments_ref,
    planes, columns, fresh_rows, scratch, own_rows, sums,
):
    step = pl.program_id(0)
    vel = place[0]
    mask = outgoing_mask(lane_index((16, 128)), scalars[vel, 0])
    totals = []

    def store(v, fresh):
        fresh_rows[pl.ds(v, 64, stride=16), :] = fresh
        send, own = own_inflow_x(fresh, place, scalars, vel, mask)
        send_ref[v] = send
        own_rows[v] = own
        z = float(SPEED[v])
        for k in range(4):
            term = (float(WEIGHT[v]) * z**k) * fresh
            if v == 0:
                sums[k] = term
            else:
                sums[k] = sums[k] + term

    relax(scalars, vel, step, right_ref, packed_ref, recv_ref, mixed_ref, planes, columns, mask, store)
    y = scalars[vel, 8 + step]
    weight = scalars[vel, 16 + step]
    s = [weight * sums[k] for k in range(4)]
    y2 = y * y
    totals = [s[0], y * s[0], s[1], y2 * s[0], s[2], y * s[1], y * (y2 * s[0] + s[2]), s[3] + y2 * s[1]]

    for j in range(8):
        rows = pl.ds(j, 64, stride=8)

        @pl.when(step == 0)
        def _(j=j, rows=rows):
            moments_ref[rows, :] = totals[j]

        @pl.when(step > 0)
        def _(j=j, rows=rows):
            moments_ref[rows, :] = moments_ref[rows, :] + totals[j]

    inflow_yz(fresh_rows.reshape(64, 16, 128), prior_ref, scratch, scalars, vel, y)
    for v in range(16):
        next_ref[v] = scratch[pl.ds(v, 64, stride=16), :] + own_rows[v]


def middle(place, scalars, prior, right, packed, recv, mixed):
    next_right, send, moments = pl.pallas_call(
        middle_kernel,
        grid=(8,),
        in_specs=[
            pl.BlockSpec(memory_space=pltpu.SMEM),
            pl.BlockSpec(memory_space=pltpu.SMEM),
            pl.BlockSpec((64, 16, 128), lambda i: (0, i, 0)),
            pl.BlockSpec((16, 64, 128), lambda i: (i, 0, 0)),
            pl.BlockSpec((16, 64, 128), lambda i: (i, 0, 0)),
            pl.BlockSpec((16, 8, 128), lambda i: (i, 0, 0)),
            pl.BlockSpec((512, 128), lambda i: (0, 0)),
        ],
        out_specs=[
            pl.BlockSpec((16, 64, 128), lambda i: (i, 0, 0)),
            pl.BlockSpec((16, 8, 128), lambda i: (i, 0, 0)),
            pl.BlockSpec((512, 128), lambda i: (0, 0)),
        ],
        out_shape=[
            jax.ShapeDtypeStruct((128, 64, 128), F32),
            jax.ShapeDtypeStruct((128, 8, 128), F32),
            jax.ShapeDtypeStruct((512, 128), F32),
        ],
        scratch_shapes=[
            pltpu.VMEM((8, 64, 128), F32),
            pltpu.VMEM((4, 64, 128), F32),
            pltpu.VMEM((1024, 128), F32),
            pltpu.VMEM((1024, 128), F32),
            pltpu.VMEM((16, 64, 128), F32),
            pltpu.VMEM((4, 64, 128), F32),
        ],
        compiler_params=pltpu.CompilerParams(vmem_limit_bytes=48 * 2**20),
        name="middle",
    )(place, scalars, prior, right, packed, recv, mixed)
    return next_right, send, moments.reshape(VEL, 16, 128)


def last_kernel(place, scalars, right_ref, packed_ref, recv_ref, mixed_ref, out_ref, planes, columns):
    step = pl.program_id(0)
    vel = place[0]
    mask = outgoing_mask(lane_index((16, 128)), scalars[vel, 0])
    flat = out_ref.reshape(1024, 128)

    def store(v, fresh):
        flat[pl.ds(v, 64, stride=16), :] = fresh

    relax(scalars, vel, step, right_ref, packed_ref, recv_ref, mixed_ref, planes, columns, mask, store)


def last(place, scalars, right, packed, recv, mixed):
    return pl.pallas_call(
        last_kernel,
        grid=(8,),
        in_specs=[
            pl.BlockSpec(memory_space=pltpu.SMEM),
            pl.BlockSpec(memory_space=pltpu.SMEM),
            pl.BlockSpec((16, 64, 128), lambda i: (i, 0, 0)),
            pl.BlockSpec((16, 64, 128), lambda i: (i, 0, 0)),
            pl.BlockSpec((16, 8, 128), lambda i: (i, 0, 0)),
            pl.BlockSpec((512, 128), lambda i: (0, 0)),
        ],
        out_specs=pl.BlockSpec((64, 16, 128), lambda i: (0, i, 0)),
        out_shape=jax.ShapeDtypeStruct((64, 128, 128), F32),
        scratch_shapes=[pltpu.VMEM((8, 64, 128), F32), pltpu.VMEM((4, 64, 128), F32)],
        compiler_params=pltpu.CompilerParams(vmem_limit_bytes=48 * 2**20),
        name="last",
    )(place, scalars, right, packed, recv, mixed)


def halo_pairs(slabs):
    pairs = []
    for slab in range(slabs):
        for vel in range(VEL):
            other = slab + 1 if SCALARS[vel, 0] > 0 else slab - 1
            if 0 <= other < slabs:
                pairs.append((slab * VEL + vel, other * VEL + vel))
    return pairs


def body(slabs, prior, block_inverse):
    shape = prior.shape
    cells = prior.reshape(64, 128, 128)
    place = jnp.stack([lax.axis_index("vel"), lax.axis_index("sp"), jnp.int32(slabs)]).astype(jnp.int32)
    scalars = jnp.asarray(SCALARS)
    hi = LOCAL.astype(jnp.bfloat16)
    lo = (LOCAL - hi.astype(np.float32)).astype(jnp.bfloat16)
    local = jnp.asarray(
        np.concatenate([np.concatenate([hi, hi], axis=2), np.concatenate([lo, lo], axis=2)], axis=1)
    )
    mix = jnp.asarray(MIX)
    axes = ("sp", "vel")
    pairs = halo_pairs(slabs)

    moments, send = first_moments(place, scalars, local, cells)
    recv = lax.ppermute(send, axes, pairs).reshape(128, 8, 128)
    mixed = sum_over_velocities(mix, moments).reshape(512, 128)
    right, packed = prepare(place, scalars, cells, block_inverse)
    right, send, moments = middle(place, scalars, cells, right, packed, recv, mixed)
    recv = lax.ppermute(send, axes, pairs)
    mixed = sum_over_velocities(mix, moments).reshape(512, 128)
    return last(place, scalars, right, packed, recv, mixed).reshape(shape)


def solution(mesh):
    spec = P(None, None, None, "vel", "sp")
    return jax.shard_map(
        functools.partial(body, mesh.shape["sp"]),
        mesh=mesh,
        in_specs=(spec, P("vel", None, None)),
        out_specs=spec,
        check_vma=False,
    )
```

```python
import functools

import jax
import jax.numpy as jnp
import numpy as np
from jax import lax
from jax.experimental import pallas as pl
from jax.experimental.pallas import tpu as pltpu
from jax.sharding import PartitionSpec as P

NV1 = 16
COUPLING = 0.25
LID_SPEED = 0.6
STEP = 6.0 / NV1
CENTRE = 0.5 * (NV1 - 1)
VEL = 32
LOCAL_Y = 8
HIGH = [float(np.sqrt(k + 0.5)) for k in range(4)]
HIGHEST = lax.Precision.HIGHEST
F32 = jnp.float32
BF16 = jnp.bfloat16
HALF = 64


def grid_speed(index):
    return (np.asarray(index, np.float64) - CENTRE) * STEP


def local_polynomials(y, z):
    r2 = y * y + z * z
    return [np.ones_like(r2), y, z, y * y, z * z, y * z, r2 * y, r2 * z]


def combination(x):
    c = np.zeros((13, 8))
    c[0, 0] = 1.0
    c[1, 0] = x
    c[2, 1] = 1.0
    c[3, 2] = 1.0
    c[4, 0] = x * x - 1.0
    c[5, 3], c[5, 0] = 1.0, -1.0
    c[6, 4], c[6, 0] = 1.0, -1.0
    c[7, 1] = x
    c[8, 2] = x
    c[9, 5] = 1.0
    c[10, 0], c[10, 3], c[10, 4] = x * (x * x - 5.0), x, x
    c[11, 1], c[11, 6] = x * x - 5.0, 1.0
    c[12, 2], c[12, 7] = x * x - 5.0, 1.0
    return c


def tables():
    speed = grid_speed(np.arange(NV1))
    weight = np.exp(-0.5 * speed * speed)
    total = weight.sum()
    weight = weight / total
    x, y, z = np.meshgrid(speed, speed, speed, indexing="ij")
    w = weight[:, None, None] * weight[None, :, None] * weight[None, None, :]
    g = np.stack(local_polynomials(y, z))
    per_x = np.stack([combination(s) for s in speed])
    h = np.einsum("xkj,jxyz->kxyz", per_x, g)
    norm = (w * h * h).sum(axis=(1, 2, 3))
    source = np.repeat(per_x * weight[:, None, None], 2, axis=0)
    target = np.repeat(per_x, 2, axis=0)
    mix = np.einsum("tkj,k,ski->tjsi", target, 1.0 / norm, source).reshape(VEL * 8, VEL * 8)
    return mix.astype(np.float32), speed, weight, float(total)


MIX, SPEED, WEIGHT, TOTAL = tables()


def split(a):
    hi = a.astype(BF16)
    return hi, (a - hi.astype(F32)).astype(BF16)


def lane_index(shape):
    return lax.broadcasted_iota(jnp.int32, shape, len(shape) - 1)


def row_index(shape):
    return lax.broadcasted_iota(jnp.int32, shape, len(shape) - 2)


class Place:
    def __init__(self, slabs):
        vel, slab = lax.axis_index("vel"), lax.axis_index("sp")
        self.vx = (vel // 2).astype(F32) * STEP - CENTRE * STEP
        self.sign_x = jnp.where(vel >= VEL // 2, 1.0, -1.0)
        self.scale_x = COUPLING * jnp.abs(self.vx)
        self.first_y = vel % 2 * LOCAL_Y
        self.sign_y = jnp.where(vel % 2 == 1, 1.0, -1.0)
        boundary = jnp.where(vel >= VEL // 2, 0, slabs - 1)
        self.wall_x = jnp.where(slab == boundary, 2.0, 0.0)

    def speed_y(self, step):
        return (self.first_y + step).astype(F32) * STEP - CENTRE * STEP


def outgoing_mask(lane, sign):
    return jnp.where(sign > 0, lane, 2 * HALF - 1 - lane) >= HALF


def trace_face(sign):
    return [HIGH[k] if k % 2 == 0 else HIGH[k] * sign for k in range(4)]


def lift_faces(sign):
    return [HIGH[k] if k % 2 == 0 else -HIGH[k] * sign for k in range(4)]


def kept(*shape, dtype=F32):
    return pltpu.VMEM(shape, dtype)


def here(x):
    return pltpu.with_memory_space_constraint(x, pltpu.VMEM)


def away(x):
    return pltpu.with_memory_space_constraint(x, pltpu.HBM)


def velocity_block(ref, step):
    return ref.at[pl.ds(pl.multiple_of(step * 16, 16), 16)]


def mode_block(ref, step):
    return ref.at[:, pl.ds(pl.multiple_of(step * 16, 16), 16), :]


def stream(pairs):
    def copies(step):
        return [pltpu.make_async_copy(source(step), target(step), sems.at[step]) for source, target, sems in pairs]

    def start(step):
        for copy in copies(step):
            copy.start()

    def wait(step):
        for copy in copies(step):
            copy.wait()

    return start, wait


AHEAD = 8


def start_first(start):
    for step in range(AHEAD):
        start(step)


def start_later(start, step):
    @pl.when(step + AHEAD < 8)
    def _():
        start(step + AHEAD)


BLOCKS_V = pltpu.VMEM((128, 64, 128), F32)
BLOCKS_Q = pltpu.VMEM((8, 64, 16, 128), F32)
SEMS = pltpu.SemaphoreType.DMA((8,))


VMEM = pl.BlockSpec(memory_space=pltpu.VMEM)
HBM = pl.BlockSpec(memory_space=pltpu.HBM)
PARAMS = pltpu.CompilerParams(vmem_limit_bytes=24 * 2**20)


def moment_weights(first_y):
    lane, row = lane_index((8, 128)), row_index((8, 128))
    y = (lane // 16 + first_y).astype(F32) * STEP - CENTRE * STEP
    z = (lane % 16).astype(F32) * STEP - CENTRE * STEP
    r2 = y * y + z * z
    polynomial = jnp.ones((8, 128), F32)
    for j, g in enumerate([y, z, y * y, z * z, y * z, r2 * y, r2 * z]):
        polynomial = jnp.where(row == j + 1, g, polynomial)
    hi, lo = split(polynomial * jnp.exp(-0.5 * r2) * (1.0 / (TOTAL * TOTAL)))
    half = jnp.concatenate([hi.astype(F32), lo.astype(F32)], axis=0).astype(BF16)
    return jnp.concatenate([half, half], axis=1)


def first_moments_kernel(prior, moments, cells, arrived):
    copies = []
    for step in range(8):
        part = pl.ds(step * 8, 8)
        copies.append(pltpu.make_async_copy(prior.at[part], cells.at[part], arrived.at[step]))
        copies[-1].start()
    weights = moment_weights(lax.axis_index("vel") % 2 * LOCAL_Y)
    for step in range(8):
        copies[step].wait()
        for q in range(step * 8, step * 8 + 8):
            hi, lo = split(cells[q])
            both = jnp.concatenate([hi, lo], axis=0)
            product = jnp.dot(weights, both, preferred_element_type=F32)
            moments[q] = product[:8] + product[8:]


def first_moments(prior):
    return pl.pallas_call(
        first_moments_kernel,
        in_specs=[HBM],
        out_specs=VMEM,
        out_shape=kept(64, 8, 128),
        scratch_shapes=[pltpu.VMEM((64, 128, 128), F32), SEMS],
        compiler_params=PARAMS,
        name="first_moments",
    )(away(prior)).reshape(VEL, 16, 128)


def pack_kernel(inverse, packed, rows, blocks, arrived):
    fetch, wait = stream([(lambda i: inverse.at[pl.ds(i * 8, 8)], lambda i: blocks.at[pl.ds(i * 8, 8)], arrived)])
    for step in range(8):
        fetch(step)
    for step in range(8):
        wait(step)
        for p in range(step * 8, step * 8 + 8):
            hi, lo = split(blocks[p])
            both = jnp.concatenate([hi.astype(F32), lo.astype(F32)], axis=0)
            rows[pl.ds(p, 128, stride=PITCH), :] = both.T

    def step(v, carry):
        packed[v] = rows[pl.ds(pl.multiple_of(v * PITCH, 8), 64), :].astype(BF16)
        return carry

    lax.fori_loop(0, 128, step, 0, unroll=8)


PITCH = 72


def pack(inverse):
    return pl.pallas_call(
        pack_kernel,
        in_specs=[HBM],
        out_specs=VMEM,
        out_shape=kept(128, 64, 128, dtype=BF16),
        scratch_shapes=[pltpu.VMEM((128 * PITCH, 128), F32), pltpu.VMEM((64, 64, 128), F32), SEMS],
        compiler_params=PARAMS,
        name="pack",
    )(away(jnp.transpose(inverse, (1, 2, 0))))


def mix_kernel(mix, gathered, mixed):
    part = jnp.concatenate([gathered[:, low * 8 : low * 8 + 8, :].reshape(VEL * 8, 128) for low in range(2)], axis=1)
    result = jnp.dot(mix[...], part, preferred_element_type=F32, precision=HIGHEST)
    for low in range(2):
        mixed[:, low * 8 : low * 8 + 8, :] = result[:, low * 128 : low * 128 + 128].reshape(VEL, 8, 128)


def mix_moments(mix, gathered):
    return pl.pallas_call(
        mix_kernel,
        in_specs=[VMEM, VMEM],
        out_specs=VMEM,
        out_shape=kept(VEL, 16, 128),
        compiler_params=PARAMS,
        name="mix_moments",
    )(here(mix), here(gathered))


def sum_over_velocities(mix, partial_sums, beside):
    gathered = lax.all_to_all(partial_sums, "vel", 0, 0)
    gathered, beside = lax.optimization_barrier((gathered, beside))
    mixed = mix_moments(mix, gathered)
    mixed, beside = lax.optimization_barrier((mixed, beside))
    return lax.all_to_all(mixed, "vel", 0, 0).reshape(512, 128), beside


def add_inflow(source, base, target, send, place, step, mask):
    y = place.speed_y(step)
    lane, row = lane_index((8, 128)), row_index((8, 128))
    trace_x, lift_x = trace_face(place.sign_x), lift_faces(place.sign_x)
    trace_y, lift_y = trace_face(place.sign_y), lift_faces(place.sign_y)
    up_y = place.sign_y > 0
    shift_y = jnp.where(up_y, 8, 120)
    cell_y = jnp.where(up_y, lane // 8 % 8, 7 - lane // 8 % 8)
    scale_y = jnp.where(cell_y > 0, COUPLING * jnp.abs(y), 0.0)
    wall_y = jnp.where(cell_y > 0, 0.0, 2.0 * COUPLING * jnp.abs(y))
    scale_x = jnp.where(mask, place.scale_x, 0.0)
    wall_x = jnp.where(mask, 0.0, place.wall_x * place.scale_x)
    lid = 2.0 * jnp.exp(jnp.full((8, 128), LID_SPEED, F32) * place.vx - 0.5 * LID_SPEED * LID_SPEED)
    for part in range(2):
        up = part == 1
        speed = jnp.abs((row + (part * 8)).astype(F32) - CENTRE) * (STEP * COUPLING)
        inside = (lane % 8 > 0) if up else (lane % 8 < 7)
        scale_z = jnp.where(inside, speed, 0.0)
        wall_z = jnp.where(inside, 0.0, speed * (2.0 if up else lid))
        trace_z, lift_z = trace_face(1.0 if up else -1.0), lift_faces(1.0 if up else -1.0)
        rows = pl.ds(pl.multiple_of(step * 16 + part * 8, 8), 8)
        face_x = [None] * 16
        for low in range(8):
            pair = []
            for r in (low, low + 8):
                trace = sum(trace_x[p0] * source(part, p0 * 16 + r) for p0 in range(4))
                turned = pltpu.roll(trace, HALF, 1)
                pair.append((trace, turned))
                face_x[r] = turned * scale_x
            send[low, rows, :] = jnp.where(mask, pair[1][0], pair[0][1])
        face_x[0] = face_x[0] + wall_x
        for p0 in range(4):
            x = [[source(part, p0 * 16 + p1 * 4 + p2) for p2 in range(4)] for p1 in range(4)]
            face_y, face_z = [], []
            for k in range(4):
                ty = sum(trace_y[p1] * x[p1][k] for p1 in range(4))
                ty = pltpu.roll(ty, shift_y, 1) * scale_y
                tz = sum(trace_z[p2] * x[k][p2] for p2 in range(4))
                tz = pltpu.roll(tz, 1 if up else 127, 1) * scale_z
                if p0 == 0 and k == 0:
                    ty = ty + wall_y
                    tz = tz + wall_z
                face_y.append(ty)
                face_z.append(tz)
            for p1 in range(4):
                for p2 in range(4):
                    q, r = p0 * 16 + p1 * 4 + p2, p1 * 4 + p2
                    value = base(part, q) + lift_x[p0] * face_x[r] + lift_y[p1] * face_y[p2] + lift_z[p2] * face_z[p1]
                    target[part * 512 + q * 8 : part * 512 + q * 8 + 8, :] = value


def velocity_rows(v):
    return pl.ds(v // 8 * 512 + v % 8, 64, stride=8)


def block_reader(ref):
    def read(part, q):
        return ref[q, part * 8 : part * 8 + 8, :]

    return read


def row_reader(ref):
    def read(part, q):
        return ref[part * 512 + q * 8 : part * 512 + q * 8 + 8, :]

    return read


def prepare_kernel(slabs, prior, right, send, scratch, cells, made, arrived, sent):
    place = Place(slabs)
    mask = outgoing_mask(lane_index((8, 128)), place.sign_x)
    fetch, wait = stream([(lambda i: mode_block(prior, i), lambda i: cells.at[i], arrived)])
    put, finish = stream([(lambda i: velocity_block(made, i), lambda i: velocity_block(right, i), sent)])
    start_first(fetch)

    def loop(step, carry):
        wait(step)
        start_later(fetch, step)
        read = block_reader(cells.at[step])
        add_inflow(read, read, scratch, send, place, step, mask)
        for v in range(16):
            made[step * 16 + v] = scratch[velocity_rows(v), :]
        put(step)
        return carry

    lax.fori_loop(0, 8, loop, 0)
    for step in range(8):
        finish(step)


def prepare(slabs, prior):
    return pl.pallas_call(
        functools.partial(prepare_kernel, slabs),
        in_specs=[HBM],
        out_specs=[HBM, VMEM],
        out_shape=[pltpu.HBM((128, 64, 128), F32), kept(8, 128, 128)],
        scratch_shapes=[pltpu.VMEM((1024, 128), F32), BLOCKS_Q, BLOCKS_V, SEMS, SEMS],
        compiler_params=PARAMS,
        name="prepare",
    )(away(prior))


def prepare_next_kernel(
    slabs, fresh, prior, right, send, rows, scratch, columns, cells, made, arrived, arrived_prior, sent
):
    place = Place(slabs)
    mask = outgoing_mask(lane_index((8, 128)), place.sign_x)
    fetch, wait = stream(
        [
            (lambda i: velocity_block(fresh, i), lambda i: velocity_block(columns, i), arrived),
            (lambda i: mode_block(prior, i), lambda i: cells.at[i], arrived_prior),
        ]
    )
    put, finish = stream([(lambda i: velocity_block(made, i), lambda i: velocity_block(right, i), sent)])
    start_first(fetch)

    def loop(step, carry):
        wait(step)
        start_later(fetch, step)
        for v in range(16):
            rows[velocity_rows(v), :] = columns[step * 16 + v]
        add_inflow(row_reader(rows), block_reader(cells.at[step]), scratch, send, place, step, mask)
        for v in range(16):
            made[step * 16 + v] = scratch[velocity_rows(v), :]
        put(step)
        return carry

    lax.fori_loop(0, 8, loop, 0)
    for step in range(8):
        finish(step)


def prepare_next(slabs, fresh, prior):
    return pl.pallas_call(
        functools.partial(prepare_next_kernel, slabs),
        in_specs=[HBM, HBM],
        out_specs=[HBM, VMEM],
        out_shape=[pltpu.HBM((128, 64, 128), F32), kept(8, 128, 128)],
        scratch_shapes=[
            pltpu.VMEM((1024, 128), F32),
            pltpu.VMEM((1024, 128), F32),
            BLOCKS_V,
            BLOCKS_Q,
            BLOCKS_V,
            SEMS,
            SEMS,
            SEMS,
        ],
        compiler_params=PARAMS,
        name="prepare_next",
    )(away(fresh), away(prior))


def split_planes(mixed, planes):
    for j in range(8):
        planes[j] = mixed[pl.ds(j, 64, stride=8), :]


def relax(place, step, right, packed, recv, planes, columns, mask, store):
    y = place.speed_y(step)
    columns[0] = planes[0] + y * (planes[1] + y * (planes[3] + y * planes[6]))
    columns[1] = planes[2] + y * (planes[5] + y * planes[7])
    columns[2] = planes[4] + y * planes[6]
    columns[3] = planes[7]
    lift = lift_faces(place.sign_x)
    for low in range(8):
        z = float(SPEED[15 - low])
        even = columns[0] + (z * z) * columns[2]
        odd = z * columns[1] + (z * z * z) * columns[3]
        for v, equilibrium in ((low, even - odd), (15 - low, even + odd)):
            at = step * 16 + v
            edge = recv[pl.ds(at, 8, stride=128), :]
            both = jnp.concatenate([edge, pltpu.roll(edge, HALF, 1)], axis=0)
            both = jnp.where(mask, 0.0, both) * place.scale_x
            inflow = jnp.concatenate([lift[p0] * both for p0 in range(4)], axis=0)
            hi, lo = split(right[at] + equilibrium + inflow)
            block = packed[at]
            fresh = jnp.dot(
                jnp.concatenate([block, block], axis=1),
                jnp.concatenate([hi, hi, lo, lo], axis=0),
                preferred_element_type=F32,
            )
            store(v, fresh)


def middle_kernel(
    slabs, right_away, packed, recv, mixed, fresh_away, moments, planes, columns, sums, right, fresh, arrived, sent
):
    place = Place(slabs)
    mask = outgoing_mask(lane_index((16, 128)), place.sign_x)
    fetch, wait = stream([(lambda i: velocity_block(right_away, i), lambda i: velocity_block(right, i), arrived)])
    put, finish = stream([(lambda i: velocity_block(fresh, i), lambda i: velocity_block(fresh_away, i), sent)])
    start_first(fetch)
    split_planes(mixed, planes)
    sums[...] = jnp.zeros_like(sums)

    def loop(step, carry):
        def store(v, column):
            fresh[step * 16 + v] = column

        wait(step)
        start_later(fetch, step)
        relax(place, step, right, packed, recv, planes, columns, mask, store)
        put(step)
        y = place.speed_y(step)
        weight = jnp.exp(jnp.full((64, 128), -0.5, F32) * (y * y)) * (1.0 / TOTAL)
        s = [None] * 4
        for low in range(8):
            z, w = float(SPEED[15 - low]), float(WEIGHT[low])
            minus, plus = fresh[step * 16 + low], fresh[step * 16 + 15 - low]
            terms = [w * (plus + minus), (w * z) * (plus - minus)]
            for k in range(4):
                term = terms[k % 2] if k < 2 else (z * z) * terms[k % 2]
                s[k] = term if s[k] is None else s[k] + term
        s = [weight * part for part in s]
        y2 = y * y
        totals = [s[0], y * s[0], s[1], y2 * s[0], s[2], y * s[1], y * (y2 * s[0] + s[2]), s[3] + y2 * s[1]]
        for j in range(8):
            sums[j] = sums[j] + totals[j]
        return carry

    lax.fori_loop(0, 8, loop, 0)
    for j in range(8):
        moments[pl.ds(j, 64, stride=8), :] = sums[j]
    for step in range(8):
        finish(step)


def middle(slabs, right, packed, recv, mixed):
    fresh, moments = pl.pallas_call(
        functools.partial(middle_kernel, slabs),
        in_specs=[HBM, VMEM, VMEM, VMEM],
        out_specs=[HBM, VMEM],
        out_shape=[pltpu.HBM((128, 64, 128), F32), kept(512, 128)],
        scratch_shapes=[
            pltpu.VMEM((8, 64, 128), F32),
            pltpu.VMEM((4, 64, 128), F32),
            pltpu.VMEM((8, 64, 128), F32),
            BLOCKS_V,
            BLOCKS_V,
            SEMS,
            SEMS,
        ],
        compiler_params=PARAMS,
        name="middle",
    )(away(right), here(packed), here(recv), here(mixed))
    return fresh, moments.reshape(VEL, 16, 128)


def last_kernel(slabs, right_away, packed, recv, mixed, out, planes, columns, right, blocks, arrived, sent):
    place = Place(slabs)
    mask = outgoing_mask(lane_index((16, 128)), place.sign_x)
    fetch, wait = stream([(lambda i: velocity_block(right_away, i), lambda i: velocity_block(right, i), arrived)])
    put, finish = stream([(lambda i: blocks.at[i], lambda i: mode_block(out, i), sent)])
    start_first(fetch)
    split_planes(mixed, planes)

    def loop(step, carry):
        flat = blocks.at[step].reshape(1024, 128)

        def store(v, fresh):
            flat[pl.ds(v, 64, stride=16), :] = fresh

        wait(step)
        start_later(fetch, step)
        relax(place, step, right, packed, recv, planes, columns, mask, store)
        put(step)
        return carry

    lax.fori_loop(0, 8, loop, 0)
    for step in range(8):
        finish(step)


def last(slabs, right, packed, recv, mixed):
    return pl.pallas_call(
        functools.partial(last_kernel, slabs),
        in_specs=[HBM, VMEM, VMEM, VMEM],
        out_specs=HBM,
        out_shape=pltpu.HBM((64, 128, 128), F32),
        scratch_shapes=[
            pltpu.VMEM((8, 64, 128), F32),
            pltpu.VMEM((4, 64, 128), F32),
            BLOCKS_V,
            BLOCKS_Q,
            SEMS,
            SEMS,
        ],
        compiler_params=PARAMS,
        name="last",
    )(away(right), here(packed), here(recv), here(mixed))


def halo_pairs(slabs):
    pairs = []
    for slab in range(slabs):
        for vel in range(VEL):
            other = slab + 1 if vel >= VEL // 2 else slab - 1
            if 0 <= other < slabs:
                pairs.append((slab * VEL + vel, other * VEL + vel))
    return pairs


def body(slabs, prior, block_inverse):
    mix = jnp.asarray(MIX)
    axes = ("sp", "vel")
    pairs = halo_pairs(slabs)
    cells = prior.reshape(64, 128, 128)
    moments = first_moments(cells)
    mixed, (right, send) = sum_over_velocities(mix, moments, prepare(slabs, cells))
    recv = lax.ppermute(send, axes, pairs).reshape(1024, 128)
    packed = pack(block_inverse)
    fresh, moments = middle(slabs, right, packed, recv, mixed)
    mixed, (right, send) = sum_over_velocities(mix, moments, prepare_next(slabs, fresh, cells))
    recv = lax.ppermute(send, axes, pairs).reshape(1024, 128)
    return last(slabs, right, packed, recv, mixed).reshape(prior.shape)


def solution(mesh):
    spec = P(None, None, None, "vel", "sp")
    return jax.shard_map(
        functools.partial(body, mesh.shape["sp"]),
        mesh=mesh,
        in_specs=(spec, P("vel", None, None)),
        out_specs=spec,
        check_vma=False,
    )
```

```python
import functools

import jax
import jax.numpy as jnp
import numpy as np
from jax import lax
from jax.experimental import pallas as pl
from jax.experimental.pallas import tpu as pltpu
from jax.sharding import PartitionSpec as P

NV1 = 16
COUPLING = 0.25
LID_SPEED = 0.6
STEP = 6.0 / NV1
CENTRE = 0.5 * (NV1 - 1)
VEL = 32
LOCAL_Y = 8
HIGH = [float(np.sqrt(k + 0.5)) for k in range(4)]
HIGHEST = lax.Precision.HIGHEST
F32 = jnp.float32
BF16 = jnp.bfloat16
HALF = 64


def ring_hops(vel):
    y, z = vel // 4 % 4, vel % 4
    return vel // 16 + min(y, 4 - y) + min(z, 4 - z)


ORDER = sorted(range(VEL), key=lambda vel: -ring_hops(vel))


def grid_speed(index):
    return (np.asarray(index, np.float64) - CENTRE) * STEP


def local_polynomials(y, z):
    r2 = y * y + z * z
    return [np.ones_like(r2), y, z, y * y, z * z, y * z, r2 * y, r2 * z]


def combination(x):
    c = np.zeros((13, 8))
    c[0, 0] = 1.0
    c[1, 0] = x
    c[2, 1] = 1.0
    c[3, 2] = 1.0
    c[4, 0] = x * x - 1.0
    c[5, 3], c[5, 0] = 1.0, -1.0
    c[6, 4], c[6, 0] = 1.0, -1.0
    c[7, 1] = x
    c[8, 2] = x
    c[9, 5] = 1.0
    c[10, 0], c[10, 3], c[10, 4] = x * (x * x - 5.0), x, x
    c[11, 1], c[11, 6] = x * x - 5.0, 1.0
    c[12, 2], c[12, 7] = x * x - 5.0, 1.0
    return c


def tables():
    speed = grid_speed(np.arange(NV1))
    weight = np.exp(-0.5 * speed * speed)
    total = weight.sum()
    weight = weight / total
    x, y, z = np.meshgrid(speed, speed, speed, indexing="ij")
    w = weight[:, None, None] * weight[None, :, None] * weight[None, None, :]
    g = np.stack(local_polynomials(y, z))
    per_x = np.stack([combination(s) for s in speed])
    h = np.einsum("xkj,jxyz->kxyz", per_x, g)
    norm = (w * h * h).sum(axis=(1, 2, 3))
    source = np.repeat(per_x * weight[:, None, None], 2, axis=0)
    target = np.repeat(per_x, 2, axis=0)
    mix = np.einsum("tkj,k,ski->tjsi", target, 1.0 / norm, source).reshape(VEL * 8, VEL * 8)
    mix = mix.reshape(VEL, 8, VEL, 8)[ORDER][:, :, ORDER].reshape(VEL * 8, VEL * 8)
    return mix.astype(np.float32), speed, weight, float(total)


MIX, SPEED, WEIGHT, TOTAL = tables()


def split(a):
    hi = a.astype(BF16)
    return hi, (a - hi.astype(F32)).astype(BF16)


def lane_index(shape):
    return lax.broadcasted_iota(jnp.int32, shape, len(shape) - 1)


def row_index(shape):
    return lax.broadcasted_iota(jnp.int32, shape, len(shape) - 2)


class Place:
    def __init__(self, slabs):
        vel, slab = lax.axis_index("vel"), lax.axis_index("sp")
        self.vx = (vel // 2).astype(F32) * STEP - CENTRE * STEP
        self.sign_x = jnp.where(vel >= VEL // 2, 1.0, -1.0)
        self.scale_x = COUPLING * jnp.abs(self.vx)
        self.first_y = vel % 2 * LOCAL_Y
        self.sign_y = jnp.where(vel % 2 == 1, 1.0, -1.0)
        boundary = jnp.where(vel >= VEL // 2, 0, slabs - 1)
        self.wall_x = jnp.where(slab == boundary, 2.0, 0.0)

    def speed_y(self, step):
        return (self.first_y + step).astype(F32) * STEP - CENTRE * STEP


def outgoing_mask(lane, sign):
    return jnp.where(sign > 0, lane, 2 * HALF - 1 - lane) >= HALF


def trace_face(sign):
    return [HIGH[k] if k % 2 == 0 else HIGH[k] * sign for k in range(4)]


def lift_faces(sign):
    return [HIGH[k] if k % 2 == 0 else -HIGH[k] * sign for k in range(4)]


def kept(*shape, dtype=F32):
    return pltpu.VMEM(shape, dtype)


def here(x):
    return pltpu.with_memory_space_constraint(x, pltpu.VMEM)


def away(x):
    return pltpu.with_memory_space_constraint(x, pltpu.HBM)


def velocity_block(ref, step):
    return ref.at[pl.ds(pl.multiple_of(step * 16, 16), 16)]


def mode_block(ref, step):
    return ref.at[:, pl.ds(pl.multiple_of(step * 16, 16), 16), :]


def stream(pairs):
    def copies(step):
        return [pltpu.make_async_copy(source(step), target(step), sems.at[step]) for source, target, sems in pairs]

    def start(step):
        for copy in copies(step):
            copy.start()

    def wait(step):
        for copy in copies(step):
            copy.wait()

    return start, wait


def start_all(start):
    for step in range(8):
        start(step)


BLOCKS_V = pltpu.VMEM((128, 64, 128), F32)
BLOCKS_Q = pltpu.VMEM((8, 64, 16, 128), F32)
SEMS = pltpu.SemaphoreType.DMA((8,))


VMEM = pl.BlockSpec(memory_space=pltpu.VMEM)
HBM = pl.BlockSpec(memory_space=pltpu.HBM)
PARAMS = pltpu.CompilerParams(vmem_limit_bytes=24 * 2**20)


def moment_weights(first_y):
    lane, row = lane_index((8, 128)), row_index((8, 128))
    y = (lane // 16 + first_y).astype(F32) * STEP - CENTRE * STEP
    z = (lane % 16).astype(F32) * STEP - CENTRE * STEP
    r2 = y * y + z * z
    polynomial = jnp.ones((8, 128), F32)
    for j, g in enumerate([y, z, y * y, z * z, y * z, r2 * y, r2 * z]):
        polynomial = jnp.where(row == j + 1, g, polynomial)
    hi, lo = split(polynomial * jnp.exp(-0.5 * r2) * (1.0 / (TOTAL * TOTAL)))
    half = jnp.concatenate([hi.astype(F32), lo.astype(F32)], axis=0).astype(BF16)
    return jnp.concatenate([half, half], axis=1)


def first_moments_kernel(prior, moments, cells, sums, arrived, sent):
    def part(ref, step):
        return ref.at[pl.ds(step * 8, 8)]

    fetch, wait = stream([(lambda i: part(prior, i), lambda i: part(cells, i), arrived)])
    put, finish = stream([(lambda i: part(sums, i), lambda i: part(moments, i), sent)])
    start_all(fetch)
    weights = moment_weights(lax.axis_index("vel") % 2 * LOCAL_Y)
    for step in range(8):
        wait(step)
        for q in range(step * 8, step * 8 + 8):
            hi, lo = split(cells[q])
            product = jnp.dot(weights, jnp.concatenate([hi, lo], axis=0), preferred_element_type=F32)
            sums[q] = product[:8] + product[8:]
        put(step)
    for step in range(8):
        finish(step)


def first_moments(prior):
    return pl.pallas_call(
        first_moments_kernel,
        in_specs=[HBM],
        out_specs=HBM,
        out_shape=pltpu.HBM((64, 8, 128), F32),
        scratch_shapes=[pltpu.VMEM((64, 128, 128), F32), pltpu.VMEM((64, 8, 128), F32), SEMS, SEMS],
        compiler_params=PARAMS,
        name="first_moments",
    )(away(prior)).reshape(VEL, 16, 128)


def pack_kernel(inverse, packed, rows, blocks, arrived):
    fetch, wait = stream([(lambda i: inverse.at[pl.ds(i * 8, 8)], lambda i: blocks.at[pl.ds(i * 8, 8)], arrived)])
    for step in range(8):
        fetch(step)
    for step in range(8):
        wait(step)
        for p in range(step * 8, step * 8 + 8):
            hi, lo = split(blocks[p])
            both = jnp.concatenate([hi.astype(F32), lo.astype(F32)], axis=0)
            rows[pl.ds(p, 128, stride=PITCH), :] = both.T

    def step(v, carry):
        packed[v] = rows[pl.ds(pl.multiple_of(v * PITCH, 8), 64), :].astype(BF16)
        return carry

    lax.fori_loop(0, 128, step, 0, unroll=8)


PITCH = 72


def pack(inverse):
    return pl.pallas_call(
        pack_kernel,
        in_specs=[HBM],
        out_specs=VMEM,
        out_shape=kept(128, 64, 128, dtype=BF16),
        scratch_shapes=[pltpu.VMEM((128 * PITCH, 128), F32), pltpu.VMEM((64, 64, 128), F32), SEMS],
        compiler_params=PARAMS,
        name="pack",
    )(away(jnp.transpose(inverse, (1, 2, 0))))


def mix_kernel(mix, gathered, mixed):
    part = jnp.concatenate([gathered[:, low * 8 : low * 8 + 8, :].reshape(VEL * 8, 128) for low in range(2)], axis=1)
    result = jnp.dot(mix[...], part, preferred_element_type=F32, precision=HIGHEST)
    for low in range(2):
        mixed[:, low * 8 : low * 8 + 8, :] = result[:, low * 128 : low * 128 + 128].reshape(VEL, 8, 128)


def mix_moments(mix, gathered):
    return pl.pallas_call(
        mix_kernel,
        in_specs=[VMEM, VMEM],
        out_specs=VMEM,
        out_shape=kept(VEL, 16, 128),
        compiler_params=PARAMS,
        name="mix_moments",
    )(here(mix), here(gathered))


def sum_over_velocities(mix, partial_sums, beside):
    gathered = lax.all_to_all(partial_sums, "vel", 0, 0, axis_index_groups=[ORDER])
    gathered, beside = lax.optimization_barrier((gathered, beside))
    mixed = mix_moments(mix, gathered)
    mixed, beside = lax.optimization_barrier((mixed, beside))
    return lax.all_to_all(mixed, "vel", 0, 0, axis_index_groups=[ORDER]).reshape(512, 128), beside


def add_inflow(source, base, target, send, place, step, mask):
    y = place.speed_y(step)
    lane, row = lane_index((8, 128)), row_index((8, 128))
    trace_x, lift_x = trace_face(place.sign_x), lift_faces(place.sign_x)
    trace_y, lift_y = trace_face(place.sign_y), lift_faces(place.sign_y)
    up_y = place.sign_y > 0
    shift_y = jnp.where(up_y, 8, 120)
    cell_y = jnp.where(up_y, lane // 8 % 8, 7 - lane // 8 % 8)
    scale_y = jnp.where(cell_y > 0, COUPLING * jnp.abs(y), 0.0)
    wall_y = jnp.where(cell_y > 0, 0.0, 2.0 * COUPLING * jnp.abs(y))
    scale_x = jnp.where(mask, place.scale_x, 0.0)
    wall_x = jnp.where(mask, 0.0, place.wall_x * place.scale_x)
    lid = 2.0 * jnp.exp(jnp.full((8, 128), LID_SPEED, F32) * place.vx - 0.5 * LID_SPEED * LID_SPEED)
    for part in range(2):
        up = part == 1
        speed = jnp.abs((row + (part * 8)).astype(F32) - CENTRE) * (STEP * COUPLING)
        inside = (lane % 8 > 0) if up else (lane % 8 < 7)
        scale_z = jnp.where(inside, speed, 0.0)
        wall_z = jnp.where(inside, 0.0, speed * (2.0 if up else lid))
        trace_z, lift_z = trace_face(1.0 if up else -1.0), lift_faces(1.0 if up else -1.0)
        rows = pl.ds(pl.multiple_of(step * 16 + part * 8, 8), 8)
        face_x = [None] * 16
        for low in range(8):
            pair = []
            for r in (low, low + 8):
                trace = sum(trace_x[p0] * source(part, p0 * 16 + r) for p0 in range(4))
                turned = pltpu.roll(trace, HALF, 1)
                pair.append((trace, turned))
                face_x[r] = turned * scale_x
            send[low, rows, :] = jnp.where(mask, pair[1][0], pair[0][1])
        face_x[0] = face_x[0] + wall_x
        for p0 in range(4):
            x = [[source(part, p0 * 16 + p1 * 4 + p2) for p2 in range(4)] for p1 in range(4)]
            face_y, face_z = [], []
            for k in range(4):
                ty = sum(trace_y[p1] * x[p1][k] for p1 in range(4))
                ty = pltpu.roll(ty, shift_y, 1) * scale_y
                tz = sum(trace_z[p2] * x[k][p2] for p2 in range(4))
                tz = pltpu.roll(tz, 1 if up else 127, 1) * scale_z
                if p0 == 0 and k == 0:
                    ty = ty + wall_y
                    tz = tz + wall_z
                face_y.append(ty)
                face_z.append(tz)
            for p1 in range(4):
                for p2 in range(4):
                    q, r = p0 * 16 + p1 * 4 + p2, p1 * 4 + p2
                    value = base(part, q) + lift_x[p0] * face_x[r] + lift_y[p1] * face_y[p2] + lift_z[p2] * face_z[p1]
                    target[part * 512 + q * 8 : part * 512 + q * 8 + 8, :] = value


def velocity_rows(v):
    return pl.ds(v // 8 * 512 + v % 8, 64, stride=8)


def block_reader(ref):
    def read(part, q):
        return ref[q, part * 8 : part * 8 + 8, :]

    return read


def row_reader(ref):
    def read(part, q):
        return ref[part * 512 + q * 8 : part * 512 + q * 8 + 8, :]

    return read


def prepare_kernel(slabs, prior, right, send, scratch, cells, made, arrived, sent):
    place = Place(slabs)
    mask = outgoing_mask(lane_index((8, 128)), place.sign_x)
    fetch, wait = stream([(lambda i: mode_block(prior, i), lambda i: cells.at[i], arrived)])
    put, finish = stream([(lambda i: velocity_block(made, i), lambda i: velocity_block(right, i), sent)])
    start_all(fetch)

    def loop(step, carry):
        wait(step)
        read = block_reader(cells.at[step])
        add_inflow(read, read, scratch, send, place, step, mask)
        for v in range(16):
            made[step * 16 + v] = scratch[velocity_rows(v), :]
        put(step)
        return carry

    lax.fori_loop(0, 8, loop, 0)
    for step in range(8):
        finish(step)


def prepare(slabs, prior):
    return pl.pallas_call(
        functools.partial(prepare_kernel, slabs),
        in_specs=[HBM],
        out_specs=[HBM, VMEM],
        out_shape=[pltpu.HBM((128, 64, 128), F32), kept(8, 128, 128)],
        scratch_shapes=[pltpu.VMEM((1024, 128), F32), BLOCKS_Q, BLOCKS_V, SEMS, SEMS],
        compiler_params=PARAMS,
        name="prepare",
    )(away(prior))


def prepare_next_kernel(
    slabs, fresh, prior, right, send, rows, scratch, columns, cells, made, arrived, arrived_prior, sent
):
    place = Place(slabs)
    mask = outgoing_mask(lane_index((8, 128)), place.sign_x)
    fetch, wait = stream(
        [
            (lambda i: velocity_block(fresh, i), lambda i: velocity_block(columns, i), arrived),
            (lambda i: mode_block(prior, i), lambda i: cells.at[i], arrived_prior),
        ]
    )
    put, finish = stream([(lambda i: velocity_block(made, i), lambda i: velocity_block(right, i), sent)])
    start_all(fetch)

    def loop(step, carry):
        wait(step)
        for v in range(16):
            rows[velocity_rows(v), :] = columns[step * 16 + v]
        add_inflow(row_reader(rows), block_reader(cells.at[step]), scratch, send, place, step, mask)
        for v in range(16):
            made[step * 16 + v] = scratch[velocity_rows(v), :]
        put(step)
        return carry

    lax.fori_loop(0, 8, loop, 0)
    for step in range(8):
        finish(step)


def prepare_next(slabs, fresh, prior):
    return pl.pallas_call(
        functools.partial(prepare_next_kernel, slabs),
        in_specs=[HBM, HBM],
        out_specs=[HBM, VMEM],
        out_shape=[pltpu.HBM((128, 64, 128), F32), kept(8, 128, 128)],
        scratch_shapes=[
            pltpu.VMEM((1024, 128), F32),
            pltpu.VMEM((1024, 128), F32),
            BLOCKS_V,
            BLOCKS_Q,
            BLOCKS_V,
            SEMS,
            SEMS,
            SEMS,
        ],
        compiler_params=PARAMS,
        name="prepare_next",
    )(away(fresh), away(prior))


def split_planes(mixed, planes):
    for j in range(8):
        planes[j] = mixed[pl.ds(j, 64, stride=8), :]


def relax(place, step, right, packed, recv, planes, columns, mask, store):
    y = place.speed_y(step)
    columns[0] = planes[0] + y * (planes[1] + y * (planes[3] + y * planes[6]))
    columns[1] = planes[2] + y * (planes[5] + y * planes[7])
    columns[2] = planes[4] + y * planes[6]
    columns[3] = planes[7]
    lift = [place.scale_x * face for face in lift_faces(place.sign_x)]
    for low in range(8):
        z = float(SPEED[15 - low])
        even = columns[0] + (z * z) * columns[2]
        odd = z * columns[1] + (z * z * z) * columns[3]
        for v, equilibrium in ((low, even - odd), (15 - low, even + odd)):
            at = step * 16 + v
            edge = recv[pl.ds(at, 8, stride=128), :]
            both = jnp.concatenate([edge, pltpu.roll(edge, HALF, 1)], axis=0)
            both = jnp.where(mask, 0.0, both)
            inflow = jnp.concatenate([lift[p0] * both for p0 in range(4)], axis=0)
            hi, lo = split(right[at] + equilibrium + inflow)
            block = packed[at]
            fresh = jnp.dot(
                jnp.concatenate([block, block], axis=1),
                jnp.concatenate([hi, hi, lo, lo], axis=0),
                preferred_element_type=F32,
            )
            store(v, fresh)


def middle_kernel(
    slabs, right_away, packed, recv, mixed, fresh_away, moments_away, planes, columns, sums,
    right, fresh, moments, arrived, sent, sent_moments,
):
    place = Place(slabs)
    mask = outgoing_mask(lane_index((16, 128)), place.sign_x)
    fetch, wait = stream([(lambda i: velocity_block(right_away, i), lambda i: velocity_block(right, i), arrived)])
    put, finish = stream([(lambda i: velocity_block(fresh, i), lambda i: velocity_block(fresh_away, i), sent)])
    start_all(fetch)
    split_planes(mixed, planes)
    sums[...] = jnp.zeros_like(sums)

    def loop(step, carry):
        def store(v, column):
            fresh[step * 16 + v] = column

        wait(step)
        relax(place, step, right, packed, recv, planes, columns, mask, store)
        put(step)
        y = place.speed_y(step)
        weight = jnp.exp(jnp.full((64, 128), -0.5, F32) * (y * y)) * (1.0 / TOTAL)
        s = [None] * 4
        for low in range(8):
            z, w = float(SPEED[15 - low]), float(WEIGHT[low])
            minus, plus = fresh[step * 16 + low], fresh[step * 16 + 15 - low]
            terms = [w * (plus + minus), (w * z) * (plus - minus)]
            for k in range(4):
                term = terms[k % 2] if k < 2 else (z * z) * terms[k % 2]
                s[k] = term if s[k] is None else s[k] + term
        s = [weight * part for part in s]
        y2 = y * y
        totals = [s[0], y * s[0], s[1], y2 * s[0], s[2], y * s[1], y * (y2 * s[0] + s[2]), s[3] + y2 * s[1]]
        for j in range(8):
            sums[j] = sums[j] + totals[j]
        return carry

    lax.fori_loop(0, 8, loop, 0)
    for j in range(8):
        moments[pl.ds(j, 64, stride=8), :] = sums[j]
    copy = pltpu.make_async_copy(moments, moments_away, sent_moments)
    copy.start()
    for step in range(8):
        finish(step)
    copy.wait()


def middle(slabs, right, packed, recv, mixed):
    fresh, moments = pl.pallas_call(
        functools.partial(middle_kernel, slabs),
        in_specs=[HBM, VMEM, VMEM, VMEM],
        out_specs=[HBM, HBM],
        out_shape=[pltpu.HBM((128, 64, 128), F32), pltpu.HBM((512, 128), F32)],
        scratch_shapes=[
            pltpu.VMEM((8, 64, 128), F32),
            pltpu.VMEM((4, 64, 128), F32),
            pltpu.VMEM((8, 64, 128), F32),
            BLOCKS_V,
            BLOCKS_V,
            pltpu.VMEM((512, 128), F32),
            SEMS,
            SEMS,
            pltpu.SemaphoreType.DMA,
        ],
        compiler_params=PARAMS,
        name="middle",
    )(away(right), here(packed), here(recv), here(mixed))
    return fresh, moments.reshape(VEL, 16, 128)


def last_kernel(slabs, right_away, packed, recv, mixed, out, planes, columns, right, blocks, arrived, sent):
    place = Place(slabs)
    mask = outgoing_mask(lane_index((16, 128)), place.sign_x)
    fetch, wait = stream([(lambda i: velocity_block(right_away, i), lambda i: velocity_block(right, i), arrived)])
    put, finish = stream([(lambda i: blocks.at[i], lambda i: mode_block(out, i), sent)])
    start_all(fetch)
    split_planes(mixed, planes)

    def loop(step, carry):
        flat = blocks.at[step].reshape(1024, 128)

        def store(v, fresh):
            flat[pl.ds(v, 64, stride=16), :] = fresh

        wait(step)
        relax(place, step, right, packed, recv, planes, columns, mask, store)
        put(step)
        return carry

    lax.fori_loop(0, 8, loop, 0)
    for step in range(8):
        finish(step)


def last(slabs, right, packed, recv, mixed):
    return pl.pallas_call(
        functools.partial(last_kernel, slabs),
        in_specs=[HBM, VMEM, VMEM, VMEM],
        out_specs=HBM,
        out_shape=pltpu.HBM((64, 128, 128), F32),
        scratch_shapes=[
            pltpu.VMEM((8, 64, 128), F32),
            pltpu.VMEM((4, 64, 128), F32),
            BLOCKS_V,
            BLOCKS_Q,
            SEMS,
            SEMS,
        ],
        compiler_params=PARAMS,
        name="last",
    )(away(right), here(packed), here(recv), here(mixed))


def halo_pairs(slabs):
    pairs = []
    for slab in range(slabs):
        for vel in range(VEL):
            other = slab + 1 if vel >= VEL // 2 else slab - 1
            if 0 <= other < slabs:
                pairs.append((slab * VEL + vel, other * VEL + vel))
    return pairs


def body(slabs, prior, block_inverse):
    mix = jnp.asarray(MIX)
    axes = ("sp", "vel")
    pairs = halo_pairs(slabs)
    cells = prior.reshape(64, 128, 128)
    moments = first_moments(cells)
    mixed, (right, send) = sum_over_velocities(mix, moments, prepare(slabs, cells))
    recv = lax.ppermute(send, axes, pairs).reshape(1024, 128)
    packed = pack(block_inverse)
    fresh, moments = middle(slabs, right, packed, recv, mixed)
    mixed, (right, send) = sum_over_velocities(mix, moments, prepare_next(slabs, fresh, cells))
    recv = lax.ppermute(send, axes, pairs).reshape(1024, 128)
    return last(slabs, right, packed, recv, mixed).reshape(prior.shape)


def solution(mesh):
    spec = P(None, None, None, "vel", "sp")
    return jax.shard_map(
        functools.partial(body, mesh.shape["sp"]),
        mesh=mesh,
        in_specs=(spec, P("vel", None, None)),
        out_specs=spec,
        check_vma=False,
    )
```

```python
import functools

import jax
import jax.numpy as jnp
import numpy as np
from jax import lax
from jax.experimental import pallas as pl
from jax.experimental.pallas import tpu as pltpu
from jax.sharding import PartitionSpec as P

NV1 = 16
COUPLING = 0.25
LID_SPEED = 0.6
STEP = 6.0 / NV1
CENTRE = 0.5 * (NV1 - 1)
VEL = 32
LOCAL_Y = 8
HIGH = [float(np.sqrt(k + 0.5)) for k in range(4)]
HIGHEST = lax.Precision.HIGHEST
F32 = jnp.float32
BF16 = jnp.bfloat16
HALF = 64


def ring_hops(vel):
    y, z = vel // 4 % 4, vel % 4
    return vel // 16 + min(y, 4 - y) + min(z, 4 - z)


ORDER = sorted(range(VEL), key=lambda vel: -ring_hops(vel))


def grid_speed(index):
    return (np.asarray(index, np.float64) - CENTRE) * STEP


def local_polynomials(y, z):
    r2 = y * y + z * z
    return [np.ones_like(r2), y, z, y * y, z * z, y * z, r2 * y, r2 * z]


def combination(x):
    c = np.zeros((13, 8))
    c[0, 0] = 1.0
    c[1, 0] = x
    c[2, 1] = 1.0
    c[3, 2] = 1.0
    c[4, 0] = x * x - 1.0
    c[5, 3], c[5, 0] = 1.0, -1.0
    c[6, 4], c[6, 0] = 1.0, -1.0
    c[7, 1] = x
    c[8, 2] = x
    c[9, 5] = 1.0
    c[10, 0], c[10, 3], c[10, 4] = x * (x * x - 5.0), x, x
    c[11, 1], c[11, 6] = x * x - 5.0, 1.0
    c[12, 2], c[12, 7] = x * x - 5.0, 1.0
    return c


def tables():
    speed = grid_speed(np.arange(NV1))
    weight = np.exp(-0.5 * speed * speed)
    total = weight.sum()
    weight = weight / total
    x, y, z = np.meshgrid(speed, speed, speed, indexing="ij")
    w = weight[:, None, None] * weight[None, :, None] * weight[None, None, :]
    g = np.stack(local_polynomials(y, z))
    per_x = np.stack([combination(s) for s in speed])
    h = np.einsum("xkj,jxyz->kxyz", per_x, g)
    norm = (w * h * h).sum(axis=(1, 2, 3))
    source = np.repeat(per_x * weight[:, None, None], 2, axis=0)
    target = np.repeat(per_x, 2, axis=0)
    mix = np.einsum("tkj,k,ski->tjsi", target, 1.0 / norm, source).reshape(VEL * 8, VEL * 8)
    mix = mix.reshape(VEL, 8, VEL, 8)[ORDER][:, :, ORDER].reshape(VEL * 8, VEL * 8)
    return mix.astype(np.float32), speed, weight, float(total)


MIX, SPEED, WEIGHT, TOTAL = tables()


def split(a):
    hi = a.astype(BF16)
    return hi, (a - hi.astype(F32)).astype(BF16)


def lane_index(shape):
    return lax.broadcasted_iota(jnp.int32, shape, len(shape) - 1)


def row_index(shape):
    return lax.broadcasted_iota(jnp.int32, shape, len(shape) - 2)


class Place:
    def __init__(self, slabs):
        vel, slab = lax.axis_index("vel"), lax.axis_index("sp")
        self.vx = (vel // 2).astype(F32) * STEP - CENTRE * STEP
        self.sign_x = jnp.where(vel >= VEL // 2, 1.0, -1.0)
        self.scale_x = COUPLING * jnp.abs(self.vx)
        self.first_y = vel % 2 * LOCAL_Y
        self.sign_y = jnp.where(vel % 2 == 1, 1.0, -1.0)
        boundary = jnp.where(vel >= VEL // 2, 0, slabs - 1)
        self.wall_x = jnp.where(slab == boundary, 2.0, 0.0)

    def speed_y(self, step):
        return (self.first_y + step).astype(F32) * STEP - CENTRE * STEP


def outgoing_mask(lane, sign):
    return jnp.where(sign > 0, lane, 2 * HALF - 1 - lane) >= HALF


def trace_face(sign):
    return [HIGH[k] if k % 2 == 0 else HIGH[k] * sign for k in range(4)]


def lift_faces(sign):
    return [HIGH[k] if k % 2 == 0 else -HIGH[k] * sign for k in range(4)]


def kept(*shape, dtype=F32):
    return pltpu.VMEM(shape, dtype)


def here(x):
    return pltpu.with_memory_space_constraint(x, pltpu.VMEM)


def away(x):
    return pltpu.with_memory_space_constraint(x, pltpu.HBM)


def velocity_block(ref, step):
    return ref.at[pl.ds(pl.multiple_of(step * 16, 16), 16)]


def mode_block(ref, step):
    return ref.at[:, pl.ds(pl.multiple_of(step * 16, 16), 16), :]


def stream(pairs):
    def copies(step):
        return [pltpu.make_async_copy(source(step), target(step), sems.at[step]) for source, target, sems in pairs]

    def start(step):
        for copy in copies(step):
            copy.start()

    def wait(step):
        for copy in copies(step):
            copy.wait()

    return start, wait


def start_all(start):
    for step in range(8):
        start(step)


BLOCKS_V = pltpu.VMEM((128, 64, 128), F32)
BLOCKS_Q = pltpu.VMEM((8, 64, 16, 128), F32)
SEMS = pltpu.SemaphoreType.DMA((8,))


VMEM = pl.BlockSpec(memory_space=pltpu.VMEM)
HBM = pl.BlockSpec(memory_space=pltpu.HBM)
PARAMS = pltpu.CompilerParams(vmem_limit_bytes=24 * 2**20)


def moment_weights(first_y):
    lane, row = lane_index((8, 128)), row_index((8, 128))
    y = (lane // 16 + first_y).astype(F32) * STEP - CENTRE * STEP
    z = (lane % 16).astype(F32) * STEP - CENTRE * STEP
    r2 = y * y + z * z
    polynomial = jnp.ones((8, 128), F32)
    for j, g in enumerate([y, z, y * y, z * z, y * z, r2 * y, r2 * z]):
        polynomial = jnp.where(row == j + 1, g, polynomial)
    hi, lo = split(polynomial * jnp.exp(-0.5 * r2) * (1.0 / (TOTAL * TOTAL)))
    half = jnp.concatenate([hi.astype(F32), lo.astype(F32)], axis=0).astype(BF16)
    return jnp.concatenate([half, half], axis=1)


def first_moments_kernel(prior, moments, cells, sums, arrived, sent):
    def part(ref, step):
        return ref.at[pl.ds(step * 8, 8)]

    fetch, wait = stream([(lambda i: part(prior, i), lambda i: part(cells, i), arrived)])
    put, finish = stream([(lambda i: part(sums, i), lambda i: part(moments, i), sent)])
    start_all(fetch)
    weights = moment_weights(lax.axis_index("vel") % 2 * LOCAL_Y)
    for step in range(8):
        wait(step)
        for q in range(step * 8, step * 8 + 8):
            hi, lo = split(cells[q])
            product = jnp.dot(weights, jnp.concatenate([hi, lo], axis=0), preferred_element_type=F32)
            sums[q] = product[:8] + product[8:]
        put(step)
    for step in range(8):
        finish(step)


def first_moments(prior):
    return pl.pallas_call(
        first_moments_kernel,
        in_specs=[HBM],
        out_specs=HBM,
        out_shape=pltpu.HBM((64, 8, 128), F32),
        scratch_shapes=[pltpu.VMEM((64, 128, 128), F32), pltpu.VMEM((64, 8, 128), F32), SEMS, SEMS],
        compiler_params=PARAMS,
        name="first_moments",
    )(away(prior)).reshape(VEL, 16, 128)


def pack_kernel(inverse, packed, rows, blocks, arrived):
    fetch, wait = stream([(lambda i: inverse.at[pl.ds(i * 8, 8)], lambda i: blocks.at[pl.ds(i * 8, 8)], arrived)])
    for step in range(8):
        fetch(step)
    for step in range(8):
        wait(step)
        for p in range(step * 8, step * 8 + 8):
            hi, lo = split(blocks[p])
            both = jnp.concatenate([hi.astype(F32), lo.astype(F32)], axis=0)
            rows[pl.ds(p, 128, stride=PITCH), :] = both.T

    def step(v, carry):
        packed[v] = rows[pl.ds(pl.multiple_of(v * PITCH, 8), 64), :].astype(BF16)
        return carry

    lax.fori_loop(0, 128, step, 0, unroll=8)


PITCH = 72


def pack(inverse):
    return pl.pallas_call(
        pack_kernel,
        in_specs=[HBM],
        out_specs=VMEM,
        out_shape=kept(128, 64, 128, dtype=BF16),
        scratch_shapes=[pltpu.VMEM((128 * PITCH, 128), F32), pltpu.VMEM((64, 64, 128), F32), SEMS],
        compiler_params=PARAMS,
        name="pack",
    )(away(jnp.transpose(inverse, (1, 2, 0))))


def mix_kernel(mix, gathered, mixed):
    part = jnp.concatenate([gathered[:, low * 8 : low * 8 + 8, :].reshape(VEL * 8, 128) for low in range(2)], axis=1)
    result = jnp.dot(mix[...], part, preferred_element_type=F32, precision=HIGHEST)
    for low in range(2):
        mixed[:, low * 8 : low * 8 + 8, :] = result[:, low * 128 : low * 128 + 128].reshape(VEL, 8, 128)


def mix_moments(mix, gathered):
    return pl.pallas_call(
        mix_kernel,
        in_specs=[VMEM, VMEM],
        out_specs=VMEM,
        out_shape=kept(VEL, 16, 128),
        compiler_params=PARAMS,
        name="mix_moments",
    )(here(mix), here(gathered))


def sum_over_velocities(mix, partial_sums, beside):
    gathered = lax.all_to_all(partial_sums, "vel", 0, 0, axis_index_groups=[ORDER])
    gathered, beside = lax.optimization_barrier((gathered, beside))
    mixed = mix_moments(mix, gathered)
    mixed, beside = lax.optimization_barrier((mixed, beside))
    return lax.all_to_all(mixed, "vel", 0, 0, axis_index_groups=[ORDER]).reshape(512, 128), beside


def add_inflow(source, base, target, send, place, step, mask):
    y = place.speed_y(step)
    lane, row = lane_index((8, 128)), row_index((8, 128))
    trace_x, lift_x = trace_face(place.sign_x), lift_faces(place.sign_x)
    trace_y, lift_y = trace_face(place.sign_y), lift_faces(place.sign_y)
    up_y = place.sign_y > 0
    shift_y = jnp.where(up_y, 8, 120)
    cell_y = jnp.where(up_y, lane // 8 % 8, 7 - lane // 8 % 8)
    scale_y = jnp.where(cell_y > 0, COUPLING * jnp.abs(y), 0.0)
    wall_y = jnp.where(cell_y > 0, 0.0, 2.0 * COUPLING * jnp.abs(y))
    scale_x = jnp.where(mask, place.scale_x, 0.0)
    wall_x = jnp.where(mask, 0.0, place.wall_x * place.scale_x)
    lid = 2.0 * jnp.exp(jnp.full((8, 128), LID_SPEED, F32) * place.vx - 0.5 * LID_SPEED * LID_SPEED)
    for part in range(2):
        up = part == 1
        speed = jnp.abs((row + (part * 8)).astype(F32) - CENTRE) * (STEP * COUPLING)
        inside = (lane % 8 > 0) if up else (lane % 8 < 7)
        scale_z = jnp.where(inside, speed, 0.0)
        wall_z = jnp.where(inside, 0.0, speed * (2.0 if up else lid))
        trace_z, lift_z = trace_face(1.0 if up else -1.0), lift_faces(1.0 if up else -1.0)
        face_x = [None] * 16
        for low in range(8):
            pair = []
            for r in (low, low + 8):
                trace = sum(trace_x[p0] * source(part, p0 * 16 + r) for p0 in range(4))
                turned = pltpu.roll(trace, HALF, 1)
                pair.append((trace, turned))
                face_x[r] = turned * scale_x
            if send is not None:
                send[part * 64 + low * 8 : part * 64 + low * 8 + 8, :] = jnp.where(mask, pair[1][0], pair[0][1])
        face_x[0] = face_x[0] + wall_x
        for p0 in range(4):
            x = [[source(part, p0 * 16 + p1 * 4 + p2) for p2 in range(4)] for p1 in range(4)]
            face_y, face_z = [], []
            for k in range(4):
                ty = sum(trace_y[p1] * x[p1][k] for p1 in range(4))
                ty = pltpu.roll(ty, shift_y, 1) * scale_y
                tz = sum(trace_z[p2] * x[k][p2] for p2 in range(4))
                tz = pltpu.roll(tz, 1 if up else 127, 1) * scale_z
                if p0 == 0 and k == 0:
                    ty = ty + wall_y
                    tz = tz + wall_z
                face_y.append(ty)
                face_z.append(tz)
            for p1 in range(4):
                for p2 in range(4):
                    q, r = p0 * 16 + p1 * 4 + p2, p1 * 4 + p2
                    value = base(part, q) + lift_x[p0] * face_x[r] + lift_y[p1] * face_y[p2] + lift_z[p2] * face_z[p1]
                    target[part * 512 + q * 8 : part * 512 + q * 8 + 8, :] = value


def velocity_rows(v):
    return pl.ds(v // 8 * 512 + v % 8, 64, stride=8)


def block_reader(ref):
    def read(part, q):
        return ref[q, part * 8 : part * 8 + 8, :]

    return read


def row_reader(ref):
    def read(part, q):
        return ref[part * 512 + q * 8 : part * 512 + q * 8 + 8, :]

    return read


def prepare_kernel(slabs, prior, right, send, scratch, outgoing, cells, made, arrived, sent):
    place = Place(slabs)
    mask = outgoing_mask(lane_index((8, 128)), place.sign_x)
    fetch, wait = stream([(lambda i: mode_block(prior, i), lambda i: cells.at[i], arrived)])
    put, finish = stream([(lambda i: velocity_block(made, i), lambda i: velocity_block(right, i), sent)])
    start_all(fetch)

    def loop(step, carry):
        wait(step)
        read = block_reader(cells.at[step])
        add_inflow(read, read, scratch, outgoing, place, step, mask)
        for v in range(16):
            made[step * 16 + v] = scratch[velocity_rows(v), :]
            send[step * 16 + v] = outgoing[pl.ds(v // 8 * 64 + v % 8, 8, stride=8), :]
        put(step)
        return carry

    lax.fori_loop(0, 8, loop, 0)
    for step in range(8):
        finish(step)


def prepare(slabs, prior):
    return pl.pallas_call(
        functools.partial(prepare_kernel, slabs),
        in_specs=[HBM],
        out_specs=[HBM, VMEM],
        out_shape=[pltpu.HBM((128, 64, 128), F32), kept(128, 8, 128)],
        scratch_shapes=[pltpu.VMEM((1024, 128), F32), pltpu.VMEM((128, 128), F32), BLOCKS_Q, BLOCKS_V, SEMS, SEMS],
        compiler_params=PARAMS,
        name="prepare",
    )(away(prior))


def prepare_next_kernel(
    slabs, fresh, prior, right, rows, scratch, columns, cells, made, arrived, arrived_prior, sent
):
    place = Place(slabs)
    mask = outgoing_mask(lane_index((8, 128)), place.sign_x)
    fetch, wait = stream(
        [
            (lambda i: velocity_block(fresh, i), lambda i: velocity_block(columns, i), arrived),
            (lambda i: mode_block(prior, i), lambda i: cells.at[i], arrived_prior),
        ]
    )
    put, finish = stream([(lambda i: velocity_block(made, i), lambda i: velocity_block(right, i), sent)])
    start_all(fetch)

    def loop(step, carry):
        wait(step)
        for v in range(16):
            rows[velocity_rows(v), :] = columns[step * 16 + v]
        add_inflow(row_reader(rows), block_reader(cells.at[step]), scratch, None, place, step, mask)
        for v in range(16):
            made[step * 16 + v] = scratch[velocity_rows(v), :]
        put(step)
        return carry

    lax.fori_loop(0, 8, loop, 0)
    for step in range(8):
        finish(step)


def prepare_next(slabs, fresh, prior):
    return pl.pallas_call(
        functools.partial(prepare_next_kernel, slabs),
        in_specs=[HBM, HBM],
        out_specs=HBM,
        out_shape=pltpu.HBM((128, 64, 128), F32),
        scratch_shapes=[
            pltpu.VMEM((1024, 128), F32),
            pltpu.VMEM((1024, 128), F32),
            BLOCKS_V,
            BLOCKS_Q,
            BLOCKS_V,
            SEMS,
            SEMS,
            SEMS,
        ],
        compiler_params=PARAMS,
        name="prepare_next",
    )(away(fresh), away(prior))


def split_planes(mixed, planes):
    for j in range(8):
        planes[j] = mixed[pl.ds(j, 64, stride=8), :]


def relax(place, step, right, packed, recv, planes, columns, mask, store):
    y = place.speed_y(step)
    columns[0] = planes[0] + y * (planes[1] + y * (planes[3] + y * planes[6]))
    columns[1] = planes[2] + y * (planes[5] + y * planes[7])
    columns[2] = planes[4] + y * planes[6]
    columns[3] = planes[7]
    lift = [place.scale_x * face for face in lift_faces(place.sign_x)]
    for low in range(8):
        z = float(SPEED[15 - low])
        even = columns[0] + (z * z) * columns[2]
        odd = z * columns[1] + (z * z * z) * columns[3]
        for v, equilibrium in ((low, even - odd), (15 - low, even + odd)):
            at = step * 16 + v
            edge = recv[at]
            both = jnp.concatenate([edge, pltpu.roll(edge, HALF, 1)], axis=0)
            both = jnp.where(mask, 0.0, both)
            inflow = jnp.concatenate([lift[p0] * both for p0 in range(4)], axis=0)
            hi, lo = split(right[at] + equilibrium + inflow)
            block = packed[at]
            fresh = jnp.dot(
                jnp.concatenate([block, block], axis=1),
                jnp.concatenate([hi, hi, lo, lo], axis=0),
                preferred_element_type=F32,
            )
            store(v, fresh)


def middle_kernel(
    slabs, right_away, packed, recv, mixed, fresh_away, moments_away, send_away, planes, columns, sums,
    right, fresh, moments, send, arrived, sent, sent_moments, sent_send,
):
    place = Place(slabs)
    mask = outgoing_mask(lane_index((16, 128)), place.sign_x)
    face = trace_face(place.sign_x)
    fetch, wait = stream([(lambda i: velocity_block(right_away, i), lambda i: velocity_block(right, i), arrived)])
    put, finish = stream(
        [
            (lambda i: velocity_block(fresh, i), lambda i: velocity_block(fresh_away, i), sent),
            (lambda i: velocity_block(send, i), lambda i: velocity_block(send_away, i), sent_send),
        ]
    )
    start_all(fetch)
    split_planes(mixed, planes)
    sums[...] = jnp.zeros_like(sums)

    def loop(step, carry):
        def store(v, column):
            fresh[step * 16 + v] = column
            trace = sum(face[p0] * column[p0 * 16 : p0 * 16 + 16] for p0 in range(4))
            outgoing = jnp.where(mask[:8], trace[8:], pltpu.roll(trace[:8], HALF, 1))
            send[step * 16 + v] = outgoing

        wait(step)
        relax(place, step, right, packed, recv, planes, columns, mask, store)
        put(step)
        y = place.speed_y(step)
        weight = jnp.exp(jnp.full((64, 128), -0.5, F32) * (y * y)) * (1.0 / TOTAL)
        s = [None] * 4
        for low in range(8):
            z, w = float(SPEED[15 - low]), float(WEIGHT[low])
            minus, plus = fresh[step * 16 + low], fresh[step * 16 + 15 - low]
            terms = [w * (plus + minus), (w * z) * (plus - minus)]
            for k in range(4):
                term = terms[k % 2] if k < 2 else (z * z) * terms[k % 2]
                s[k] = term if s[k] is None else s[k] + term
        s = [weight * part for part in s]
        y2 = y * y
        totals = [s[0], y * s[0], s[1], y2 * s[0], s[2], y * s[1], y * (y2 * s[0] + s[2]), s[3] + y2 * s[1]]
        for j in range(8):
            sums[j] = sums[j] + totals[j]
        return carry

    lax.fori_loop(0, 8, loop, 0)
    for j in range(8):
        moments[pl.ds(j, 64, stride=8), :] = sums[j]
    copy = pltpu.make_async_copy(moments, moments_away, sent_moments)
    copy.start()
    for step in range(8):
        finish(step)
    copy.wait()


def middle(slabs, right, packed, recv, mixed):
    fresh, moments, send = pl.pallas_call(
        functools.partial(middle_kernel, slabs),
        in_specs=[HBM, VMEM, VMEM, VMEM],
        out_specs=[HBM] * 3,
        out_shape=[pltpu.HBM((128, 64, 128), F32), pltpu.HBM((512, 128), F32), pltpu.HBM((128, 8, 128), F32)],
        scratch_shapes=[
            pltpu.VMEM((8, 64, 128), F32),
            pltpu.VMEM((4, 64, 128), F32),
            pltpu.VMEM((8, 64, 128), F32),
            BLOCKS_V,
            BLOCKS_V,
            pltpu.VMEM((512, 128), F32),
            pltpu.VMEM((128, 8, 128), F32),
            SEMS,
            SEMS,
            pltpu.SemaphoreType.DMA,
            SEMS,
        ],
        compiler_params=PARAMS,
        name="middle",
    )(away(right), here(packed), here(recv), here(mixed))
    return fresh, moments.reshape(VEL, 16, 128), send


def last_kernel(slabs, right_away, packed, recv, mixed, out, planes, columns, right, blocks, arrived, sent):
    place = Place(slabs)
    mask = outgoing_mask(lane_index((16, 128)), place.sign_x)
    fetch, wait = stream([(lambda i: velocity_block(right_away, i), lambda i: velocity_block(right, i), arrived)])
    put, finish = stream([(lambda i: blocks.at[i], lambda i: mode_block(out, i), sent)])
    start_all(fetch)
    split_planes(mixed, planes)

    def loop(step, carry):
        flat = blocks.at[step].reshape(1024, 128)

        def store(v, fresh):
            flat[pl.ds(v, 64, stride=16), :] = fresh

        wait(step)
        relax(place, step, right, packed, recv, planes, columns, mask, store)
        put(step)
        return carry

    lax.fori_loop(0, 8, loop, 0)
    for step in range(8):
        finish(step)


def last(slabs, right, packed, recv, mixed):
    return pl.pallas_call(
        functools.partial(last_kernel, slabs),
        in_specs=[HBM, VMEM, VMEM, VMEM],
        out_specs=HBM,
        out_shape=pltpu.HBM((64, 128, 128), F32),
        scratch_shapes=[
            pltpu.VMEM((8, 64, 128), F32),
            pltpu.VMEM((4, 64, 128), F32),
            BLOCKS_V,
            BLOCKS_Q,
            SEMS,
            SEMS,
        ],
        compiler_params=PARAMS,
        name="last",
    )(away(right), here(packed), here(recv), here(mixed))


def halo_pairs(slabs):
    pairs = []
    for slab in range(slabs):
        for vel in range(VEL):
            other = slab + 1 if vel >= VEL // 2 else slab - 1
            if 0 <= other < slabs:
                pairs.append((slab * VEL + vel, other * VEL + vel))
    return pairs


def body(slabs, prior, block_inverse):
    mix = jnp.asarray(MIX)
    axes = ("sp", "vel")
    pairs = halo_pairs(slabs)
    cells = prior.reshape(64, 128, 128)
    moments = first_moments(cells)
    mixed, (right, send) = sum_over_velocities(mix, moments, prepare(slabs, cells))
    recv = lax.ppermute(send, axes, pairs)
    packed = pack(block_inverse)
    fresh, moments, send = middle(slabs, right, packed, recv, mixed)
    recv = lax.ppermute(send, axes, pairs)
    mixed, right = sum_over_velocities(mix, moments, prepare_next(slabs, fresh, cells))
    return last(slabs, right, packed, recv, mixed).reshape(prior.shape)


def solution(mesh):
    spec = P(None, None, None, "vel", "sp")
    return jax.shard_map(
        functools.partial(body, mesh.shape["sp"]),
        mesh=mesh,
        in_specs=(spec, P("vel", None, None)),
        out_specs=spec,
        check_vma=False,
    )
```

```python
import functools

import jax
import jax.numpy as jnp
import numpy as np
from jax import lax
from jax.experimental import pallas as pl
from jax.experimental.pallas import tpu as pltpu
from jax.sharding import PartitionSpec as P

NV1 = 16
COUPLING = 0.25
LID_SPEED = 0.6
STEP = 6.0 / NV1
CENTRE = 0.5 * (NV1 - 1)
VEL = 32
LOCAL_Y = 8
HIGH = [float(np.sqrt(k + 0.5)) for k in range(4)]
HIGHEST = lax.Precision.HIGHEST
F32 = jnp.float32
BF16 = jnp.bfloat16
HALF = 64


def ring_hops(vel):
    along_y, along_z = min(vel // 4 % 4, 4 - vel // 4 % 4), min(vel % 4, 4 - vel % 4)
    return vel // 16, along_y + along_z, vel


ORDER = sorted(range(VEL), key=ring_hops, reverse=True)


def grid_speed(index):
    return (np.asarray(index, np.float64) - CENTRE) * STEP


def local_polynomials(y, z):
    r2 = y * y + z * z
    return [np.ones_like(r2), y, z, y * y, z * z, y * z, r2 * y, r2 * z]


def combination(x):
    c = np.zeros((13, 8))
    c[0, 0] = 1.0
    c[1, 0] = x
    c[2, 1] = 1.0
    c[3, 2] = 1.0
    c[4, 0] = x * x - 1.0
    c[5, 3], c[5, 0] = 1.0, -1.0
    c[6, 4], c[6, 0] = 1.0, -1.0
    c[7, 1] = x
    c[8, 2] = x
    c[9, 5] = 1.0
    c[10, 0], c[10, 3], c[10, 4] = x * (x * x - 5.0), x, x
    c[11, 1], c[11, 6] = x * x - 5.0, 1.0
    c[12, 2], c[12, 7] = x * x - 5.0, 1.0
    return c


def tables():
    speed = grid_speed(np.arange(NV1))
    weight = np.exp(-0.5 * speed * speed)
    total = weight.sum()
    weight = weight / total
    x, y, z = np.meshgrid(speed, speed, speed, indexing="ij")
    w = weight[:, None, None] * weight[None, :, None] * weight[None, None, :]
    g = np.stack(local_polynomials(y, z))
    per_x = np.stack([combination(s) for s in speed])
    h = np.einsum("xkj,jxyz->kxyz", per_x, g)
    norm = (w * h * h).sum(axis=(1, 2, 3))
    source = np.repeat(per_x * weight[:, None, None], 2, axis=0)
    target = np.repeat(per_x, 2, axis=0)
    mix = np.einsum("tkj,k,ski->tjsi", target, 1.0 / norm, source).reshape(VEL * 8, VEL * 8)
    mix = mix.reshape(VEL, 8, VEL, 8)[ORDER][:, :, ORDER].reshape(VEL * 8, VEL * 8)
    return mix.astype(np.float32), speed, weight, float(total)


MIX, SPEED, WEIGHT, TOTAL = tables()


def split(a):
    hi = a.astype(BF16)
    return hi, (a - hi.astype(F32)).astype(BF16)


def lane_index(shape):
    return lax.broadcasted_iota(jnp.int32, shape, len(shape) - 1)


def row_index(shape):
    return lax.broadcasted_iota(jnp.int32, shape, len(shape) - 2)


class Place:
    def __init__(self, slabs):
        vel, slab = lax.axis_index("vel"), lax.axis_index("sp")
        self.vx = (vel // 2).astype(F32) * STEP - CENTRE * STEP
        self.sign_x = jnp.where(vel >= VEL // 2, 1.0, -1.0)
        self.scale_x = COUPLING * jnp.abs(self.vx)
        self.first_y = vel % 2 * LOCAL_Y
        self.sign_y = jnp.where(vel % 2 == 1, 1.0, -1.0)
        boundary = jnp.where(vel >= VEL // 2, 0, slabs - 1)
        self.wall_x = jnp.where(slab == boundary, 2.0, 0.0)

    def speed_y(self, step):
        return (self.first_y + step).astype(F32) * STEP - CENTRE * STEP


def outgoing_mask(lane, sign):
    return jnp.where(sign > 0, lane, 2 * HALF - 1 - lane) >= HALF


def trace_face(sign):
    return [HIGH[k] if k % 2 == 0 else HIGH[k] * sign for k in range(4)]


def lift_faces(sign):
    return [HIGH[k] if k % 2 == 0 else -HIGH[k] * sign for k in range(4)]


def kept(*shape, dtype=F32):
    return pltpu.VMEM(shape, dtype)


def here(x):
    return pltpu.with_memory_space_constraint(x, pltpu.VMEM)


def away(x):
    return pltpu.with_memory_space_constraint(x, pltpu.HBM)


def velocity_block(ref, step):
    return ref.at[pl.ds(pl.multiple_of(step * 16, 16), 16)]


def mode_block(ref, step):
    return ref.at[:, pl.ds(pl.multiple_of(step * 16, 16), 16), :]


def stream(pairs):
    def copies(step):
        return [pltpu.make_async_copy(source(step), target(step), sems.at[step]) for source, target, sems in pairs]

    def start(step):
        for copy in copies(step):
            copy.start()

    def wait(step):
        for copy in copies(step):
            copy.wait()

    return start, wait


def start_all(start):
    for step in range(8):
        start(step)


BLOCKS_V = pltpu.VMEM((128, 64, 128), F32)
BLOCKS_Q = pltpu.VMEM((8, 64, 16, 128), F32)
SEMS = pltpu.SemaphoreType.DMA((8,))


VMEM = pl.BlockSpec(memory_space=pltpu.VMEM)
HBM = pl.BlockSpec(memory_space=pltpu.HBM)
PARAMS = pltpu.CompilerParams(vmem_limit_bytes=24 * 2**20)


def moment_weights(first_y):
    lane, row = lane_index((8, 128)), row_index((8, 128))
    y = (lane // 16 + first_y).astype(F32) * STEP - CENTRE * STEP
    z = (lane % 16).astype(F32) * STEP - CENTRE * STEP
    r2 = y * y + z * z
    polynomial = jnp.ones((8, 128), F32)
    for j, g in enumerate([y, z, y * y, z * z, y * z, r2 * y, r2 * z]):
        polynomial = jnp.where(row == j + 1, g, polynomial)
    hi, lo = split(polynomial * jnp.exp(-0.5 * r2) * (1.0 / (TOTAL * TOTAL)))
    half = jnp.concatenate([hi.astype(F32), lo.astype(F32)], axis=0).astype(BF16)
    return jnp.concatenate([half, half], axis=1)


def first_moments_kernel(prior, moments, cells, sums, arrived, sent):
    def part(ref, step):
        return ref.at[pl.ds(step * 8, 8)]

    fetch, wait = stream([(lambda i: part(prior, i), lambda i: part(cells, i), arrived)])
    put, finish = stream([(lambda i: part(sums, i), lambda i: part(moments, i), sent)])
    start_all(fetch)
    weights = moment_weights(lax.axis_index("vel") % 2 * LOCAL_Y)
    for step in range(8):
        wait(step)
        for q in range(step * 8, step * 8 + 8):
            hi, lo = split(cells[q])
            product = jnp.dot(weights, jnp.concatenate([hi, lo], axis=0), preferred_element_type=F32)
            sums[q] = product[:8] + product[8:]
        put(step)
    for step in range(8):
        finish(step)


def first_moments(prior):
    return pl.pallas_call(
        first_moments_kernel,
        in_specs=[HBM],
        out_specs=HBM,
        out_shape=pltpu.HBM((64, 8, 128), F32),
        scratch_shapes=[pltpu.VMEM((64, 128, 128), F32), pltpu.VMEM((64, 8, 128), F32), SEMS, SEMS],
        compiler_params=PARAMS,
        name="first_moments",
    )(away(prior)).reshape(VEL, 16, 128)


def pack_kernel(inverse, packed, rows, blocks, arrived):
    fetch, wait = stream([(lambda i: inverse.at[pl.ds(i * 8, 8)], lambda i: blocks.at[pl.ds(i * 8, 8)], arrived)])
    for step in range(8):
        fetch(step)
    for step in range(8):
        wait(step)
        for p in range(step * 8, step * 8 + 8):
            hi, lo = split(blocks[p])
            both = jnp.concatenate([hi.astype(F32), lo.astype(F32)], axis=0)
            rows[pl.ds(p, 128, stride=PITCH), :] = both.T

    def step(v, carry):
        packed[v] = rows[pl.ds(pl.multiple_of(v * PITCH, 8), 64), :].astype(BF16)
        return carry

    lax.fori_loop(0, 128, step, 0, unroll=8)


PITCH = 72


def pack(inverse):
    return pl.pallas_call(
        pack_kernel,
        in_specs=[HBM],
        out_specs=VMEM,
        out_shape=kept(128, 64, 128, dtype=BF16),
        scratch_shapes=[pltpu.VMEM((128 * PITCH, 128), F32), pltpu.VMEM((64, 64, 128), F32), SEMS],
        compiler_params=PARAMS,
        name="pack",
    )(away(jnp.transpose(inverse, (1, 2, 0))))


def mix_kernel(mix, gathered, mixed):
    part = jnp.concatenate([gathered[:, low * 8 : low * 8 + 8, :].reshape(VEL * 8, 128) for low in range(2)], axis=1)
    result = jnp.dot(mix[...], part, preferred_element_type=F32, precision=HIGHEST)
    for low in range(2):
        mixed[:, low * 8 : low * 8 + 8, :] = result[:, low * 128 : low * 128 + 128].reshape(VEL, 8, 128)


def mix_moments(mix, gathered):
    return pl.pallas_call(
        mix_kernel,
        in_specs=[VMEM, VMEM],
        out_specs=VMEM,
        out_shape=kept(VEL, 16, 128),
        compiler_params=PARAMS,
        name="mix_moments",
    )(here(mix), here(gathered))


def sum_over_velocities(mix, partial_sums, beside):
    gathered = lax.all_to_all(partial_sums, "vel", 0, 0, axis_index_groups=[ORDER])
    gathered, beside = lax.optimization_barrier((gathered, beside))
    mixed = mix_moments(mix, gathered)
    mixed, beside = lax.optimization_barrier((mixed, beside))
    return lax.all_to_all(mixed, "vel", 0, 0, axis_index_groups=[ORDER]).reshape(512, 128), beside


def add_inflow(source, base, target, send, place, step, mask):
    y = place.speed_y(step)
    lane, row = lane_index((8, 128)), row_index((8, 128))
    trace_x, lift_x = trace_face(place.sign_x), lift_faces(place.sign_x)
    trace_y, lift_y = trace_face(place.sign_y), lift_faces(place.sign_y)
    up_y = place.sign_y > 0
    shift_y = jnp.where(up_y, 8, 120)
    cell_y = jnp.where(up_y, lane // 8 % 8, 7 - lane // 8 % 8)
    scale_y = jnp.where(cell_y > 0, COUPLING * jnp.abs(y), 0.0)
    wall_y = jnp.where(cell_y > 0, 0.0, 2.0 * COUPLING * jnp.abs(y))
    scale_x = jnp.where(mask, place.scale_x, 0.0)
    wall_x = jnp.where(mask, 0.0, place.wall_x * place.scale_x)
    lid = 2.0 * jnp.exp(jnp.full((8, 128), LID_SPEED, F32) * place.vx - 0.5 * LID_SPEED * LID_SPEED)
    for part in range(2):
        up = part == 1
        speed = jnp.abs((row + (part * 8)).astype(F32) - CENTRE) * (STEP * COUPLING)
        inside = (lane % 8 > 0) if up else (lane % 8 < 7)
        scale_z = jnp.where(inside, speed, 0.0)
        wall_z = jnp.where(inside, 0.0, speed * (2.0 if up else lid))
        trace_z, lift_z = trace_face(1.0 if up else -1.0), lift_faces(1.0 if up else -1.0)
        face_x = [None] * 16
        for low in range(8):
            pair = []
            for r in (low, low + 8):
                trace = sum(trace_x[p0] * source(part, p0 * 16 + r) for p0 in range(4))
                turned = pltpu.roll(trace, HALF, 1)
                pair.append((trace, turned))
                face_x[r] = turned * scale_x
            if send is not None:
                send[part * 64 + low * 8 : part * 64 + low * 8 + 8, :] = jnp.where(mask, pair[1][0], pair[0][1])
        face_x[0] = face_x[0] + wall_x
        for p0 in range(4):
            x = [[source(part, p0 * 16 + p1 * 4 + p2) for p2 in range(4)] for p1 in range(4)]
            face_y, face_z = [], []
            for k in range(4):
                ty = sum(trace_y[p1] * x[p1][k] for p1 in range(4))
                ty = pltpu.roll(ty, shift_y, 1) * scale_y
                tz = sum(trace_z[p2] * x[k][p2] for p2 in range(4))
                tz = pltpu.roll(tz, 1 if up else 127, 1) * scale_z
                if p0 == 0 and k == 0:
                    ty = ty + wall_y
                    tz = tz + wall_z
                face_y.append(ty)
                face_z.append(tz)
            for p1 in range(4):
                for p2 in range(4):
                    q, r = p0 * 16 + p1 * 4 + p2, p1 * 4 + p2
                    value = base(part, q) + lift_x[p0] * face_x[r] + lift_y[p1] * face_y[p2] + lift_z[p2] * face_z[p1]
                    target[part * 512 + q * 8 : part * 512 + q * 8 + 8, :] = value


def velocity_rows(v):
    return pl.ds(v // 8 * 512 + v % 8, 64, stride=8)


def block_reader(ref):
    def read(part, q):
        return ref[q, part * 8 : part * 8 + 8, :]

    return read


def row_reader(ref):
    def read(part, q):
        return ref[part * 512 + q * 8 : part * 512 + q * 8 + 8, :]

    return read


def prepare_kernel(slabs, prior, right, send, scratch, outgoing, cells, made, arrived, sent):
    place = Place(slabs)
    mask = outgoing_mask(lane_index((8, 128)), place.sign_x)
    fetch, wait = stream([(lambda i: mode_block(prior, i), lambda i: cells.at[i], arrived)])
    put, finish = stream([(lambda i: velocity_block(made, i), lambda i: velocity_block(right, i), sent)])
    start_all(fetch)

    def loop(step, carry):
        wait(step)
        read = block_reader(cells.at[step])
        add_inflow(read, read, scratch, outgoing, place, step, mask)
        for v in range(16):
            made[step * 16 + v] = scratch[velocity_rows(v), :]
            send[step * 16 + v] = outgoing[pl.ds(v // 8 * 64 + v % 8, 8, stride=8), :]
        put(step)
        return carry

    lax.fori_loop(0, 8, loop, 0)
    for step in range(8):
        finish(step)


def prepare(slabs, prior):
    return pl.pallas_call(
        functools.partial(prepare_kernel, slabs),
        in_specs=[HBM],
        out_specs=[HBM, VMEM],
        out_shape=[pltpu.HBM((128, 64, 128), F32), kept(128, 8, 128)],
        scratch_shapes=[pltpu.VMEM((1024, 128), F32), pltpu.VMEM((128, 128), F32), BLOCKS_Q, BLOCKS_V, SEMS, SEMS],
        compiler_params=PARAMS,
        name="prepare",
    )(away(prior))


def prepare_next_kernel(
    slabs, fresh, prior, right, rows, scratch, columns, cells, made, arrived, arrived_prior, sent
):
    place = Place(slabs)
    mask = outgoing_mask(lane_index((8, 128)), place.sign_x)
    fetch, wait = stream(
        [
            (lambda i: velocity_block(fresh, i), lambda i: velocity_block(columns, i), arrived),
            (lambda i: mode_block(prior, i), lambda i: cells.at[i], arrived_prior),
        ]
    )
    put, finish = stream([(lambda i: velocity_block(made, i), lambda i: velocity_block(right, i), sent)])
    start_all(fetch)

    def loop(step, carry):
        wait(step)
        for v in range(16):
            rows[velocity_rows(v), :] = columns[step * 16 + v]
        add_inflow(row_reader(rows), block_reader(cells.at[step]), scratch, None, place, step, mask)
        for v in range(16):
            made[step * 16 + v] = scratch[velocity_rows(v), :]
        put(step)
        return carry

    lax.fori_loop(0, 8, loop, 0)
    for step in range(8):
        finish(step)


def prepare_next(slabs, fresh, prior):
    return pl.pallas_call(
        functools.partial(prepare_next_kernel, slabs),
        in_specs=[HBM, HBM],
        out_specs=HBM,
        out_shape=pltpu.HBM((128, 64, 128), F32),
        scratch_shapes=[
            pltpu.VMEM((1024, 128), F32),
            pltpu.VMEM((1024, 128), F32),
            BLOCKS_V,
            BLOCKS_Q,
            BLOCKS_V,
            SEMS,
            SEMS,
            SEMS,
        ],
        compiler_params=PARAMS,
        name="prepare_next",
    )(away(fresh), away(prior))


def split_planes(mixed, planes):
    for j in range(8):
        planes[j] = mixed[pl.ds(j, 64, stride=8), :]


def relax(place, step, right, packed, recv, planes, columns, mask, store):
    y = place.speed_y(step)
    columns[0] = planes[0] + y * (planes[1] + y * (planes[3] + y * planes[6]))
    columns[1] = planes[2] + y * (planes[5] + y * planes[7])
    columns[2] = planes[4] + y * planes[6]
    columns[3] = planes[7]
    lift = [place.scale_x * face for face in lift_faces(place.sign_x)]
    for low in range(8):
        z = float(SPEED[15 - low])
        even = columns[0] + (z * z) * columns[2]
        odd = z * columns[1] + (z * z * z) * columns[3]
        for v, equilibrium in ((low, even - odd), (15 - low, even + odd)):
            at = step * 16 + v
            edge = recv[at]
            both = jnp.concatenate([edge, pltpu.roll(edge, HALF, 1)], axis=0)
            both = jnp.where(mask, 0.0, both)
            inflow = jnp.concatenate([lift[p0] * both for p0 in range(4)], axis=0)
            hi, lo = split(right[at] + equilibrium + inflow)
            block = packed[at]
            fresh = jnp.dot(
                jnp.concatenate([block, block], axis=1),
                jnp.concatenate([hi, hi, lo, lo], axis=0),
                preferred_element_type=F32,
            )
            store(v, fresh)


def middle_kernel(
    slabs, right_away, packed, recv, mixed, fresh_away, moments_away, send_away, planes, columns, sums,
    right, fresh, moments, send, arrived, sent, sent_moments, sent_send,
):
    place = Place(slabs)
    mask = outgoing_mask(lane_index((16, 128)), place.sign_x)
    face = trace_face(place.sign_x)
    fetch, wait = stream([(lambda i: velocity_block(right_away, i), lambda i: velocity_block(right, i), arrived)])
    put, finish = stream(
        [
            (lambda i: velocity_block(fresh, i), lambda i: velocity_block(fresh_away, i), sent),
            (lambda i: velocity_block(send, i), lambda i: velocity_block(send_away, i), sent_send),
        ]
    )
    start_all(fetch)
    split_planes(mixed, planes)
    sums[...] = jnp.zeros_like(sums)

    def loop(step, carry):
        def store(v, column):
            fresh[step * 16 + v] = column
            trace = sum(face[p0] * column[p0 * 16 : p0 * 16 + 16] for p0 in range(4))
            outgoing = jnp.where(mask[:8], trace[8:], pltpu.roll(trace[:8], HALF, 1))
            send[step * 16 + v] = outgoing

        wait(step)
        relax(place, step, right, packed, recv, planes, columns, mask, store)
        put(step)
        y = place.speed_y(step)
        weight = jnp.exp(jnp.full((64, 128), -0.5, F32) * (y * y)) * (1.0 / TOTAL)
        s = [None] * 4
        for low in range(8):
            z, w = float(SPEED[15 - low]), float(WEIGHT[low])
            minus, plus = fresh[step * 16 + low], fresh[step * 16 + 15 - low]
            terms = [w * (plus + minus), (w * z) * (plus - minus)]
            for k in range(4):
                term = terms[k % 2] if k < 2 else (z * z) * terms[k % 2]
                s[k] = term if s[k] is None else s[k] + term
        s = [weight * part for part in s]
        y2 = y * y
        totals = [s[0], y * s[0], s[1], y2 * s[0], s[2], y * s[1], y * (y2 * s[0] + s[2]), s[3] + y2 * s[1]]
        for j in range(8):
            sums[j] = sums[j] + totals[j]
        return carry

    lax.fori_loop(0, 8, loop, 0)
    for j in range(8):
        moments[pl.ds(j, 64, stride=8), :] = sums[j]
    copy = pltpu.make_async_copy(moments, moments_away, sent_moments)
    copy.start()
    for step in range(8):
        finish(step)
    copy.wait()


def middle(slabs, right, packed, recv, mixed):
    fresh, moments, send = pl.pallas_call(
        functools.partial(middle_kernel, slabs),
        in_specs=[HBM, VMEM, VMEM, VMEM],
        out_specs=[HBM] * 3,
        out_shape=[pltpu.HBM((128, 64, 128), F32), pltpu.HBM((512, 128), F32), pltpu.HBM((128, 8, 128), F32)],
        scratch_shapes=[
            pltpu.VMEM((8, 64, 128), F32),
            pltpu.VMEM((4, 64, 128), F32),
            pltpu.VMEM((8, 64, 128), F32),
            BLOCKS_V,
            BLOCKS_V,
            pltpu.VMEM((512, 128), F32),
            pltpu.VMEM((128, 8, 128), F32),
            SEMS,
            SEMS,
            pltpu.SemaphoreType.DMA,
            SEMS,
        ],
        compiler_params=PARAMS,
        name="middle",
    )(away(right), here(packed), here(recv), here(mixed))
    return fresh, moments.reshape(VEL, 16, 128), send


def last_kernel(slabs, right_away, packed, recv, mixed, out, planes, columns, right, blocks, arrived, sent):
    place = Place(slabs)
    mask = outgoing_mask(lane_index((16, 128)), place.sign_x)
    fetch, wait = stream([(lambda i: velocity_block(right_away, i), lambda i: velocity_block(right, i), arrived)])
    put, finish = stream([(lambda i: blocks.at[i], lambda i: mode_block(out, i), sent)])
    start_all(fetch)
    split_planes(mixed, planes)

    def loop(step, carry):
        flat = blocks.at[step].reshape(1024, 128)

        def store(v, fresh):
            flat[pl.ds(v, 64, stride=16), :] = fresh

        wait(step)
        relax(place, step, right, packed, recv, planes, columns, mask, store)
        put(step)
        return carry

    lax.fori_loop(0, 8, loop, 0)
    for step in range(8):
        finish(step)


def last(slabs, right, packed, recv, mixed):
    return pl.pallas_call(
        functools.partial(last_kernel, slabs),
        in_specs=[HBM, VMEM, VMEM, VMEM],
        out_specs=HBM,
        out_shape=pltpu.HBM((64, 128, 128), F32),
        scratch_shapes=[
            pltpu.VMEM((8, 64, 128), F32),
            pltpu.VMEM((4, 64, 128), F32),
            BLOCKS_V,
            BLOCKS_Q,
            SEMS,
            SEMS,
        ],
        compiler_params=PARAMS,
        name="last",
    )(away(right), here(packed), here(recv), here(mixed))


def halo_pairs(slabs):
    pairs = []
    for slab in range(slabs):
        for vel in range(VEL):
            other = slab + 1 if vel >= VEL // 2 else slab - 1
            if 0 <= other < slabs:
                pairs.append((slab * VEL + vel, other * VEL + vel))
    return pairs


def body(slabs, prior, block_inverse):
    mix = jnp.asarray(MIX)
    axes = ("sp", "vel")
    pairs = halo_pairs(slabs)
    cells = prior.reshape(64, 128, 128)
    moments = first_moments(cells)
    mixed, (right, send) = sum_over_velocities(mix, moments, prepare(slabs, cells))
    recv = lax.ppermute(send, axes, pairs)
    packed = pack(block_inverse)
    fresh, moments, send = middle(slabs, right, packed, recv, mixed)
    recv = lax.ppermute(send, axes, pairs)
    mixed, right = sum_over_velocities(mix, moments, prepare_next(slabs, fresh, cells))
    return last(slabs, right, packed, recv, mixed).reshape(prior.shape)


def solution(mesh):
    spec = P(None, None, None, "vel", "sp")
    return jax.shard_map(
        functools.partial(body, mesh.shape["sp"]),
        mesh=mesh,
        in_specs=(spec, P("vel", None, None)),
        out_specs=spec,
        check_vma=False,
    )
```

```python
import functools

import jax
import jax.numpy as jnp
import numpy as np
from jax import lax
from jax.experimental import pallas as pl
from jax.experimental.pallas import tpu as pltpu
from jax.sharding import PartitionSpec as P

NV1 = 16
COUPLING = 0.25
LID_SPEED = 0.6
STEP = 6.0 / NV1
CENTRE = 0.5 * (NV1 - 1)
VEL = 32
LOCAL_Y = 8
HIGH = [float(np.sqrt(k + 0.5)) for k in range(4)]
HIGHEST = lax.Precision.HIGHEST
F32 = jnp.float32
BF16 = jnp.bfloat16
HALF = 64


def ring_hops(vel):
    along_y, along_z = min(vel // 4 % 4, 4 - vel // 4 % 4), min(vel % 4, 4 - vel % 4)
    return vel // 16, along_y + along_z, vel


ORDER = sorted(range(VEL), key=ring_hops, reverse=True)


def grid_speed(index):
    return (np.asarray(index, np.float64) - CENTRE) * STEP


def local_polynomials(y, z):
    r2 = y * y + z * z
    return [np.ones_like(r2), y, z, y * y, z * z, y * z, r2 * y, r2 * z]


def combination(x):
    c = np.zeros((13, 8))
    c[0, 0] = 1.0
    c[1, 0] = x
    c[2, 1] = 1.0
    c[3, 2] = 1.0
    c[4, 0] = x * x - 1.0
    c[5, 3], c[5, 0] = 1.0, -1.0
    c[6, 4], c[6, 0] = 1.0, -1.0
    c[7, 1] = x
    c[8, 2] = x
    c[9, 5] = 1.0
    c[10, 0], c[10, 3], c[10, 4] = x * (x * x - 5.0), x, x
    c[11, 1], c[11, 6] = x * x - 5.0, 1.0
    c[12, 2], c[12, 7] = x * x - 5.0, 1.0
    return c


def tables():
    speed = grid_speed(np.arange(NV1))
    weight = np.exp(-0.5 * speed * speed)
    total = weight.sum()
    weight = weight / total
    x, y, z = np.meshgrid(speed, speed, speed, indexing="ij")
    w = weight[:, None, None] * weight[None, :, None] * weight[None, None, :]
    g = np.stack(local_polynomials(y, z))
    per_x = np.stack([combination(s) for s in speed])
    h = np.einsum("xkj,jxyz->kxyz", per_x, g)
    norm = (w * h * h).sum(axis=(1, 2, 3))
    source = np.repeat(per_x * weight[:, None, None], 2, axis=0)
    target = np.repeat(per_x, 2, axis=0)
    mix = np.einsum("tkj,k,ski->tjsi", target, 1.0 / norm, source).reshape(VEL * 8, VEL * 8)
    mix = mix.reshape(VEL, 8, VEL, 8)[ORDER][:, :, ORDER].reshape(VEL * 8, VEL * 8)
    return mix.astype(np.float32), speed, weight, float(total)


MIX, SPEED, WEIGHT, TOTAL = tables()


def split(a):
    hi = a.astype(BF16)
    return hi, (a - hi.astype(F32)).astype(BF16)


def lane_index(shape):
    return lax.broadcasted_iota(jnp.int32, shape, len(shape) - 1)


def row_index(shape):
    return lax.broadcasted_iota(jnp.int32, shape, len(shape) - 2)


class Place:
    def __init__(self, slabs):
        vel, slab = lax.axis_index("vel"), lax.axis_index("sp")
        self.vx = (vel // 2).astype(F32) * STEP - CENTRE * STEP
        self.sign_x = jnp.where(vel >= VEL // 2, 1.0, -1.0)
        self.scale_x = COUPLING * jnp.abs(self.vx)
        self.first_y = vel % 2 * LOCAL_Y
        self.sign_y = jnp.where(vel % 2 == 1, 1.0, -1.0)
        boundary = jnp.where(vel >= VEL // 2, 0, slabs - 1)
        self.wall_x = jnp.where(slab == boundary, 2.0, 0.0)

    def speed_y(self, step):
        return (self.first_y + step).astype(F32) * STEP - CENTRE * STEP


def outgoing_mask(lane, sign):
    return jnp.where(sign > 0, lane, 2 * HALF - 1 - lane) >= HALF


def trace_face(sign):
    return [HIGH[k] if k % 2 == 0 else HIGH[k] * sign for k in range(4)]


def lift_faces(sign):
    return [HIGH[k] if k % 2 == 0 else -HIGH[k] * sign for k in range(4)]


def kept(*shape, dtype=F32):
    return pltpu.VMEM(shape, dtype)


def here(x):
    return pltpu.with_memory_space_constraint(x, pltpu.VMEM)


def away(x):
    return pltpu.with_memory_space_constraint(x, pltpu.HBM)


def velocity_block(ref, step):
    return ref.at[pl.ds(pl.multiple_of(step * 16, 16), 16)]


def mode_block(ref, step):
    return ref.at[:, pl.ds(pl.multiple_of(step * 16, 16), 16), :]


def stream(pairs):
    def copies(step):
        return [pltpu.make_async_copy(source(step), target(step), sems.at[step]) for source, target, sems in pairs]

    def start(step):
        for copy in copies(step):
            copy.start()

    def wait(step):
        for copy in copies(step):
            copy.wait()

    return start, wait


def start_all(start):
    for step in range(8):
        start(step)


BLOCKS_V = pltpu.VMEM((128, 64, 128), F32)
BLOCKS_Q = pltpu.VMEM((8, 64, 16, 128), F32)
SEMS = pltpu.SemaphoreType.DMA((8,))


VMEM = pl.BlockSpec(memory_space=pltpu.VMEM)
HBM = pl.BlockSpec(memory_space=pltpu.HBM)
PARAMS = pltpu.CompilerParams(vmem_limit_bytes=24 * 2**20)


def moment_weights(first_y):
    lane, row = lane_index((8, 128)), row_index((8, 128))
    y = (lane // 16 + first_y).astype(F32) * STEP - CENTRE * STEP
    z = (lane % 16).astype(F32) * STEP - CENTRE * STEP
    r2 = y * y + z * z
    polynomial = jnp.ones((8, 128), F32)
    for j, g in enumerate([y, z, y * y, z * z, y * z, r2 * y, r2 * z]):
        polynomial = jnp.where(row == j + 1, g, polynomial)
    hi, lo = split(polynomial * jnp.exp(-0.5 * r2) * (1.0 / (TOTAL * TOTAL)))
    half = jnp.concatenate([hi.astype(F32), lo.astype(F32)], axis=0).astype(BF16)
    return jnp.concatenate([half, half], axis=1)


FIRST = 16
FIRST_SEMS = pltpu.SemaphoreType.DMA((64 // FIRST,))


def first_moments_kernel(prior, moments, cells, sums, arrived, sent):
    def part(ref, step):
        return ref.at[pl.ds(step * FIRST, FIRST)]

    fetch, wait = stream([(lambda i: part(prior, i), lambda i: part(cells, i), arrived)])
    put, finish = stream([(lambda i: part(sums, i), lambda i: part(moments, i), sent)])
    for step in range(64 // FIRST):
        fetch(step)
    weights = moment_weights(lax.axis_index("vel") % 2 * LOCAL_Y)
    for step in range(64 // FIRST):
        wait(step)
        for q in range(step * FIRST, step * FIRST + FIRST):
            hi, lo = split(cells[q])
            product = jnp.dot(weights, jnp.concatenate([hi, lo], axis=0), preferred_element_type=F32)
            sums[q] = product[:8] + product[8:]
        put(step)
    for step in range(64 // FIRST):
        finish(step)


def first_moments(prior):
    return pl.pallas_call(
        first_moments_kernel,
        in_specs=[HBM],
        out_specs=HBM,
        out_shape=pltpu.HBM((64, 8, 128), F32),
        scratch_shapes=[pltpu.VMEM((64, 128, 128), F32), pltpu.VMEM((64, 8, 128), F32), FIRST_SEMS, FIRST_SEMS],
        compiler_params=PARAMS,
        name="first_moments",
    )(away(prior)).reshape(VEL, 16, 128)


def pack_kernel(inverse, packed, rows, blocks, arrived):
    fetch, wait = stream([(lambda i: inverse.at[pl.ds(i * 8, 8)], lambda i: blocks.at[pl.ds(i * 8, 8)], arrived)])
    for step in range(8):
        fetch(step)
    for step in range(8):
        wait(step)
        for p in range(step * 8, step * 8 + 8):
            hi, lo = split(blocks[p])
            both = jnp.concatenate([hi.astype(F32), lo.astype(F32)], axis=0)
            rows[pl.ds(p, 128, stride=PITCH), :] = both.T

    def step(v, carry):
        packed[v] = rows[pl.ds(pl.multiple_of(v * PITCH, 8), 64), :].astype(BF16)
        return carry

    lax.fori_loop(0, 128, step, 0, unroll=8)


PITCH = 72


def pack(inverse):
    return pl.pallas_call(
        pack_kernel,
        in_specs=[HBM],
        out_specs=VMEM,
        out_shape=kept(128, 64, 128, dtype=BF16),
        scratch_shapes=[pltpu.VMEM((128 * PITCH, 128), F32), pltpu.VMEM((64, 64, 128), F32), SEMS],
        compiler_params=PARAMS,
        name="pack",
    )(away(jnp.transpose(inverse, (1, 2, 0))))


def mix_kernel(mix, gathered, mixed):
    part = jnp.concatenate([gathered[:, low * 8 : low * 8 + 8, :].reshape(VEL * 8, 128) for low in range(2)], axis=1)
    result = jnp.dot(mix[...], part, preferred_element_type=F32, precision=HIGHEST)
    for low in range(2):
        mixed[:, low * 8 : low * 8 + 8, :] = result[:, low * 128 : low * 128 + 128].reshape(VEL, 8, 128)


def mix_moments(mix, gathered):
    return pl.pallas_call(
        mix_kernel,
        in_specs=[VMEM, VMEM],
        out_specs=VMEM,
        out_shape=kept(VEL, 16, 128),
        compiler_params=PARAMS,
        name="mix_moments",
    )(here(mix), here(gathered))


def sum_over_velocities(mix, partial_sums, beside):
    gathered = lax.all_to_all(partial_sums, "vel", 0, 0, axis_index_groups=[ORDER])
    gathered, beside = lax.optimization_barrier((gathered, beside))
    mixed = mix_moments(mix, gathered)
    mixed, beside = lax.optimization_barrier((mixed, beside))
    return lax.all_to_all(mixed, "vel", 0, 0, axis_index_groups=[ORDER]).reshape(512, 128), beside


def add_inflow(source, base, target, send, place, step, mask):
    y = place.speed_y(step)
    lane, row = lane_index((8, 128)), row_index((8, 128))
    trace_x, lift_x = trace_face(place.sign_x), lift_faces(place.sign_x)
    trace_y, lift_y = trace_face(place.sign_y), lift_faces(place.sign_y)
    up_y = place.sign_y > 0
    shift_y = jnp.where(up_y, 8, 120)
    cell_y = jnp.where(up_y, lane // 8 % 8, 7 - lane // 8 % 8)
    scale_y = jnp.where(cell_y > 0, COUPLING * jnp.abs(y), 0.0)
    wall_y = jnp.where(cell_y > 0, 0.0, 2.0 * COUPLING * jnp.abs(y))
    scale_x = jnp.where(mask, place.scale_x, 0.0)
    wall_x = jnp.where(mask, 0.0, place.wall_x * place.scale_x)
    lid = 2.0 * jnp.exp(jnp.full((8, 128), LID_SPEED, F32) * place.vx - 0.5 * LID_SPEED * LID_SPEED)
    for part in range(2):
        up = part == 1
        speed = jnp.abs((row + (part * 8)).astype(F32) - CENTRE) * (STEP * COUPLING)
        inside = (lane % 8 > 0) if up else (lane % 8 < 7)
        scale_z = jnp.where(inside, speed, 0.0)
        wall_z = jnp.where(inside, 0.0, speed * (2.0 if up else lid))
        trace_z, lift_z = trace_face(1.0 if up else -1.0), lift_faces(1.0 if up else -1.0)
        face_x = [None] * 16
        for low in range(8):
            pair = []
            for r in (low, low + 8):
                trace = sum(trace_x[p0] * source(part, p0 * 16 + r) for p0 in range(4))
                turned = pltpu.roll(trace, HALF, 1)
                pair.append((trace, turned))
                face_x[r] = turned * scale_x
            if send is not None:
                send[part * 64 + low * 8 : part * 64 + low * 8 + 8, :] = jnp.where(mask, pair[1][0], pair[0][1])
        face_x[0] = face_x[0] + wall_x
        for p0 in range(4):
            x = [[source(part, p0 * 16 + p1 * 4 + p2) for p2 in range(4)] for p1 in range(4)]
            face_y, face_z = [], []
            for k in range(4):
                ty = sum(trace_y[p1] * x[p1][k] for p1 in range(4))
                ty = pltpu.roll(ty, shift_y, 1) * scale_y
                tz = sum(trace_z[p2] * x[k][p2] for p2 in range(4))
                tz = pltpu.roll(tz, 1 if up else 127, 1) * scale_z
                if p0 == 0 and k == 0:
                    ty = ty + wall_y
                    tz = tz + wall_z
                face_y.append(ty)
                face_z.append(tz)
            for p1 in range(4):
                for p2 in range(4):
                    q, r = p0 * 16 + p1 * 4 + p2, p1 * 4 + p2
                    value = base(part, q) + lift_x[p0] * face_x[r] + lift_y[p1] * face_y[p2] + lift_z[p2] * face_z[p1]
                    target[part * 512 + q * 8 : part * 512 + q * 8 + 8, :] = value


def velocity_rows(v):
    return pl.ds(v // 8 * 512 + v % 8, 64, stride=8)


def block_reader(ref):
    def read(part, q):
        return ref[q, part * 8 : part * 8 + 8, :]

    return read


def row_reader(ref):
    def read(part, q):
        return ref[part * 512 + q * 8 : part * 512 + q * 8 + 8, :]

    return read


def prepare_kernel(
    slabs, prior, right, send_away, scratch, outgoing, cells, made, send, arrived, sent, sent_send
):
    place = Place(slabs)
    mask = outgoing_mask(lane_index((8, 128)), place.sign_x)
    fetch, wait = stream([(lambda i: mode_block(prior, i), lambda i: cells.at[i], arrived)])
    put, finish = stream(
        [
            (lambda i: velocity_block(made, i), lambda i: velocity_block(right, i), sent),
            (lambda i: velocity_block(send, i), lambda i: velocity_block(send_away, i), sent_send),
        ]
    )
    start_all(fetch)

    def loop(step, carry):
        wait(step)
        read = block_reader(cells.at[step])
        add_inflow(read, read, scratch, outgoing, place, step, mask)
        for v in range(16):
            made[step * 16 + v] = scratch[velocity_rows(v), :]
            send[step * 16 + v] = outgoing[pl.ds(v // 8 * 64 + v % 8, 8, stride=8), :]
        put(step)
        return carry

    lax.fori_loop(0, 8, loop, 0)
    for step in range(8):
        finish(step)


def prepare(slabs, prior):
    return pl.pallas_call(
        functools.partial(prepare_kernel, slabs),
        in_specs=[HBM],
        out_specs=[HBM, HBM],
        out_shape=[pltpu.HBM((128, 64, 128), F32), pltpu.HBM((128, 8, 128), F32)],
        scratch_shapes=[
            pltpu.VMEM((1024, 128), F32),
            pltpu.VMEM((128, 128), F32),
            BLOCKS_Q,
            BLOCKS_V,
            pltpu.VMEM((128, 8, 128), F32),
            SEMS,
            SEMS,
            SEMS,
        ],
        compiler_params=PARAMS,
        name="prepare",
    )(away(prior))


def prepare_next_kernel(
    slabs, fresh, prior, right, rows, scratch, columns, cells, made, arrived, arrived_prior, sent
):
    place = Place(slabs)
    mask = outgoing_mask(lane_index((8, 128)), place.sign_x)
    fetch, wait = stream(
        [
            (lambda i: velocity_block(fresh, i), lambda i: velocity_block(columns, i), arrived),
            (lambda i: mode_block(prior, i), lambda i: cells.at[i], arrived_prior),
        ]
    )
    put, finish = stream([(lambda i: velocity_block(made, i), lambda i: velocity_block(right, i), sent)])
    start_all(fetch)

    def loop(step, carry):
        wait(step)
        for v in range(16):
            rows[velocity_rows(v), :] = columns[step * 16 + v]
        add_inflow(row_reader(rows), block_reader(cells.at[step]), scratch, None, place, step, mask)
        for v in range(16):
            made[step * 16 + v] = scratch[velocity_rows(v), :]
        put(step)
        return carry

    lax.fori_loop(0, 8, loop, 0)
    for step in range(8):
        finish(step)


def prepare_next(slabs, fresh, prior):
    return pl.pallas_call(
        functools.partial(prepare_next_kernel, slabs),
        in_specs=[HBM, HBM],
        out_specs=HBM,
        out_shape=pltpu.HBM((128, 64, 128), F32),
        scratch_shapes=[
            pltpu.VMEM((1024, 128), F32),
            pltpu.VMEM((1024, 128), F32),
            BLOCKS_V,
            BLOCKS_Q,
            BLOCKS_V,
            SEMS,
            SEMS,
            SEMS,
        ],
        compiler_params=PARAMS,
        name="prepare_next",
    )(away(fresh), away(prior))


def split_planes(mixed, planes):
    for j in range(8):
        planes[j] = mixed[pl.ds(j, 64, stride=8), :]


def relax(place, step, right, packed, recv, planes, columns, mask, store):
    y = place.speed_y(step)
    columns[0] = planes[0] + y * (planes[1] + y * (planes[3] + y * planes[6]))
    columns[1] = planes[2] + y * (planes[5] + y * planes[7])
    columns[2] = planes[4] + y * planes[6]
    columns[3] = planes[7]
    lift = [place.scale_x * face for face in lift_faces(place.sign_x)]
    for low in range(8):
        z = float(SPEED[15 - low])
        even = columns[0] + (z * z) * columns[2]
        odd = z * columns[1] + (z * z * z) * columns[3]
        for v, equilibrium in ((low, even - odd), (15 - low, even + odd)):
            at = step * 16 + v
            edge = recv[at]
            both = jnp.concatenate([edge, pltpu.roll(edge, HALF, 1)], axis=0)
            both = jnp.where(mask, 0.0, both)
            inflow = jnp.concatenate([lift[p0] * both for p0 in range(4)], axis=0)
            hi, lo = split(right[at] + equilibrium + inflow)
            block = packed[at]
            fresh = jnp.dot(
                jnp.concatenate([block, block], axis=1),
                jnp.concatenate([hi, hi, lo, lo], axis=0),
                preferred_element_type=F32,
            )
            store(v, fresh)


def middle_kernel(
    slabs, right_away, packed, recv, mixed, fresh_away, moments_away, send_away, planes, columns, sums,
    right, fresh, moments, send, arrived, sent, sent_moments, sent_send,
):
    place = Place(slabs)
    mask = outgoing_mask(lane_index((16, 128)), place.sign_x)
    face = trace_face(place.sign_x)
    fetch, wait = stream([(lambda i: velocity_block(right_away, i), lambda i: velocity_block(right, i), arrived)])
    put, finish = stream(
        [
            (lambda i: velocity_block(fresh, i), lambda i: velocity_block(fresh_away, i), sent),
            (lambda i: velocity_block(send, i), lambda i: velocity_block(send_away, i), sent_send),
        ]
    )
    start_all(fetch)
    split_planes(mixed, planes)
    sums[...] = jnp.zeros_like(sums)

    def loop(step, carry):
        def store(v, column):
            fresh[step * 16 + v] = column
            trace = sum(face[p0] * column[p0 * 16 : p0 * 16 + 16] for p0 in range(4))
            outgoing = jnp.where(mask[:8], trace[8:], pltpu.roll(trace[:8], HALF, 1))
            send[step * 16 + v] = outgoing

        wait(step)
        relax(place, step, right, packed, recv, planes, columns, mask, store)
        put(step)
        y = place.speed_y(step)
        weight = jnp.exp(jnp.full((64, 128), -0.5, F32) * (y * y)) * (1.0 / TOTAL)
        s = [None] * 4
        for low in range(8):
            z, w = float(SPEED[15 - low]), float(WEIGHT[low])
            minus, plus = fresh[step * 16 + low], fresh[step * 16 + 15 - low]
            terms = [w * (plus + minus), (w * z) * (plus - minus)]
            for k in range(4):
                term = terms[k % 2] if k < 2 else (z * z) * terms[k % 2]
                s[k] = term if s[k] is None else s[k] + term
        s = [weight * part for part in s]
        y2 = y * y
        totals = [s[0], y * s[0], s[1], y2 * s[0], s[2], y * s[1], y * (y2 * s[0] + s[2]), s[3] + y2 * s[1]]
        for j in range(8):
            sums[j] = sums[j] + totals[j]
        return carry

    lax.fori_loop(0, 8, loop, 0)
    for j in range(8):
        moments[pl.ds(j, 64, stride=8), :] = sums[j]
    copy = pltpu.make_async_copy(moments, moments_away, sent_moments)
    copy.start()
    for step in range(8):
        finish(step)
    copy.wait()


def middle(slabs, right, packed, recv, mixed):
    fresh, moments, send = pl.pallas_call(
        functools.partial(middle_kernel, slabs),
        in_specs=[HBM, VMEM, VMEM, VMEM],
        out_specs=[HBM] * 3,
        out_shape=[pltpu.HBM((128, 64, 128), F32), pltpu.HBM((512, 128), F32), pltpu.HBM((128, 8, 128), F32)],
        scratch_shapes=[
            pltpu.VMEM((8, 64, 128), F32),
            pltpu.VMEM((4, 64, 128), F32),
            pltpu.VMEM((8, 64, 128), F32),
            BLOCKS_V,
            BLOCKS_V,
            pltpu.VMEM((512, 128), F32),
            pltpu.VMEM((128, 8, 128), F32),
            SEMS,
            SEMS,
            pltpu.SemaphoreType.DMA,
            SEMS,
        ],
        compiler_params=PARAMS,
        name="middle",
    )(away(right), here(packed), here(recv), here(mixed))
    return fresh, moments.reshape(VEL, 16, 128), send


def last_kernel(slabs, right_away, packed, recv, mixed, out, planes, columns, right, blocks, arrived, sent):
    place = Place(slabs)
    mask = outgoing_mask(lane_index((16, 128)), place.sign_x)
    fetch, wait = stream([(lambda i: velocity_block(right_away, i), lambda i: velocity_block(right, i), arrived)])
    put, finish = stream([(lambda i: blocks.at[i], lambda i: mode_block(out, i), sent)])
    start_all(fetch)
    split_planes(mixed, planes)

    def loop(step, carry):
        flat = blocks.at[step].reshape(1024, 128)

        def store(v, fresh):
            flat[pl.ds(v, 64, stride=16), :] = fresh

        wait(step)
        relax(place, step, right, packed, recv, planes, columns, mask, store)
        put(step)
        return carry

    lax.fori_loop(0, 8, loop, 0)
    for step in range(8):
        finish(step)


def last(slabs, right, packed, recv, mixed):
    return pl.pallas_call(
        functools.partial(last_kernel, slabs),
        in_specs=[HBM, VMEM, VMEM, VMEM],
        out_specs=HBM,
        out_shape=pltpu.HBM((64, 128, 128), F32),
        scratch_shapes=[
            pltpu.VMEM((8, 64, 128), F32),
            pltpu.VMEM((4, 64, 128), F32),
            BLOCKS_V,
            BLOCKS_Q,
            SEMS,
            SEMS,
        ],
        compiler_params=PARAMS,
        name="last",
    )(away(right), here(packed), here(recv), here(mixed))


def halo_pairs(slabs):
    pairs = []
    for slab in range(slabs):
        for vel in range(VEL):
            other = slab + 1 if vel >= VEL // 2 else slab - 1
            if 0 <= other < slabs:
                pairs.append((slab * VEL + vel, other * VEL + vel))
    return pairs


def body(slabs, prior, block_inverse):
    mix = jnp.asarray(MIX)
    axes = ("sp", "vel")
    pairs = halo_pairs(slabs)
    cells = prior.reshape(64, 128, 128)
    moments = first_moments(cells)
    mixed, (right, send) = sum_over_velocities(mix, moments, prepare(slabs, cells))
    recv = lax.ppermute(send, axes, pairs)
    packed = pack(block_inverse)
    fresh, moments, send = middle(slabs, right, packed, recv, mixed)
    recv = lax.ppermute(send, axes, pairs)
    mixed, right = sum_over_velocities(mix, moments, prepare_next(slabs, fresh, cells))
    return last(slabs, right, packed, recv, mixed).reshape(prior.shape)


def solution(mesh):
    spec = P(None, None, None, "vel", "sp")
    return jax.shard_map(
        functools.partial(body, mesh.shape["sp"]),
        mesh=mesh,
        in_specs=(spec, P("vel", None, None)),
        out_specs=spec,
        check_vma=False,
    )
```

```python
import functools

import jax
import jax.numpy as jnp
import numpy as np
from jax import lax
from jax.experimental import pallas as pl
from jax.experimental.pallas import tpu as pltpu
from jax.sharding import PartitionSpec as P

NV1 = 16
COUPLING = 0.25
LID_SPEED = 0.6
STEP = 6.0 / NV1
CENTRE = 0.5 * (NV1 - 1)
VEL = 32
LOCAL_Y = 8
HIGH = [float(np.sqrt(k + 0.5)) for k in range(4)]
HIGHEST = lax.Precision.HIGHEST
F32 = jnp.float32
BF16 = jnp.bfloat16
HALF = 64


def ring_hops(vel):
    along_y, along_z = min(vel // 4 % 4, 4 - vel // 4 % 4), min(vel % 4, 4 - vel % 4)
    return vel // 16, along_y + along_z, vel


ORDER = sorted(range(VEL), key=ring_hops, reverse=True)


def grid_speed(index):
    return (np.asarray(index, np.float64) - CENTRE) * STEP


def local_polynomials(y, z):
    r2 = y * y + z * z
    return [np.ones_like(r2), y, z, y * y, z * z, y * z, r2 * y, r2 * z]


def combination(x):
    c = np.zeros((13, 8))
    c[0, 0] = 1.0
    c[1, 0] = x
    c[2, 1] = 1.0
    c[3, 2] = 1.0
    c[4, 0] = x * x - 1.0
    c[5, 3], c[5, 0] = 1.0, -1.0
    c[6, 4], c[6, 0] = 1.0, -1.0
    c[7, 1] = x
    c[8, 2] = x
    c[9, 5] = 1.0
    c[10, 0], c[10, 3], c[10, 4] = x * (x * x - 5.0), x, x
    c[11, 1], c[11, 6] = x * x - 5.0, 1.0
    c[12, 2], c[12, 7] = x * x - 5.0, 1.0
    return c


def tables():
    speed = grid_speed(np.arange(NV1))
    weight = np.exp(-0.5 * speed * speed)
    total = weight.sum()
    weight = weight / total
    x, y, z = np.meshgrid(speed, speed, speed, indexing="ij")
    w = weight[:, None, None] * weight[None, :, None] * weight[None, None, :]
    g = np.stack(local_polynomials(y, z))
    per_x = np.stack([combination(s) for s in speed])
    h = np.einsum("xkj,jxyz->kxyz", per_x, g)
    norm = (w * h * h).sum(axis=(1, 2, 3))
    source = np.repeat(per_x * weight[:, None, None], 2, axis=0)
    target = np.repeat(per_x, 2, axis=0)
    mix = np.einsum("tkj,k,ski->tjsi", target, 1.0 / norm, source).reshape(VEL * 8, VEL * 8)
    mix = mix.reshape(VEL, 8, VEL, 8)[ORDER][:, :, ORDER].reshape(VEL * 8, VEL * 8)
    return mix.astype(np.float32), speed, weight, float(total)


MIX, SPEED, WEIGHT, TOTAL = tables()


def split(a):
    hi = a.astype(BF16)
    return hi, (a - hi.astype(F32)).astype(BF16)


def lane_index(shape):
    return lax.broadcasted_iota(jnp.int32, shape, len(shape) - 1)


def row_index(shape):
    return lax.broadcasted_iota(jnp.int32, shape, len(shape) - 2)


class Place:
    def __init__(self, slabs):
        vel, slab = lax.axis_index("vel"), lax.axis_index("sp")
        self.vx = (vel // 2).astype(F32) * STEP - CENTRE * STEP
        self.sign_x = jnp.where(vel >= VEL // 2, 1.0, -1.0)
        self.scale_x = COUPLING * jnp.abs(self.vx)
        self.first_y = vel % 2 * LOCAL_Y
        self.sign_y = jnp.where(vel % 2 == 1, 1.0, -1.0)
        boundary = jnp.where(vel >= VEL // 2, 0, slabs - 1)
        self.wall_x = jnp.where(slab == boundary, 2.0, 0.0)

    def speed_y(self, step):
        return (self.first_y + step).astype(F32) * STEP - CENTRE * STEP


def outgoing_mask(lane, sign):
    return jnp.where(sign > 0, lane, 2 * HALF - 1 - lane) >= HALF


def trace_face(sign):
    return [HIGH[k] if k % 2 == 0 else HIGH[k] * sign for k in range(4)]


def lift_faces(sign):
    return [HIGH[k] if k % 2 == 0 else -HIGH[k] * sign for k in range(4)]


def kept(*shape, dtype=F32):
    return pltpu.VMEM(shape, dtype)


def here(x):
    return pltpu.with_memory_space_constraint(x, pltpu.VMEM)


def away(x):
    return pltpu.with_memory_space_constraint(x, pltpu.HBM)


def velocity_block(ref, step):
    return ref.at[pl.ds(pl.multiple_of(step * 16, 16), 16)]


def mode_block(ref, step):
    return ref.at[:, pl.ds(pl.multiple_of(step * 16, 16), 16), :]


def stream(pairs):
    def copies(step):
        return [pltpu.make_async_copy(source(step), target(step), sems.at[step]) for source, target, sems in pairs]

    def start(step):
        for copy in copies(step):
            copy.start()

    def wait(step):
        for copy in copies(step):
            copy.wait()

    return start, wait


def start_all(start):
    for step in range(8):
        start(step)


BLOCKS_V = pltpu.VMEM((128, 64, 128), F32)
BLOCKS_Q = pltpu.VMEM((8, 64, 16, 128), F32)
SEMS = pltpu.SemaphoreType.DMA((8,))


VMEM = pl.BlockSpec(memory_space=pltpu.VMEM)
HBM = pl.BlockSpec(memory_space=pltpu.HBM)
PARAMS = pltpu.CompilerParams(vmem_limit_bytes=24 * 2**20)


def moment_weights(first_y):
    lane, row = lane_index((8, 128)), row_index((8, 128))
    y = (lane // 16 + first_y).astype(F32) * STEP - CENTRE * STEP
    z = (lane % 16).astype(F32) * STEP - CENTRE * STEP
    r2 = y * y + z * z
    polynomial = jnp.ones((8, 128), F32)
    for j, g in enumerate([y, z, y * y, z * z, y * z, r2 * y, r2 * z]):
        polynomial = jnp.where(row == j + 1, g, polynomial)
    hi, lo = split(polynomial * jnp.exp(-0.5 * r2) * (1.0 / (TOTAL * TOTAL)))
    half = jnp.concatenate([hi.astype(F32), lo.astype(F32)], axis=0).astype(BF16)
    return jnp.concatenate([half, half], axis=1)


FIRST = 16
FIRST_SEMS = pltpu.SemaphoreType.DMA((64 // FIRST,))


def first_moments_kernel(prior, moments, cells, sums, arrived, sent):
    def part(ref, step):
        return ref.at[pl.ds(step * FIRST, FIRST)]

    fetch, wait = stream([(lambda i: part(prior, i), lambda i: part(cells, i), arrived)])
    put, finish = stream([(lambda i: part(sums, i), lambda i: part(moments, i), sent)])
    for step in range(64 // FIRST):
        fetch(step)
    weights = moment_weights(lax.axis_index("vel") % 2 * LOCAL_Y)
    for step in range(64 // FIRST):
        wait(step)
        for q in range(step * FIRST, step * FIRST + FIRST):
            hi, lo = split(cells[q])
            product = jnp.dot(weights, jnp.concatenate([hi, lo], axis=0), preferred_element_type=F32)
            sums[q] = product[:8] + product[8:]
        put(step)
    for step in range(64 // FIRST):
        finish(step)


def first_moments(prior):
    return pl.pallas_call(
        first_moments_kernel,
        in_specs=[HBM],
        out_specs=HBM,
        out_shape=pltpu.HBM((64, 8, 128), F32),
        scratch_shapes=[pltpu.VMEM((64, 128, 128), F32), pltpu.VMEM((64, 8, 128), F32), FIRST_SEMS, FIRST_SEMS],
        compiler_params=PARAMS,
        name="first_moments",
    )(away(prior)).reshape(VEL, 16, 128)


def pack_kernel(inverse, packed, rows, blocks, arrived):
    fetch, wait = stream([(lambda i: inverse.at[pl.ds(i * 8, 8)], lambda i: blocks.at[pl.ds(i * 8, 8)], arrived)])
    for step in range(8):
        fetch(step)
    for step in range(8):
        wait(step)
        for p in range(step * 8, step * 8 + 8):
            hi, lo = split(blocks[p])
            both = jnp.concatenate([hi.astype(F32), lo.astype(F32)], axis=0)
            rows[pl.ds(p, 128, stride=PITCH), :] = both.T

    def step(v, carry):
        packed[v] = rows[pl.ds(pl.multiple_of(v * PITCH, 8), 64), :].astype(BF16)
        return carry

    lax.fori_loop(0, 128, step, 0, unroll=8)


PITCH = 72


def pack(inverse):
    return pl.pallas_call(
        pack_kernel,
        in_specs=[HBM],
        out_specs=VMEM,
        out_shape=kept(128, 64, 128, dtype=BF16),
        scratch_shapes=[pltpu.VMEM((128 * PITCH, 128), F32), pltpu.VMEM((64, 64, 128), F32), SEMS],
        compiler_params=PARAMS,
        name="pack",
    )(away(jnp.transpose(inverse, (1, 2, 0))))


def mix_kernel(mix, gathered, mixed):
    part = jnp.concatenate([gathered[:, low * 8 : low * 8 + 8, :].reshape(VEL * 8, 128) for low in range(2)], axis=1)
    result = jnp.dot(mix[...], part, preferred_element_type=F32, precision=HIGHEST)
    for low in range(2):
        mixed[:, low * 8 : low * 8 + 8, :] = result[:, low * 128 : low * 128 + 128].reshape(VEL, 8, 128)


def mix_moments(mix, gathered):
    return pl.pallas_call(
        mix_kernel,
        in_specs=[VMEM, VMEM],
        out_specs=VMEM,
        out_shape=kept(VEL, 16, 128),
        compiler_params=PARAMS,
        name="mix_moments",
    )(here(mix), here(gathered))


def sum_over_velocities(mix, partial_sums, beside):
    gathered = lax.all_to_all(partial_sums, "vel", 0, 0, axis_index_groups=[ORDER])
    gathered, beside = lax.optimization_barrier((gathered, beside))
    mixed = mix_moments(mix, gathered)
    return lax.all_to_all(mixed, "vel", 0, 0, axis_index_groups=[ORDER]).reshape(512, 128), beside


def add_inflow(source, base, target, send, place, step, mask):
    y = place.speed_y(step)
    lane, row = lane_index((8, 128)), row_index((8, 128))
    trace_x, lift_x = trace_face(place.sign_x), lift_faces(place.sign_x)
    trace_y, lift_y = trace_face(place.sign_y), lift_faces(place.sign_y)
    up_y = place.sign_y > 0
    shift_y = jnp.where(up_y, 8, 120)
    cell_y = jnp.where(up_y, lane // 8 % 8, 7 - lane // 8 % 8)
    scale_y = jnp.where(cell_y > 0, COUPLING * jnp.abs(y), 0.0)
    wall_y = jnp.where(cell_y > 0, 0.0, 2.0 * COUPLING * jnp.abs(y))
    scale_x = jnp.where(mask, place.scale_x, 0.0)
    wall_x = jnp.where(mask, 0.0, place.wall_x * place.scale_x)
    lid = 2.0 * jnp.exp(jnp.full((8, 128), LID_SPEED, F32) * place.vx - 0.5 * LID_SPEED * LID_SPEED)
    for part in range(2):
        up = part == 1
        speed = jnp.abs((row + (part * 8)).astype(F32) - CENTRE) * (STEP * COUPLING)
        inside = (lane % 8 > 0) if up else (lane % 8 < 7)
        scale_z = jnp.where(inside, speed, 0.0)
        wall_z = jnp.where(inside, 0.0, speed * (2.0 if up else lid))
        trace_z, lift_z = trace_face(1.0 if up else -1.0), lift_faces(1.0 if up else -1.0)
        face_x = [None] * 16
        for low in range(8):
            pair = []
            for r in (low, low + 8):
                trace = sum(trace_x[p0] * source(part, p0 * 16 + r) for p0 in range(4))
                turned = pltpu.roll(trace, HALF, 1)
                pair.append((trace, turned))
                face_x[r] = turned * scale_x
            if send is not None:
                send[part * 64 + low * 8 : part * 64 + low * 8 + 8, :] = jnp.where(mask, pair[1][0], pair[0][1])
        face_x[0] = face_x[0] + wall_x
        for p0 in range(4):
            x = [[source(part, p0 * 16 + p1 * 4 + p2) for p2 in range(4)] for p1 in range(4)]
            face_y, face_z = [], []
            for k in range(4):
                ty = sum(trace_y[p1] * x[p1][k] for p1 in range(4))
                ty = pltpu.roll(ty, shift_y, 1) * scale_y
                tz = sum(trace_z[p2] * x[k][p2] for p2 in range(4))
                tz = pltpu.roll(tz, 1 if up else 127, 1) * scale_z
                if p0 == 0 and k == 0:
                    ty = ty + wall_y
                    tz = tz + wall_z
                face_y.append(ty)
                face_z.append(tz)
            for p1 in range(4):
                for p2 in range(4):
                    q, r = p0 * 16 + p1 * 4 + p2, p1 * 4 + p2
                    value = base(part, q) + lift_x[p0] * face_x[r] + lift_y[p1] * face_y[p2] + lift_z[p2] * face_z[p1]
                    target[part * 512 + q * 8 : part * 512 + q * 8 + 8, :] = value


def velocity_rows(v):
    return pl.ds(v // 8 * 512 + v % 8, 64, stride=8)


def block_reader(ref):
    def read(part, q):
        return ref[q, part * 8 : part * 8 + 8, :]

    return read


def row_reader(ref):
    def read(part, q):
        return ref[part * 512 + q * 8 : part * 512 + q * 8 + 8, :]

    return read


def prepare_kernel(
    slabs, prior, right, send_away, scratch, outgoing, cells, made, send, arrived, sent, sent_send
):
    place = Place(slabs)
    mask = outgoing_mask(lane_index((8, 128)), place.sign_x)
    fetch, wait = stream([(lambda i: mode_block(prior, i), lambda i: cells.at[i], arrived)])
    put, finish = stream(
        [
            (lambda i: velocity_block(made, i), lambda i: velocity_block(right, i), sent),
            (lambda i: velocity_block(send, i), lambda i: velocity_block(send_away, i), sent_send),
        ]
    )
    start_all(fetch)

    def loop(step, carry):
        wait(step)
        read = block_reader(cells.at[step])
        add_inflow(read, read, scratch, outgoing, place, step, mask)
        for v in range(16):
            made[step * 16 + v] = scratch[velocity_rows(v), :]
            send[step * 16 + v] = outgoing[pl.ds(v // 8 * 64 + v % 8, 8, stride=8), :]
        put(step)
        return carry

    lax.fori_loop(0, 8, loop, 0)
    for step in range(8):
        finish(step)


def prepare(slabs, prior):
    return pl.pallas_call(
        functools.partial(prepare_kernel, slabs),
        in_specs=[HBM],
        out_specs=[HBM, HBM],
        out_shape=[pltpu.HBM((128, 64, 128), F32), pltpu.HBM((128, 8, 128), F32)],
        scratch_shapes=[
            pltpu.VMEM((1024, 128), F32),
            pltpu.VMEM((128, 128), F32),
            BLOCKS_Q,
            BLOCKS_V,
            pltpu.VMEM((128, 8, 128), F32),
            SEMS,
            SEMS,
            SEMS,
        ],
        compiler_params=PARAMS,
        name="prepare",
    )(away(prior))


def prepare_next_kernel(
    slabs, fresh, prior, right, rows, scratch, columns, cells, made, arrived, arrived_prior, sent
):
    place = Place(slabs)
    mask = outgoing_mask(lane_index((8, 128)), place.sign_x)
    fetch, wait = stream(
        [
            (lambda i: velocity_block(fresh, i), lambda i: velocity_block(columns, i), arrived),
            (lambda i: mode_block(prior, i), lambda i: cells.at[i], arrived_prior),
        ]
    )
    put, finish = stream([(lambda i: velocity_block(made, i), lambda i: velocity_block(right, i), sent)])
    start_all(fetch)

    def loop(step, carry):
        wait(step)
        for v in range(16):
            rows[velocity_rows(v), :] = columns[step * 16 + v]
        add_inflow(row_reader(rows), block_reader(cells.at[step]), scratch, None, place, step, mask)
        for v in range(16):
            made[step * 16 + v] = scratch[velocity_rows(v), :]
        put(step)
        return carry

    lax.fori_loop(0, 8, loop, 0)
    for step in range(8):
        finish(step)


def prepare_next(slabs, fresh, prior):
    return pl.pallas_call(
        functools.partial(prepare_next_kernel, slabs),
        in_specs=[HBM, HBM],
        out_specs=HBM,
        out_shape=pltpu.HBM((128, 64, 128), F32),
        scratch_shapes=[
            pltpu.VMEM((1024, 128), F32),
            pltpu.VMEM((1024, 128), F32),
            BLOCKS_V,
            BLOCKS_Q,
            BLOCKS_V,
            SEMS,
            SEMS,
            SEMS,
        ],
        compiler_params=PARAMS,
        name="prepare_next",
    )(away(fresh), away(prior))


def split_planes(mixed, planes):
    for j in range(8):
        planes[j] = mixed[pl.ds(j, 64, stride=8), :]


def relax(place, step, right, packed, recv, planes, columns, mask, store):
    y = place.speed_y(step)
    columns[0] = planes[0] + y * (planes[1] + y * (planes[3] + y * planes[6]))
    columns[1] = planes[2] + y * (planes[5] + y * planes[7])
    columns[2] = planes[4] + y * planes[6]
    columns[3] = planes[7]
    lift = [place.scale_x * face for face in lift_faces(place.sign_x)]
    for low in range(8):
        z = float(SPEED[15 - low])
        even = columns[0] + (z * z) * columns[2]
        odd = z * columns[1] + (z * z * z) * columns[3]
        for v, equilibrium in ((low, even - odd), (15 - low, even + odd)):
            at = step * 16 + v
            edge = recv[at]
            both = jnp.concatenate([edge, pltpu.roll(edge, HALF, 1)], axis=0)
            both = jnp.where(mask, 0.0, both)
            inflow = jnp.concatenate([lift[p0] * both for p0 in range(4)], axis=0)
            hi, lo = split(right[at] + equilibrium + inflow)
            block = packed[at]
            fresh = jnp.dot(
                jnp.concatenate([block, block], axis=1),
                jnp.concatenate([hi, hi, lo, lo], axis=0),
                preferred_element_type=F32,
            )
            store(v, fresh)


def middle_kernel(
    slabs, right_away, packed, recv, mixed, fresh_away, moments_away, send_away, planes, columns, sums,
    right, fresh, moments, send, arrived, sent, sent_moments, sent_send,
):
    place = Place(slabs)
    mask = outgoing_mask(lane_index((16, 128)), place.sign_x)
    face = trace_face(place.sign_x)
    fetch, wait = stream([(lambda i: velocity_block(right_away, i), lambda i: velocity_block(right, i), arrived)])
    put, finish = stream(
        [
            (lambda i: velocity_block(fresh, i), lambda i: velocity_block(fresh_away, i), sent),
            (lambda i: velocity_block(send, i), lambda i: velocity_block(send_away, i), sent_send),
        ]
    )
    start_all(fetch)
    split_planes(mixed, planes)
    sums[...] = jnp.zeros_like(sums)

    def loop(step, carry):
        def store(v, column):
            fresh[step * 16 + v] = column
            trace = sum(face[p0] * column[p0 * 16 : p0 * 16 + 16] for p0 in range(4))
            outgoing = jnp.where(mask[:8], trace[8:], pltpu.roll(trace[:8], HALF, 1))
            send[step * 16 + v] = outgoing

        wait(step)
        relax(place, step, right, packed, recv, planes, columns, mask, store)
        put(step)
        y = place.speed_y(step)
        weight = jnp.exp(jnp.full((64, 128), -0.5, F32) * (y * y)) * (1.0 / TOTAL)
        s = [None] * 4
        for low in range(8):
            z, w = float(SPEED[15 - low]), float(WEIGHT[low])
            minus, plus = fresh[step * 16 + low], fresh[step * 16 + 15 - low]
            terms = [w * (plus + minus), (w * z) * (plus - minus)]
            for k in range(4):
                term = terms[k % 2] if k < 2 else (z * z) * terms[k % 2]
                s[k] = term if s[k] is None else s[k] + term
        s = [weight * part for part in s]
        y2 = y * y
        totals = [s[0], y * s[0], s[1], y2 * s[0], s[2], y * s[1], y * (y2 * s[0] + s[2]), s[3] + y2 * s[1]]
        for j in range(8):
            sums[j] = sums[j] + totals[j]
        return carry

    lax.fori_loop(0, 8, loop, 0)
    for j in range(8):
        moments[pl.ds(j, 64, stride=8), :] = sums[j]
    copy = pltpu.make_async_copy(moments, moments_away, sent_moments)
    copy.start()
    for step in range(8):
        finish(step)
    copy.wait()


def middle(slabs, right, packed, recv, mixed):
    fresh, moments, send = pl.pallas_call(
        functools.partial(middle_kernel, slabs),
        in_specs=[HBM, VMEM, VMEM, VMEM],
        out_specs=[HBM] * 3,
        out_shape=[pltpu.HBM((128, 64, 128), F32), pltpu.HBM((512, 128), F32), pltpu.HBM((128, 8, 128), F32)],
        scratch_shapes=[
            pltpu.VMEM((8, 64, 128), F32),
            pltpu.VMEM((4, 64, 128), F32),
            pltpu.VMEM((8, 64, 128), F32),
            BLOCKS_V,
            BLOCKS_V,
            pltpu.VMEM((512, 128), F32),
            pltpu.VMEM((128, 8, 128), F32),
            SEMS,
            SEMS,
            pltpu.SemaphoreType.DMA,
            SEMS,
        ],
        compiler_params=PARAMS,
        name="middle",
    )(away(right), here(packed), here(recv), here(mixed))
    return fresh, moments.reshape(VEL, 16, 128), send


def last_kernel(slabs, right_away, packed, recv, mixed, out, planes, columns, right, blocks, arrived, sent):
    place = Place(slabs)
    mask = outgoing_mask(lane_index((16, 128)), place.sign_x)
    fetch, wait = stream([(lambda i: velocity_block(right_away, i), lambda i: velocity_block(right, i), arrived)])
    put, finish = stream([(lambda i: blocks.at[i], lambda i: mode_block(out, i), sent)])
    start_all(fetch)
    split_planes(mixed, planes)

    def loop(step, carry):
        flat = blocks.at[step].reshape(1024, 128)

        def store(v, fresh):
            flat[pl.ds(v, 64, stride=16), :] = fresh

        wait(step)
        relax(place, step, right, packed, recv, planes, columns, mask, store)
        put(step)
        return carry

    lax.fori_loop(0, 8, loop, 0)
    for step in range(8):
        finish(step)


def last(slabs, right, packed, recv, mixed):
    return pl.pallas_call(
        functools.partial(last_kernel, slabs),
        in_specs=[HBM, VMEM, VMEM, VMEM],
        out_specs=HBM,
        out_shape=pltpu.HBM((64, 128, 128), F32),
        scratch_shapes=[
            pltpu.VMEM((8, 64, 128), F32),
            pltpu.VMEM((4, 64, 128), F32),
            BLOCKS_V,
            BLOCKS_Q,
            SEMS,
            SEMS,
        ],
        compiler_params=PARAMS,
        name="last",
    )(away(right), here(packed), here(recv), here(mixed))


def halo_pairs(slabs):
    pairs = []
    for slab in range(slabs):
        for vel in range(VEL):
            other = slab + 1 if vel >= VEL // 2 else slab - 1
            if 0 <= other < slabs:
                pairs.append((slab * VEL + vel, other * VEL + vel))
    return pairs


def body(slabs, prior, block_inverse):
    mix = jnp.asarray(MIX)
    axes = ("sp", "vel")
    pairs = halo_pairs(slabs)
    cells = prior.reshape(64, 128, 128)
    moments = first_moments(cells)
    mixed, (right, send) = sum_over_velocities(mix, moments, prepare(slabs, cells))
    recv = lax.ppermute(send, axes, pairs)
    packed = pack(block_inverse)
    fresh, moments, send = middle(slabs, right, packed, recv, mixed)
    recv = lax.ppermute(send, axes, pairs)
    mixed, right = sum_over_velocities(mix, moments, prepare_next(slabs, fresh, cells))
    return last(slabs, right, packed, recv, mixed).reshape(prior.shape)


def solution(mesh):
    spec = P(None, None, None, "vel", "sp")
    return jax.shard_map(
        functools.partial(body, mesh.shape["sp"]),
        mesh=mesh,
        in_specs=(spec, P("vel", None, None)),
        out_specs=spec,
        check_vma=False,
    )
```

```python
import functools

import jax
import jax.numpy as jnp
import numpy as np
from jax import lax
from jax.experimental import pallas as pl
from jax.experimental.pallas import tpu as pltpu
from jax.sharding import PartitionSpec as P

NV1 = 16
COUPLING = 0.25
LID_SPEED = 0.6
STEP = 6.0 / NV1
CENTRE = 0.5 * (NV1 - 1)
VEL = 32
LOCAL_Y = 8
HIGH = [float(np.sqrt(k + 0.5)) for k in range(4)]
F32 = jnp.float32
BF16 = jnp.bfloat16
HALF = 64


def ring_hops(vel):
    along_y, along_z = min(vel // 4 % 4, 4 - vel // 4 % 4), min(vel % 4, 4 - vel % 4)
    return vel // 16, along_y + along_z, vel


ORDER = sorted(range(VEL), key=ring_hops, reverse=True)


def grid_speed(index):
    return (np.asarray(index, np.float64) - CENTRE) * STEP


def local_polynomials(y, z):
    r2 = y * y + z * z
    return [np.ones_like(r2), y, z, y * y, z * z, y * z, r2 * y, r2 * z]


def combination(x):
    c = np.zeros((13, 8))
    c[0, 0] = 1.0
    c[1, 0] = x
    c[2, 1] = 1.0
    c[3, 2] = 1.0
    c[4, 0] = x * x - 1.0
    c[5, 3], c[5, 0] = 1.0, -1.0
    c[6, 4], c[6, 0] = 1.0, -1.0
    c[7, 1] = x
    c[8, 2] = x
    c[9, 5] = 1.0
    c[10, 0], c[10, 3], c[10, 4] = x * (x * x - 5.0), x, x
    c[11, 1], c[11, 6] = x * x - 5.0, 1.0
    c[12, 2], c[12, 7] = x * x - 5.0, 1.0
    return c


def tables():
    speed = grid_speed(np.arange(NV1))
    weight = np.exp(-0.5 * speed * speed)
    total = weight.sum()
    weight = weight / total
    x, y, z = np.meshgrid(speed, speed, speed, indexing="ij")
    w = weight[:, None, None] * weight[None, :, None] * weight[None, None, :]
    g = np.stack(local_polynomials(y, z))
    per_x = np.stack([combination(s) for s in speed])
    h = np.einsum("xkj,jxyz->kxyz", per_x, g)
    norm = (w * h * h).sum(axis=(1, 2, 3))
    source = np.repeat(per_x * weight[:, None, None], 2, axis=0)
    target = np.repeat(per_x, 2, axis=0)
    mix = np.einsum("tkj,k,ski->tjsi", target, 1.0 / norm, source).reshape(VEL * 8, VEL * 8)
    mix = mix.reshape(VEL, 8, VEL, 8)[ORDER][:, :, ORDER].reshape(VEL * 8, VEL * 8)
    return mix.astype(np.float32), speed, weight, float(total)


MIX, SPEED, WEIGHT, TOTAL = tables()


def split(a):
    hi = a.astype(BF16)
    return hi, (a - hi.astype(F32)).astype(BF16)


def lane_index(shape):
    return lax.broadcasted_iota(jnp.int32, shape, len(shape) - 1)


def row_index(shape):
    return lax.broadcasted_iota(jnp.int32, shape, len(shape) - 2)


class Place:
    def __init__(self, slabs):
        vel, slab = lax.axis_index("vel"), lax.axis_index("sp")
        self.vx = (vel // 2).astype(F32) * STEP - CENTRE * STEP
        self.sign_x = jnp.where(vel >= VEL // 2, 1.0, -1.0)
        self.scale_x = COUPLING * jnp.abs(self.vx)
        self.first_y = vel % 2 * LOCAL_Y
        self.sign_y = jnp.where(vel % 2 == 1, 1.0, -1.0)
        boundary = jnp.where(vel >= VEL // 2, 0, slabs - 1)
        self.wall_x = jnp.where(slab == boundary, 2.0, 0.0)

    def speed_y(self, step):
        return (self.first_y + step).astype(F32) * STEP - CENTRE * STEP


def outgoing_mask(lane, sign):
    return jnp.where(sign > 0, lane, 2 * HALF - 1 - lane) >= HALF


def trace_face(sign):
    return [HIGH[k] if k % 2 == 0 else HIGH[k] * sign for k in range(4)]


def lift_faces(sign):
    return [HIGH[k] if k % 2 == 0 else -HIGH[k] * sign for k in range(4)]


def kept(*shape, dtype=F32):
    return pltpu.VMEM(shape, dtype)


def here(x):
    return pltpu.with_memory_space_constraint(x, pltpu.VMEM)


def away(x):
    return pltpu.with_memory_space_constraint(x, pltpu.HBM)


def velocity_block(ref, step):
    return ref.at[pl.ds(pl.multiple_of(step * 16, 16), 16)]


def mode_block(ref, step):
    return ref.at[:, pl.ds(pl.multiple_of(step * 16, 16), 16), :]


def stream(pairs):
    def copies(step):
        return [pltpu.make_async_copy(source(step), target(step), sems.at[step]) for source, target, sems in pairs]

    def start(step):
        for copy in copies(step):
            copy.start()

    def wait(step):
        for copy in copies(step):
            copy.wait()

    return start, wait


def start_all(start):
    for step in range(8):
        start(step)


BLOCKS_V = pltpu.VMEM((128, 64, 128), F32)
BLOCKS_Q = pltpu.VMEM((8, 64, 16, 128), F32)
SEMS = pltpu.SemaphoreType.DMA((8,))


VMEM = pl.BlockSpec(memory_space=pltpu.VMEM)
HBM = pl.BlockSpec(memory_space=pltpu.HBM)
PARAMS = pltpu.CompilerParams(vmem_limit_bytes=24 * 2**20)


def moment_weights(first_y):
    lane, row = lane_index((8, 128)), row_index((8, 128))
    y = (lane // 16 + first_y).astype(F32) * STEP - CENTRE * STEP
    z = (lane % 16).astype(F32) * STEP - CENTRE * STEP
    r2 = y * y + z * z
    polynomial = jnp.ones((8, 128), F32)
    for j, g in enumerate([y, z, y * y, z * z, y * z, r2 * y, r2 * z]):
        polynomial = jnp.where(row == j + 1, g, polynomial)
    hi, lo = split(polynomial * jnp.exp(-0.5 * r2) * (1.0 / (TOTAL * TOTAL)))
    half = jnp.concatenate([hi.astype(F32), lo.astype(F32)], axis=0).astype(BF16)
    return jnp.concatenate([half, half], axis=1)


FIRST = 16
FIRST_SEMS = pltpu.SemaphoreType.DMA((64 // FIRST,))


def first_moments_kernel(prior, moments, cells, sums, arrived, sent):
    def part(ref, step):
        return ref.at[pl.ds(step * FIRST, FIRST)]

    fetch, wait = stream([(lambda i: part(prior, i), lambda i: part(cells, i), arrived)])
    put, finish = stream([(lambda i: part(sums, i), lambda i: part(moments, i), sent)])
    for step in range(64 // FIRST):
        fetch(step)
    weights = moment_weights(lax.axis_index("vel") % 2 * LOCAL_Y)
    for step in range(64 // FIRST):
        wait(step)
        for q in range(step * FIRST, step * FIRST + FIRST):
            hi, lo = split(cells[q])
            product = jnp.dot(weights, jnp.concatenate([hi, lo], axis=0), preferred_element_type=F32)
            sums[q] = product[:8] + product[8:]
        put(step)
    for step in range(64 // FIRST):
        finish(step)


def first_moments(prior):
    return pl.pallas_call(
        first_moments_kernel,
        in_specs=[HBM],
        out_specs=HBM,
        out_shape=pltpu.HBM((64, 8, 128), F32),
        scratch_shapes=[pltpu.VMEM((64, 128, 128), F32), pltpu.VMEM((64, 8, 128), F32), FIRST_SEMS, FIRST_SEMS],
        compiler_params=PARAMS,
        name="first_moments",
    )(away(prior)).reshape(VEL, 16, 128)


def pack_kernel(inverse, packed, rows, blocks, arrived):
    fetch, wait = stream([(lambda i: inverse.at[pl.ds(i * 8, 8)], lambda i: blocks.at[pl.ds(i * 8, 8)], arrived)])
    for step in range(8):
        fetch(step)
    for step in range(8):
        wait(step)
        for p in range(step * 8, step * 8 + 8):
            hi, lo = split(blocks[p])
            both = jnp.concatenate([hi.astype(F32), lo.astype(F32)], axis=0)
            rows[pl.ds(p, 128, stride=PITCH), :] = both.T

    def step(v, carry):
        packed[v] = rows[pl.ds(pl.multiple_of(v * PITCH, 8), 64), :].astype(BF16)
        return carry

    lax.fori_loop(0, 128, step, 0, unroll=8)


PITCH = 72


def pack(inverse):
    return pl.pallas_call(
        pack_kernel,
        in_specs=[HBM],
        out_specs=VMEM,
        out_shape=kept(128, 64, 128, dtype=BF16),
        scratch_shapes=[pltpu.VMEM((128 * PITCH, 128), F32), pltpu.VMEM((64, 64, 128), F32), SEMS],
        compiler_params=PARAMS,
        name="pack",
    )(away(jnp.transpose(inverse, (1, 2, 0))))


def mix_kernel(mix, gathered, mixed):
    part = jnp.concatenate([gathered[:, low * 8 : low * 8 + 8, :].reshape(VEL * 8, 128) for low in range(2)], axis=1)
    hi, lo = split(part)
    result = jnp.dot(mix[...], jnp.concatenate([hi, hi, lo], axis=0), preferred_element_type=F32)
    for low in range(2):
        mixed[:, low * 8 : low * 8 + 8, :] = result[:, low * 128 : low * 128 + 128].reshape(VEL, 8, 128)


def mix_moments(mix, gathered):
    return pl.pallas_call(
        mix_kernel,
        in_specs=[VMEM, VMEM],
        out_specs=VMEM,
        out_shape=kept(VEL, 16, 128),
        compiler_params=PARAMS,
        name="mix_moments",
    )(here(mix), here(gathered))


def sum_over_velocities(mix, partial_sums, beside):
    gathered = lax.all_to_all(partial_sums, "vel", 0, 0, axis_index_groups=[ORDER])
    gathered, beside = lax.optimization_barrier((gathered, beside))
    mixed = mix_moments(mix, gathered)
    return lax.all_to_all(mixed, "vel", 0, 0, axis_index_groups=[ORDER]).reshape(512, 128), beside


def add_inflow(source, base, target, send, place, step, mask):
    y = place.speed_y(step)
    lane, row = lane_index((8, 128)), row_index((8, 128))
    trace_x, lift_x = trace_face(place.sign_x), lift_faces(place.sign_x)
    trace_y, lift_y = trace_face(place.sign_y), lift_faces(place.sign_y)
    up_y = place.sign_y > 0
    shift_y = jnp.where(up_y, 8, 120)
    cell_y = jnp.where(up_y, lane // 8 % 8, 7 - lane // 8 % 8)
    scale_y = jnp.where(cell_y > 0, COUPLING * jnp.abs(y), 0.0)
    wall_y = jnp.where(cell_y > 0, 0.0, 2.0 * COUPLING * jnp.abs(y))
    scale_x = jnp.where(mask, place.scale_x, 0.0)
    wall_x = jnp.where(mask, 0.0, place.wall_x * place.scale_x)
    lid = 2.0 * jnp.exp(jnp.full((8, 128), LID_SPEED, F32) * place.vx - 0.5 * LID_SPEED * LID_SPEED)
    for part in range(2):
        up = part == 1
        speed = jnp.abs((row + (part * 8)).astype(F32) - CENTRE) * (STEP * COUPLING)
        inside = (lane % 8 > 0) if up else (lane % 8 < 7)
        scale_z = jnp.where(inside, speed, 0.0)
        wall_z = jnp.where(inside, 0.0, speed * (2.0 if up else lid))
        trace_z, lift_z = trace_face(1.0 if up else -1.0), lift_faces(1.0 if up else -1.0)
        face_x = [None] * 16
        for low in range(8):
            pair = []
            for r in (low, low + 8):
                trace = sum(trace_x[p0] * source(part, p0 * 16 + r) for p0 in range(4))
                turned = pltpu.roll(trace, HALF, 1)
                pair.append((trace, turned))
                face_x[r] = turned * scale_x
            if send is not None:
                send[part * 64 + low * 8 : part * 64 + low * 8 + 8, :] = jnp.where(mask, pair[1][0], pair[0][1])
        face_x[0] = face_x[0] + wall_x
        for p0 in range(4):
            x = [[source(part, p0 * 16 + p1 * 4 + p2) for p2 in range(4)] for p1 in range(4)]
            face_y, face_z = [], []
            for k in range(4):
                ty = sum(trace_y[p1] * x[p1][k] for p1 in range(4))
                ty = pltpu.roll(ty, shift_y, 1) * scale_y
                tz = sum(trace_z[p2] * x[k][p2] for p2 in range(4))
                tz = pltpu.roll(tz, 1 if up else 127, 1) * scale_z
                if p0 == 0 and k == 0:
                    ty = ty + wall_y
                    tz = tz + wall_z
                face_y.append(ty)
                face_z.append(tz)
            for p1 in range(4):
                for p2 in range(4):
                    q, r = p0 * 16 + p1 * 4 + p2, p1 * 4 + p2
                    value = base(part, q) + lift_x[p0] * face_x[r] + lift_y[p1] * face_y[p2] + lift_z[p2] * face_z[p1]
                    target[part * 512 + q * 8 : part * 512 + q * 8 + 8, :] = value


def velocity_rows(v):
    return pl.ds(v // 8 * 512 + v % 8, 64, stride=8)


def block_reader(ref):
    def read(part, q):
        return ref[q, part * 8 : part * 8 + 8, :]

    return read


def row_reader(ref):
    def read(part, q):
        return ref[part * 512 + q * 8 : part * 512 + q * 8 + 8, :]

    return read


def prepare_kernel(
    slabs, prior, right, send_away, scratch, outgoing, cells, made, send, arrived, sent, sent_send
):
    place = Place(slabs)
    mask = outgoing_mask(lane_index((8, 128)), place.sign_x)
    fetch, wait = stream([(lambda i: mode_block(prior, i), lambda i: cells.at[i], arrived)])
    put, finish = stream(
        [
            (lambda i: velocity_block(made, i), lambda i: velocity_block(right, i), sent),
            (lambda i: velocity_block(send, i), lambda i: velocity_block(send_away, i), sent_send),
        ]
    )
    start_all(fetch)

    def loop(step, carry):
        wait(step)
        read = block_reader(cells.at[step])
        add_inflow(read, read, scratch, outgoing, place, step, mask)
        for v in range(16):
            made[step * 16 + v] = scratch[velocity_rows(v), :]
            send[step * 16 + v] = outgoing[pl.ds(v // 8 * 64 + v % 8, 8, stride=8), :]
        put(step)
        return carry

    lax.fori_loop(0, 8, loop, 0)
    for step in range(8):
        finish(step)


def prepare(slabs, prior):
    return pl.pallas_call(
        functools.partial(prepare_kernel, slabs),
        in_specs=[HBM],
        out_specs=[HBM, HBM],
        out_shape=[pltpu.HBM((128, 64, 128), F32), pltpu.HBM((128, 8, 128), F32)],
        scratch_shapes=[
            pltpu.VMEM((1024, 128), F32),
            pltpu.VMEM((128, 128), F32),
            BLOCKS_Q,
            BLOCKS_V,
            pltpu.VMEM((128, 8, 128), F32),
            SEMS,
            SEMS,
            SEMS,
        ],
        compiler_params=PARAMS,
        name="prepare",
    )(away(prior))


def prepare_next_kernel(
    slabs, fresh, prior, right, rows, scratch, columns, cells, made, arrived, arrived_prior, sent
):
    place = Place(slabs)
    mask = outgoing_mask(lane_index((8, 128)), place.sign_x)
    fetch, wait = stream(
        [
            (lambda i: velocity_block(fresh, i), lambda i: velocity_block(columns, i), arrived),
            (lambda i: mode_block(prior, i), lambda i: cells.at[i], arrived_prior),
        ]
    )
    put, finish = stream([(lambda i: velocity_block(made, i), lambda i: velocity_block(right, i), sent)])
    start_all(fetch)

    def loop(step, carry):
        wait(step)
        for v in range(16):
            rows[velocity_rows(v), :] = columns[step * 16 + v]
        add_inflow(row_reader(rows), block_reader(cells.at[step]), scratch, None, place, step, mask)
        for v in range(16):
            made[step * 16 + v] = scratch[velocity_rows(v), :]
        put(step)
        return carry

    lax.fori_loop(0, 8, loop, 0)
    for step in range(8):
        finish(step)


def prepare_next(slabs, fresh, prior):
    return pl.pallas_call(
        functools.partial(prepare_next_kernel, slabs),
        in_specs=[HBM, HBM],
        out_specs=HBM,
        out_shape=pltpu.HBM((128, 64, 128), F32),
        scratch_shapes=[
            pltpu.VMEM((1024, 128), F32),
            pltpu.VMEM((1024, 128), F32),
            BLOCKS_V,
            BLOCKS_Q,
            BLOCKS_V,
            SEMS,
            SEMS,
            SEMS,
        ],
        compiler_params=PARAMS,
        name="prepare_next",
    )(away(fresh), away(prior))


def split_planes(mixed, planes):
    for j in range(8):
        planes[j] = mixed[pl.ds(j, 64, stride=8), :]


def relax(place, step, right, packed, recv, planes, columns, mask, store):
    y = place.speed_y(step)
    columns[0] = planes[0] + y * (planes[1] + y * (planes[3] + y * planes[6]))
    columns[1] = planes[2] + y * (planes[5] + y * planes[7])
    columns[2] = planes[4] + y * planes[6]
    columns[3] = planes[7]
    lift = [place.scale_x * face for face in lift_faces(place.sign_x)]
    for low in range(8):
        z = float(SPEED[15 - low])
        even = columns[0] + (z * z) * columns[2]
        odd = z * columns[1] + (z * z * z) * columns[3]
        for v, equilibrium in ((low, even - odd), (15 - low, even + odd)):
            at = step * 16 + v
            edge = recv[at]
            both = jnp.concatenate([edge, pltpu.roll(edge, HALF, 1)], axis=0)
            both = jnp.where(mask, 0.0, both)
            inflow = jnp.concatenate([lift[p0] * both for p0 in range(4)], axis=0)
            hi, lo = split(right[at] + equilibrium + inflow)
            block = packed[at]
            fresh = jnp.dot(
                jnp.concatenate([block, block], axis=1),
                jnp.concatenate([hi, hi, lo, lo], axis=0),
                preferred_element_type=F32,
            )
            store(v, fresh)


def middle_kernel(
    slabs, right_away, packed, recv, mixed, fresh_away, moments_away, send_away, planes, columns, sums,
    right, fresh, moments, send, arrived, sent, sent_moments, sent_send,
):
    place = Place(slabs)
    mask = outgoing_mask(lane_index((16, 128)), place.sign_x)
    face = trace_face(place.sign_x)
    fetch, wait = stream([(lambda i: velocity_block(right_away, i), lambda i: velocity_block(right, i), arrived)])
    put, finish = stream(
        [
            (lambda i: velocity_block(fresh, i), lambda i: velocity_block(fresh_away, i), sent),
            (lambda i: velocity_block(send, i), lambda i: velocity_block(send_away, i), sent_send),
        ]
    )
    start_all(fetch)
    split_planes(mixed, planes)
    sums[...] = jnp.zeros_like(sums)

    def loop(step, carry):
        def store(v, column):
            fresh[step * 16 + v] = column
            trace = sum(face[p0] * column[p0 * 16 : p0 * 16 + 16] for p0 in range(4))
            outgoing = jnp.where(mask[:8], trace[8:], pltpu.roll(trace[:8], HALF, 1))
            send[step * 16 + v] = outgoing

        wait(step)
        relax(place, step, right, packed, recv, planes, columns, mask, store)
        put(step)
        y = place.speed_y(step)
        weight = jnp.exp(jnp.full((64, 128), -0.5, F32) * (y * y)) * (1.0 / TOTAL)
        s = [None] * 4
        for low in range(8):
            z, w = float(SPEED[15 - low]), float(WEIGHT[low])
            minus, plus = fresh[step * 16 + low], fresh[step * 16 + 15 - low]
            terms = [w * (plus + minus), (w * z) * (plus - minus)]
            for k in range(4):
                term = terms[k % 2] if k < 2 else (z * z) * terms[k % 2]
                s[k] = term if s[k] is None else s[k] + term
        s = [weight * part for part in s]
        y2 = y * y
        totals = [s[0], y * s[0], s[1], y2 * s[0], s[2], y * s[1], y * (y2 * s[0] + s[2]), s[3] + y2 * s[1]]
        for j in range(8):
            sums[j] = sums[j] + totals[j]
        return carry

    lax.fori_loop(0, 8, loop, 0)
    for j in range(8):
        moments[pl.ds(j, 64, stride=8), :] = sums[j]
    copy = pltpu.make_async_copy(moments, moments_away, sent_moments)
    copy.start()
    for step in range(8):
        finish(step)
    copy.wait()


def middle(slabs, right, packed, recv, mixed):
    fresh, moments, send = pl.pallas_call(
        functools.partial(middle_kernel, slabs),
        in_specs=[HBM, VMEM, VMEM, VMEM],
        out_specs=[HBM] * 3,
        out_shape=[pltpu.HBM((128, 64, 128), F32), pltpu.HBM((512, 128), F32), pltpu.HBM((128, 8, 128), F32)],
        scratch_shapes=[
            pltpu.VMEM((8, 64, 128), F32),
            pltpu.VMEM((4, 64, 128), F32),
            pltpu.VMEM((8, 64, 128), F32),
            BLOCKS_V,
            BLOCKS_V,
            pltpu.VMEM((512, 128), F32),
            pltpu.VMEM((128, 8, 128), F32),
            SEMS,
            SEMS,
            pltpu.SemaphoreType.DMA,
            SEMS,
        ],
        compiler_params=PARAMS,
        name="middle",
    )(away(right), here(packed), here(recv), here(mixed))
    return fresh, moments.reshape(VEL, 16, 128), send


def last_kernel(slabs, right_away, packed, recv, mixed, out, planes, columns, right, blocks, arrived, sent):
    place = Place(slabs)
    mask = outgoing_mask(lane_index((16, 128)), place.sign_x)
    fetch, wait = stream([(lambda i: velocity_block(right_away, i), lambda i: velocity_block(right, i), arrived)])
    put, finish = stream([(lambda i: blocks.at[i], lambda i: mode_block(out, i), sent)])
    start_all(fetch)
    split_planes(mixed, planes)

    def loop(step, carry):
        flat = blocks.at[step].reshape(1024, 128)

        def store(v, fresh):
            flat[pl.ds(v, 64, stride=16), :] = fresh

        wait(step)
        relax(place, step, right, packed, recv, planes, columns, mask, store)
        put(step)
        return carry

    lax.fori_loop(0, 8, loop, 0)
    for step in range(8):
        finish(step)


def last(slabs, right, packed, recv, mixed):
    return pl.pallas_call(
        functools.partial(last_kernel, slabs),
        in_specs=[HBM, VMEM, VMEM, VMEM],
        out_specs=HBM,
        out_shape=pltpu.HBM((64, 128, 128), F32),
        scratch_shapes=[
            pltpu.VMEM((8, 64, 128), F32),
            pltpu.VMEM((4, 64, 128), F32),
            BLOCKS_V,
            BLOCKS_Q,
            SEMS,
            SEMS,
        ],
        compiler_params=PARAMS,
        name="last",
    )(away(right), here(packed), here(recv), here(mixed))


def halo_pairs(slabs):
    pairs = []
    for slab in range(slabs):
        for vel in range(VEL):
            other = slab + 1 if vel >= VEL // 2 else slab - 1
            if 0 <= other < slabs:
                pairs.append((slab * VEL + vel, other * VEL + vel))
    return pairs


def body(slabs, prior, block_inverse):
    leading = MIX.astype(jnp.bfloat16)
    rest = (MIX - leading.astype(np.float32)).astype(jnp.bfloat16)
    mix = jnp.asarray(np.concatenate([leading, rest, leading], axis=1))
    axes = ("sp", "vel")
    pairs = halo_pairs(slabs)
    cells = prior.reshape(64, 128, 128)
    moments = first_moments(cells)
    mixed, (right, send) = sum_over_velocities(mix, moments, prepare(slabs, cells))
    recv = lax.ppermute(send, axes, pairs)
    packed = pack(block_inverse)
    fresh, moments, send = middle(slabs, right, packed, recv, mixed)
    recv = lax.ppermute(send, axes, pairs)
    mixed, right = sum_over_velocities(mix, moments, prepare_next(slabs, fresh, cells))
    return last(slabs, right, packed, recv, mixed).reshape(prior.shape)


def solution(mesh):
    spec = P(None, None, None, "vel", "sp")
    return jax.shard_map(
        functools.partial(body, mesh.shape["sp"]),
        mesh=mesh,
        in_specs=(spec, P("vel", None, None)),
        out_specs=spec,
        check_vma=False,
    )
```

```python
import functools

import jax
import jax.numpy as jnp
import numpy as np
from jax import lax
from jax.experimental import pallas as pl
from jax.experimental.pallas import tpu as pltpu
from jax.sharding import PartitionSpec as P

NV1 = 16
COUPLING = 0.25
LID_SPEED = 0.6
STEP = 6.0 / NV1
CENTRE = 0.5 * (NV1 - 1)
VEL = 32
LOCAL_Y = 8
HIGH = [float(np.sqrt(k + 0.5)) for k in range(4)]
F32 = jnp.float32
BF16 = jnp.bfloat16
HALF = 64


def ring_hops(vel):
    along_y, along_z = min(vel // 4 % 4, 4 - vel // 4 % 4), min(vel % 4, 4 - vel % 4)
    return vel // 16, along_y + along_z, vel


ORDER = sorted(range(VEL), key=ring_hops, reverse=True)


def grid_speed(index):
    return (np.asarray(index, np.float64) - CENTRE) * STEP


def local_polynomials(y, z):
    r2 = y * y + z * z
    return [np.ones_like(r2), y, z, y * y, z * z, y * z, r2 * y, r2 * z]


def combination(x):
    c = np.zeros((13, 8))
    c[0, 0] = 1.0
    c[1, 0] = x
    c[2, 1] = 1.0
    c[3, 2] = 1.0
    c[4, 0] = x * x - 1.0
    c[5, 3], c[5, 0] = 1.0, -1.0
    c[6, 4], c[6, 0] = 1.0, -1.0
    c[7, 1] = x
    c[8, 2] = x
    c[9, 5] = 1.0
    c[10, 0], c[10, 3], c[10, 4] = x * (x * x - 5.0), x, x
    c[11, 1], c[11, 6] = x * x - 5.0, 1.0
    c[12, 2], c[12, 7] = x * x - 5.0, 1.0
    return c


def tables():
    speed = grid_speed(np.arange(NV1))
    weight = np.exp(-0.5 * speed * speed)
    total = weight.sum()
    weight = weight / total
    x, y, z = np.meshgrid(speed, speed, speed, indexing="ij")
    w = weight[:, None, None] * weight[None, :, None] * weight[None, None, :]
    g = np.stack(local_polynomials(y, z))
    per_x = np.stack([combination(s) for s in speed])
    h = np.einsum("xkj,jxyz->kxyz", per_x, g)
    norm = (w * h * h).sum(axis=(1, 2, 3))
    source = np.repeat(per_x * weight[:, None, None], 2, axis=0)
    target = np.repeat(per_x, 2, axis=0)
    mix = np.einsum("tkj,k,ski->tjsi", target, 1.0 / norm, source).reshape(VEL * 8, VEL * 8)
    mix = mix.reshape(VEL, 8, VEL, 8)[ORDER][:, :, ORDER].reshape(VEL * 8, VEL * 8)
    return mix.astype(np.float32), speed, weight, float(total)


MIX, SPEED, WEIGHT, TOTAL = tables()


def split(a):
    hi = a.astype(BF16)
    return hi, (a - hi.astype(F32)).astype(BF16)


def lane_index(shape):
    return lax.broadcasted_iota(jnp.int32, shape, len(shape) - 1)


def row_index(shape):
    return lax.broadcasted_iota(jnp.int32, shape, len(shape) - 2)


class Place:
    def __init__(self, slabs):
        vel, slab = lax.axis_index("vel"), lax.axis_index("sp")
        self.vx = (vel // 2).astype(F32) * STEP - CENTRE * STEP
        self.sign_x = jnp.where(vel >= VEL // 2, 1.0, -1.0)
        self.scale_x = COUPLING * jnp.abs(self.vx)
        self.first_y = vel % 2 * LOCAL_Y
        self.sign_y = jnp.where(vel % 2 == 1, 1.0, -1.0)
        boundary = jnp.where(vel >= VEL // 2, 0, slabs - 1)
        self.wall_x = jnp.where(slab == boundary, 2.0, 0.0)

    def speed_y(self, step):
        return (self.first_y + step).astype(F32) * STEP - CENTRE * STEP


def outgoing_mask(lane, sign):
    return jnp.where(sign > 0, lane, 2 * HALF - 1 - lane) >= HALF


def trace_face(sign):
    return [HIGH[k] if k % 2 == 0 else HIGH[k] * sign for k in range(4)]


def lift_faces(sign):
    return [HIGH[k] if k % 2 == 0 else -HIGH[k] * sign for k in range(4)]


def kept(*shape, dtype=F32):
    return pltpu.VMEM(shape, dtype)


def here(x):
    return pltpu.with_memory_space_constraint(x, pltpu.VMEM)


def away(x):
    return pltpu.with_memory_space_constraint(x, pltpu.HBM)


def velocity_block(ref, step):
    return ref.at[pl.ds(pl.multiple_of(step * 16, 16), 16)]


def mode_block(ref, step):
    return ref.at[:, pl.ds(pl.multiple_of(step * 16, 16), 16), :]


def stream(pairs):
    def copies(step):
        return [pltpu.make_async_copy(source(step), target(step), sems.at[step]) for source, target, sems in pairs]

    def start(step):
        for copy in copies(step):
            copy.start()

    def wait(step):
        for copy in copies(step):
            copy.wait()

    return start, wait


def start_all(start):
    for step in range(8):
        start(step)


BLOCKS_V = pltpu.VMEM((128, 64, 128), F32)
BLOCKS_Q = pltpu.VMEM((8, 64, 16, 128), F32)
SEMS = pltpu.SemaphoreType.DMA((8,))


VMEM = pl.BlockSpec(memory_space=pltpu.VMEM)
HBM = pl.BlockSpec(memory_space=pltpu.HBM)
PARAMS = pltpu.CompilerParams(vmem_limit_bytes=24 * 2**20)


def moment_weights(first_y):
    lane, row = lane_index((8, 128)), row_index((8, 128))
    y = (lane // 16 + first_y).astype(F32) * STEP - CENTRE * STEP
    z = (lane % 16).astype(F32) * STEP - CENTRE * STEP
    r2 = y * y + z * z
    polynomial = jnp.ones((8, 128), F32)
    for j, g in enumerate([y, z, y * y, z * z, y * z, r2 * y, r2 * z]):
        polynomial = jnp.where(row == j + 1, g, polynomial)
    hi, lo = split(polynomial * jnp.exp(-0.5 * r2) * (1.0 / (TOTAL * TOTAL)))
    half = jnp.concatenate([hi.astype(F32), lo.astype(F32)], axis=0).astype(BF16)
    return jnp.concatenate([half, half], axis=1)


FIRST = 16
FIRST_SEMS = pltpu.SemaphoreType.DMA((64 // FIRST,))


def first_moments_kernel(prior, moments, cells, sums, arrived, sent):
    def part(ref, step):
        return ref.at[pl.ds(step * FIRST, FIRST)]

    fetch, wait = stream([(lambda i: part(prior, i), lambda i: part(cells, i), arrived)])
    put, finish = stream([(lambda i: part(sums, i), lambda i: part(moments, i), sent)])
    for step in range(64 // FIRST):
        fetch(step)
    weights = moment_weights(lax.axis_index("vel") % 2 * LOCAL_Y)
    for step in range(64 // FIRST):
        wait(step)
        for q in range(step * FIRST, step * FIRST + FIRST):
            hi, lo = split(cells[q])
            product = jnp.dot(weights, jnp.concatenate([hi, lo], axis=0), preferred_element_type=F32)
            sums[q] = product[:8] + product[8:]
        put(step)
    for step in range(64 // FIRST):
        finish(step)


def first_moments(prior):
    return pl.pallas_call(
        first_moments_kernel,
        in_specs=[HBM],
        out_specs=HBM,
        out_shape=pltpu.HBM((64, 8, 128), F32),
        scratch_shapes=[pltpu.VMEM((64, 128, 128), F32), pltpu.VMEM((64, 8, 128), F32), FIRST_SEMS, FIRST_SEMS],
        compiler_params=PARAMS,
        name="first_moments",
    )(away(prior)).reshape(VEL, 16, 128)


def pack_kernel(inverse, packed, rows, blocks, arrived):
    fetch, wait = stream([(lambda i: inverse.at[pl.ds(i * 8, 8)], lambda i: blocks.at[pl.ds(i * 8, 8)], arrived)])
    for step in range(8):
        fetch(step)
    for step in range(8):
        wait(step)
        for p in range(step * 8, step * 8 + 8):
            hi, lo = split(blocks[p])
            both = jnp.concatenate([hi.astype(F32), lo.astype(F32)], axis=0)
            rows[pl.ds(p, 128, stride=PITCH), :] = both.T

    def step(v, carry):
        packed[v] = rows[pl.ds(pl.multiple_of(v * PITCH, 8), 64), :].astype(BF16)
        return carry

    lax.fori_loop(0, 128, step, 0, unroll=8)


PITCH = 72


def pack(inverse):
    return pl.pallas_call(
        pack_kernel,
        in_specs=[HBM],
        out_specs=VMEM,
        out_shape=kept(128, 64, 128, dtype=BF16),
        scratch_shapes=[pltpu.VMEM((128 * PITCH, 128), F32), pltpu.VMEM((64, 64, 128), F32), SEMS],
        compiler_params=PARAMS,
        name="pack",
    )(away(jnp.transpose(inverse, (1, 2, 0))))


def mix_kernel(mix, gathered, mixed):
    part = jnp.concatenate([gathered[:, low * 8 : low * 8 + 8, :].reshape(VEL * 8, 128) for low in range(2)], axis=1)
    hi, lo = split(part)
    result = jnp.dot(mix[...], jnp.concatenate([hi, hi, lo], axis=0), preferred_element_type=F32)
    for low in range(2):
        mixed[:, low * 8 : low * 8 + 8, :] = result[:, low * 128 : low * 128 + 128].reshape(VEL, 8, 128)


def mix_moments(mix, gathered):
    return pl.pallas_call(
        mix_kernel,
        in_specs=[VMEM, VMEM],
        out_specs=VMEM,
        out_shape=kept(VEL, 16, 128),
        compiler_params=PARAMS,
        name="mix_moments",
    )(here(mix), here(gathered))


def sum_over_velocities(mix, partial_sums, beside):
    gathered = lax.all_to_all(partial_sums, "vel", 0, 0, axis_index_groups=[ORDER])
    gathered, beside = lax.optimization_barrier((gathered, beside))
    mixed = mix_moments(mix, gathered)
    return lax.all_to_all(mixed, "vel", 0, 0, axis_index_groups=[ORDER]).reshape(512, 128), beside


def add_inflow(source, base, target, send, place, step, mask):
    y = place.speed_y(step)
    lane, row = lane_index((8, 128)), row_index((8, 128))
    trace_x, lift_x = trace_face(place.sign_x), lift_faces(place.sign_x)
    trace_y, lift_y = trace_face(place.sign_y), lift_faces(place.sign_y)
    up_y = place.sign_y > 0
    shift_y = jnp.where(up_y, 8, 120)
    cell_y = jnp.where(up_y, lane // 8 % 8, 7 - lane // 8 % 8)
    scale_y = jnp.where(cell_y > 0, COUPLING * jnp.abs(y), 0.0)
    wall_y = jnp.where(cell_y > 0, 0.0, 2.0 * COUPLING * jnp.abs(y))
    scale_x = jnp.where(mask, place.scale_x, 0.0)
    wall_x = jnp.where(mask, 0.0, place.wall_x * place.scale_x)
    lid = 2.0 * jnp.exp(jnp.full((8, 128), LID_SPEED, F32) * place.vx - 0.5 * LID_SPEED * LID_SPEED)
    for part in range(2):
        up = part == 1
        speed = jnp.abs((row + (part * 8)).astype(F32) - CENTRE) * (STEP * COUPLING)
        inside = (lane % 8 > 0) if up else (lane % 8 < 7)
        scale_z = jnp.where(inside, speed, 0.0)
        wall_z = jnp.where(inside, 0.0, speed * (2.0 if up else lid))
        trace_z, lift_z = trace_face(1.0 if up else -1.0), lift_faces(1.0 if up else -1.0)
        face_x = [None] * 16
        for low in range(8):
            pair = []
            for r in (low, low + 8):
                trace = sum(trace_x[p0] * source(part, p0 * 16 + r) for p0 in range(4))
                turned = pltpu.roll(trace, HALF, 1)
                pair.append((trace, turned))
                face_x[r] = turned * scale_x
            if send is not None:
                send[part * 64 + low * 8 : part * 64 + low * 8 + 8, :] = jnp.where(mask, pair[1][0], pair[0][1])
        face_x[0] = face_x[0] + wall_x
        for p0 in range(4):
            x = [[source(part, p0 * 16 + p1 * 4 + p2) for p2 in range(4)] for p1 in range(4)]
            face_y, face_z = [], []
            for k in range(4):
                ty = sum(trace_y[p1] * x[p1][k] for p1 in range(4))
                ty = pltpu.roll(ty, shift_y, 1) * scale_y
                tz = sum(trace_z[p2] * x[k][p2] for p2 in range(4))
                tz = pltpu.roll(tz, 1 if up else 127, 1) * scale_z
                if p0 == 0 and k == 0:
                    ty = ty + wall_y
                    tz = tz + wall_z
                face_y.append(ty)
                face_z.append(tz)
            for p1 in range(4):
                for p2 in range(4):
                    q, r = p0 * 16 + p1 * 4 + p2, p1 * 4 + p2
                    value = base(part, q) + lift_x[p0] * face_x[r] + lift_y[p1] * face_y[p2] + lift_z[p2] * face_z[p1]
                    target[part * 512 + q * 8 : part * 512 + q * 8 + 8, :] = value


def velocity_rows(v):
    return pl.ds(v // 8 * 512 + v % 8, 64, stride=8)


def block_reader(ref):
    def read(part, q):
        return ref[q, part * 8 : part * 8 + 8, :]

    return read


def row_reader(ref):
    def read(part, q):
        return ref[part * 512 + q * 8 : part * 512 + q * 8 + 8, :]

    return read


def prepare_kernel(
    slabs, prior, right, send_away, scratch, outgoing, cells, made, send, arrived, sent, sent_send
):
    place = Place(slabs)
    mask = outgoing_mask(lane_index((8, 128)), place.sign_x)
    fetch, wait = stream([(lambda i: mode_block(prior, i), lambda i: cells.at[i], arrived)])
    put, finish = stream(
        [
            (lambda i: velocity_block(made, i), lambda i: velocity_block(right, i), sent),
            (lambda i: velocity_block(send, i), lambda i: velocity_block(send_away, i), sent_send),
        ]
    )
    start_all(fetch)

    def loop(step, carry):
        wait(step)
        read = block_reader(cells.at[step])
        add_inflow(read, read, scratch, outgoing, place, step, mask)
        for v in range(16):
            made[step * 16 + v] = scratch[velocity_rows(v), :]
            send[step * 16 + v] = outgoing[pl.ds(v // 8 * 64 + v % 8, 8, stride=8), :]
        put(step)
        return carry

    lax.fori_loop(0, 8, loop, 0)
    for step in range(8):
        finish(step)


def prepare(slabs, prior):
    return pl.pallas_call(
        functools.partial(prepare_kernel, slabs),
        in_specs=[HBM],
        out_specs=[HBM, HBM],
        out_shape=[pltpu.HBM((128, 64, 128), F32), pltpu.HBM((128, 8, 128), F32)],
        scratch_shapes=[
            pltpu.VMEM((1024, 128), F32),
            pltpu.VMEM((128, 128), F32),
            BLOCKS_Q,
            BLOCKS_V,
            pltpu.VMEM((128, 8, 128), F32),
            SEMS,
            SEMS,
            SEMS,
        ],
        compiler_params=PARAMS,
        name="prepare",
    )(away(prior))


def prepare_next_kernel(
    slabs, fresh, prior, right, rows, scratch, columns, cells, made, arrived, arrived_prior, sent
):
    place = Place(slabs)
    mask = outgoing_mask(lane_index((8, 128)), place.sign_x)
    fetch, wait = stream(
        [
            (lambda i: velocity_block(fresh, i), lambda i: velocity_block(columns, i), arrived),
            (lambda i: mode_block(prior, i), lambda i: cells.at[i], arrived_prior),
        ]
    )
    put, finish = stream([(lambda i: velocity_block(made, i), lambda i: velocity_block(right, i), sent)])
    start_all(fetch)

    def loop(step, carry):
        wait(step)
        for v in range(16):
            rows[velocity_rows(v), :] = columns[step * 16 + v]
        add_inflow(row_reader(rows), block_reader(cells.at[step]), scratch, None, place, step, mask)
        for v in range(16):
            made[step * 16 + v] = scratch[velocity_rows(v), :]
        put(step)
        return carry

    lax.fori_loop(0, 8, loop, 0)
    for step in range(8):
        finish(step)


def prepare_next(slabs, fresh, prior):
    return pl.pallas_call(
        functools.partial(prepare_next_kernel, slabs),
        in_specs=[HBM, HBM],
        out_specs=HBM,
        out_shape=pltpu.HBM((128, 64, 128), F32),
        scratch_shapes=[
            pltpu.VMEM((1024, 128), F32),
            pltpu.VMEM((1024, 128), F32),
            BLOCKS_V,
            BLOCKS_Q,
            BLOCKS_V,
            SEMS,
            SEMS,
            SEMS,
        ],
        compiler_params=PARAMS,
        name="prepare_next",
    )(away(fresh), away(prior))


def split_planes(mixed, planes):
    for j in range(8):
        planes[j] = mixed[pl.ds(j, 64, stride=8), :]


def relax(place, step, right, packed, recv, planes, columns, mask, store):
    y = place.speed_y(step)
    columns[0] = planes[0] + y * (planes[1] + y * (planes[3] + y * planes[6]))
    columns[1] = planes[2] + y * (planes[5] + y * planes[7])
    columns[2] = planes[4] + y * planes[6]
    columns[3] = planes[7]
    lift = [place.scale_x * face for face in lift_faces(place.sign_x)]
    for low in range(8):
        z = float(SPEED[15 - low])
        even = columns[0] + (z * z) * columns[2]
        odd = z * columns[1] + (z * z * z) * columns[3]
        for v, equilibrium in ((low, even - odd), (15 - low, even + odd)):
            at = step * 16 + v
            edge = recv[at]
            both = jnp.concatenate([edge, pltpu.roll(edge, HALF, 1)], axis=0)
            both = jnp.where(mask, 0.0, both)
            inflow = jnp.concatenate([lift[p0] * both for p0 in range(4)], axis=0)
            hi, lo = split(right[at] + equilibrium + inflow)
            block = packed[at]
            fresh = jnp.dot(
                jnp.concatenate([block, block], axis=1),
                jnp.concatenate([hi, hi, lo, lo], axis=0),
                preferred_element_type=F32,
            )
            store(v, fresh)


def middle_kernel(
    slabs, right_away, packed, recv, mixed, fresh_away, moments_away, send_away, planes, columns, sums,
    right, fresh, moments, send, arrived, sent, sent_moments, sent_send,
):
    place = Place(slabs)
    mask = outgoing_mask(lane_index((16, 128)), place.sign_x)
    face = trace_face(place.sign_x)
    fetch, wait = stream([(lambda i: velocity_block(right_away, i), lambda i: velocity_block(right, i), arrived)])
    put, finish = stream(
        [
            (lambda i: velocity_block(fresh, i), lambda i: velocity_block(fresh_away, i), sent),
            (lambda i: velocity_block(send, i), lambda i: velocity_block(send_away, i), sent_send),
        ]
    )
    start_all(fetch)
    split_planes(mixed, planes)
    sums[...] = jnp.zeros_like(sums)

    def loop(step, carry):
        def store(v, column):
            fresh[step * 16 + v] = column
            trace = sum(face[p0] * column[p0 * 16 : p0 * 16 + 16] for p0 in range(4))
            outgoing = jnp.where(mask[:8], trace[8:], pltpu.roll(trace[:8], HALF, 1))
            send[step * 16 + v] = outgoing

        wait(step)
        relax(place, step, right, packed, recv, planes, columns, mask, store)
        put(step)
        y = place.speed_y(step)
        weight = jnp.exp(jnp.full((64, 128), -0.5, F32) * (y * y)) * (1.0 / TOTAL)
        s = [None] * 4
        for low in range(8):
            z, w = float(SPEED[15 - low]), float(WEIGHT[low])
            minus, plus = fresh[step * 16 + low], fresh[step * 16 + 15 - low]
            terms = [w * (plus + minus), (w * z) * (plus - minus)]
            for k in range(4):
                term = terms[k % 2] if k < 2 else (z * z) * terms[k % 2]
                s[k] = term if s[k] is None else s[k] + term
        s = [weight * part for part in s]
        y2 = y * y
        totals = [s[0], y * s[0], s[1], y2 * s[0], s[2], y * s[1], y * (y2 * s[0] + s[2]), s[3] + y2 * s[1]]
        for j in range(8):
            sums[j] = sums[j] + totals[j]
        return carry

    lax.fori_loop(0, 8, loop, 0)
    for j in range(8):
        moments[pl.ds(j, 64, stride=8), :] = sums[j]
    copy = pltpu.make_async_copy(moments, moments_away, sent_moments)
    copy.start()
    for step in range(8):
        finish(step)
    copy.wait()


def middle(slabs, right, packed, recv, mixed):
    fresh, moments, send = pl.pallas_call(
        functools.partial(middle_kernel, slabs),
        in_specs=[HBM, VMEM, VMEM, VMEM],
        out_specs=[HBM] * 3,
        out_shape=[pltpu.HBM((128, 64, 128), F32), pltpu.HBM((512, 128), F32), pltpu.HBM((128, 8, 128), F32)],
        scratch_shapes=[
            pltpu.VMEM((8, 64, 128), F32),
            pltpu.VMEM((4, 64, 128), F32),
            pltpu.VMEM((8, 64, 128), F32),
            BLOCKS_V,
            BLOCKS_V,
            pltpu.VMEM((512, 128), F32),
            pltpu.VMEM((128, 8, 128), F32),
            SEMS,
            SEMS,
            pltpu.SemaphoreType.DMA,
            SEMS,
        ],
        compiler_params=PARAMS,
        name="middle",
    )(away(right), here(packed), here(recv), here(mixed))
    return fresh, moments.reshape(VEL, 16, 128), send


def last_kernel(slabs, right_away, packed, recv, mixed, out, planes, columns, right, blocks, arrived, sent):
    place = Place(slabs)
    mask = outgoing_mask(lane_index((16, 128)), place.sign_x)
    fetch, wait = stream([(lambda i: velocity_block(right_away, i), lambda i: velocity_block(right, i), arrived)])
    put, finish = stream([(lambda i: blocks.at[i], lambda i: mode_block(out, i), sent)])
    start_all(fetch)
    split_planes(mixed, planes)

    def loop(step, carry):
        flat = blocks.at[step].reshape(1024, 128)

        def store(v, fresh):
            flat[pl.ds(v, 64, stride=16), :] = fresh

        wait(step)
        relax(place, step, right, packed, recv, planes, columns, mask, store)
        put(step)
        return carry

    for step in range(8):
        loop(step, 0)
    for step in range(8):
        finish(step)


def last(slabs, right, packed, recv, mixed):
    return pl.pallas_call(
        functools.partial(last_kernel, slabs),
        in_specs=[HBM, VMEM, VMEM, VMEM],
        out_specs=HBM,
        out_shape=pltpu.HBM((64, 128, 128), F32),
        scratch_shapes=[
            pltpu.VMEM((8, 64, 128), F32),
            pltpu.VMEM((4, 64, 128), F32),
            BLOCKS_V,
            BLOCKS_Q,
            SEMS,
            SEMS,
        ],
        compiler_params=PARAMS,
        name="last",
    )(away(right), here(packed), here(recv), here(mixed))


def halo_pairs(slabs):
    pairs = []
    for slab in range(slabs):
        for vel in range(VEL):
            other = slab + 1 if vel >= VEL // 2 else slab - 1
            if 0 <= other < slabs:
                pairs.append((slab * VEL + vel, other * VEL + vel))
    return pairs


def body(slabs, prior, block_inverse):
    leading = MIX.astype(jnp.bfloat16)
    rest = (MIX - leading.astype(np.float32)).astype(jnp.bfloat16)
    mix = jnp.asarray(np.concatenate([leading, rest, leading], axis=1))
    axes = ("sp", "vel")
    pairs = halo_pairs(slabs)
    cells = prior.reshape(64, 128, 128)
    moments = first_moments(cells)
    mixed, (right, send) = sum_over_velocities(mix, moments, prepare(slabs, cells))
    recv = lax.ppermute(send, axes, pairs)
    packed = pack(block_inverse)
    fresh, moments, send = middle(slabs, right, packed, recv, mixed)
    recv = lax.ppermute(send, axes, pairs)
    mixed, right = sum_over_velocities(mix, moments, prepare_next(slabs, fresh, cells))
    return last(slabs, right, packed, recv, mixed).reshape(prior.shape)


def solution(mesh):
    spec = P(None, None, None, "vel", "sp")
    return jax.shard_map(
        functools.partial(body, mesh.shape["sp"]),
        mesh=mesh,
        in_specs=(spec, P("vel", None, None)),
        out_specs=spec,
        check_vma=False,
    )
```
